32 devices in a mesh: parts: 2 (over x), store: 16 (over z, y, core).
Axes of the slice: x: 2, y: 2, z: 4, core: 2. Of those that a mesh axis runs over, the one named last changes fastest.
Arguments:
- tokens: bfloat16 [16384, 8192], P(('parts', 'store')), parts along dimension 0, may hold values from -6 to 6
- base_weight: bfloat16 [8192, 512], P('store'), may hold values from -0.0625 to 0.0625
- adapter_down: bfloat16 [128, 8192, 64], P(None, 'store'), may hold values from -0.0625 to 0.0625
- adapter_up: bfloat16 [128, 512, 64], P(None, 'store'), may hold values from -0.75 to 0.75
- request_lengths: int32 [32, 16], P(('parts', 'store')), parts along dimension 0, may hold values from 1 to 256, 512 in all within a row
- group_adapters: int32 [32, 2], P('parts'), parts along dimension 0, may hold values from 0 to 127, as said below
- request_slot: int32 [32, 16], P('parts'), parts along dimension 0, may hold values from 0 to 1
Outputs:
- values: bfloat16 [16384, 512], P(('parts', 'store')), parts along dimension 0
The draws below stay inside these ranges and needn't reach their ends.
There are 2 independent parts, one for each index of `parts`. The reference program is written for one: setup_inputs(seed, part) draws one part's arguments, and reference() takes and returns one part's arrays. A program takes and returns all parts, laid end to end along the dimension named above; an argument that names none is the same for every part. Nothing has to cross between parts.
Inputs may be any that keep to these rules, and one draw needn't show every extreme that they name: `group_adapters`: each row names 2 different adapters.
All inputs are finite; a program needn't handle non-finite values.
Results may differ from the reference program's by a relative error of at most 0.0065.
Values may be sent and summed in bfloat16 or wider, within the bound.
No kernel may reach another device: no remote copies, remote signals or barrier semaphores. Data moves between devices by JAX's collectives and lax.ppermute only.
A program may use at most 128 MiB of HBM per device.

```python
import math
import jax
import jax.numpy as jnp
import numpy as np
from jax import lax

D = 8192
KV = 512
R = 64
TOK_DEV = 512
REQ_DEV = 16
DIST = 2
GROUPS = 16
ADAPTERS = 128
TOKENS = 8192


def draw_group_adapters(key, part):
    key = jax.random.fold_in(key, 11)
    first_key, step_key = jax.random.split(key)
    first = jax.random.randint(first_key, (GROUPS, 1), 0, ADAPTERS, dtype=jnp.int32)
    steps_drawn = jax.random.randint(step_key, (GROUPS, DIST - 1), 1, ADAPTERS // DIST, dtype=jnp.int32)
    offsets = jnp.concatenate([jnp.zeros((GROUPS, 1), jnp.int32), jnp.cumsum(steps_drawn, axis=1).astype(jnp.int32)], axis=1)
    return ((first + offsets) % ADAPTERS).astype(jnp.int32)


def with_ends(drawn, own_key, low, largest):
    extent = drawn.shape
    place = [jax.random.randint(jax.random.fold_in(own_key, axis), (), 0, extent[axis]) for axis in range(len(extent))]
    drawn = drawn.at[tuple(place)].set(low)
    longest = extent.index(max(extent))
    place[longest] = (place[longest] + 1) % extent[longest]
    return drawn.at[tuple(place)].set(largest)


def block_levels(stream_key, extent, cuts, smallest, largest):
    gain, own = 1.0, jax.random.fold_in(stream_key, 6)
    for dim, blocks in cuts:
        heights = jnp.exp(jax.random.uniform(jax.random.fold_in(own, dim), (blocks,), jnp.float32, smallest / len(cuts), largest / len(cuts)))
        gain = gain * jnp.repeat(heights, extent[dim] // blocks).reshape([-1 if axis == dim else 1 for axis in range(len(extent))])
    return gain


def profile(number_of, total, bound, skew):
    weights = [(1 << 20) // math.isqrt(grade ** skew) + 1 for grade in range(2, number_of + 1)]
    spare, given = total - bound - (number_of - 1), [1] * (number_of - 1)
    while spare > 0:
        candidates = [i for i in range(number_of - 1) if given[i] < bound]
        whole, remaining = sum([weights[i] for i in candidates]), spare
        for i in candidates:
            more = min(bound - given[i], max(1, remaining * weights[i] // whole), spare)
            given[i] = given[i] + more
            spare = spare - more
    return np.array([bound] + given)


def uneven_parts(stream_key, amount, total, limit, slope):
    if amount == 2:
        one = jax.random.randint(stream_key, (), max(1, total - limit), min(limit, total - 1) + 1)
        return jnp.stack([one, total - one])
    tallies = jnp.asarray(profile(amount, total, limit, slope), jnp.int32)
    pairs = (amount - 1) // 2
    giver, sink = tallies[1:1 + 2 * pairs:2], tallies[2:2 + 2 * pairs:2]
    room = jnp.minimum(giver - 1, limit - sink)
    passed = jax.random.randint(jax.random.fold_in(stream_key, 1), (pairs,), 0, 1 << 20) % (room + 1)
    tallies = tallies.at[1:1 + 2 * pairs:2].set(giver - passed).at[2:2 + 2 * pairs:2].set(sink + passed)
    return tallies[jax.random.permutation(jax.random.fold_in(stream_key, 2), amount)]


def centred(key, dims, spread, reach, shards=(), kind=jnp.bfloat16):
    drawn = spread * jax.random.normal(key, dims, jnp.float32)
    if shards:
        drawn = drawn * block_levels(key, dims, shards, -0.22, 0.18)
    return jnp.clip(drawn, -reach, reach).astype(kind)


def setup_inputs(seed: int = 0, part: int = 0) -> dict:
    keys = jax.random.split(jax.random.key(seed), 8)
    part_splits = jax.random.split(jax.random.fold_in(keys[7], part), 8)
    return {
        "tokens": centred(part_splits[0], (TOKENS, D), 1.0, 6.0, ((0, 16),)),
        "base_weight": centred(keys[1], (D, KV), D ** -0.5, 0.0625, ((0, 16),)),
        "adapter_down": centred(keys[2], (ADAPTERS, D, R), D ** -0.5, 0.0625, ((1, 16),)),
        "adapter_up": centred(keys[3], (ADAPTERS, KV, R), R ** -0.5, 0.75, ((1, 16),)),
        "request_lengths": jax.vmap(lambda own: uneven_parts(own, REQ_DEV, TOK_DEV, TOK_DEV // 2, 2))(jax.random.split(part_splits[4], GROUPS)).reshape((GROUPS, REQ_DEV)).astype(jnp.int32),
        "group_adapters": draw_group_adapters(jax.random.fold_in(jax.random.fold_in(keys[7], part), 71), part),
        "request_slot": with_ends(jax.random.randint(part_splits[6], (GROUPS, REQ_DEV), 0, DIST), jax.random.fold_in(part_splits[6], 1), 0, DIST - 1).astype(jnp.int32),
    }


def reference(tokens, base_weight, adapter_down, adapter_up, request_lengths, group_adapters, request_slot):
    base = jnp.dot(tokens, base_weight, preferred_element_type=jnp.float32)
    groups = request_lengths.shape[0]
    rows = tokens.shape[0] // groups
    width = base_weight.shape[1]
    choices_count = group_adapters.shape[1]

    def one_group(group):
        block = lax.dynamic_slice_in_dim(tokens, (group * rows).astype(jnp.int32), rows, 0)
        lengths = lax.dynamic_index_in_dim(request_lengths, group, 0, keepdims=False)
        slots = lax.dynamic_index_in_dim(request_slot, group, 0, keepdims=False)
        adapters = lax.dynamic_index_in_dim(group_adapters, group, 0, keepdims=False)
        ends = jnp.cumsum(lengths).astype(jnp.int32)
        starts = ends - lengths
        position = jnp.arange(rows, dtype=jnp.int32)[:, None]
        member = (position >= starts[None, :]) & (position < ends[None, :])
        chosen = jnp.sum(jnp.where(member, slots[None, :], 0), axis=1).astype(jnp.int32)
        select = (chosen[:, None] == jnp.arange(choices_count, dtype=jnp.int32)[None, :]).astype(jnp.float32)
        down = jnp.take(adapter_down, adapters, axis=0).astype(jnp.float32)
        upper = jnp.take(adapter_up, adapters, axis=0).astype(jnp.float32)
        shrink_all = jnp.einsum("td,kdr->tkr", block.astype(jnp.float32), down)
        shrink = jnp.sum(select[:, :, None] * shrink_all, axis=1).astype(jnp.bfloat16)
        picked = select[:, :, None] * shrink.astype(jnp.float32)[:, None, :]
        return jnp.einsum("tkr,kvr->tv", picked, upper)

    deltas = lax.map(one_group, jnp.arange(groups, dtype=jnp.int32))
    return (base + deltas.reshape(groups * rows, width)).astype(jnp.bfloat16)
```

```python
import functools

import jax
import jax.numpy as jnp
from jax import lax
from jax.experimental import pallas as pl
from jax.experimental.pallas import tpu as pltpu
from jax.sharding import Mesh
from jax.sharding import PartitionSpec as P

HALF = 256
MIB = 1024 * 1024


def send_kernel(
    wanted, wanted_column, down, up, out, even_rows, odd_rows, up_narrow, down_sems, up_sems
):
    groups, choices = wanted.shape
    rank = down.shape[1]
    halves = down.shape[2] // HALF
    per_group = choices * halves

    def copy_of(n):
        group, rest = n // per_group, lax.rem(n, per_group)
        choice, half = rest // halves, lax.rem(rest, halves)
        return pltpu.make_async_copy(
            down.at[wanted[group, choice], :, pl.ds(half * HALF, HALF)],
            out.at[group, pl.ds(half * choices * rank + choice * rank, rank), :],
            down_sems.at[n],
        )

    def start(n, carry):
        copy_of(n).start()
        return carry

    def wait(n, carry):
        copy_of(n).wait()
        return carry

    lax.fori_loop(0, groups * per_group, start, 0)

    ids = lax.broadcasted_iota(jnp.int32, (choices * groups, up.shape[1]), 1)
    pick = (ids == wanted_column[...]).astype(jnp.float32).astype(jnp.bfloat16)
    rows = lax.dot_general(
        pick, up[...], (((1,), (1,)), ((), ())), preferred_element_type=jnp.float32
    )
    first, second = rows[:groups], rows[groups:]
    low = lax.broadcasted_iota(jnp.int32, (groups, 2 * rank), 1) < rank
    count = up_narrow.shape[0] // groups
    for i in range(count):
        a = first[:, 2 * rank * i : 2 * rank * (i + 1)]
        b = second[:, 2 * rank * i : 2 * rank * (i + 1)]
        even_rows[pl.ds(i, groups, stride=count), :] = jnp.where(low, a, pltpu.roll(b, rank, 1))
        odd_rows[pl.ds(i, groups, stride=count), :] = jnp.where(low, pltpu.roll(a, rank, 1), b)
    up_narrow[:, : 2 * rank] = even_rows[...].astype(jnp.bfloat16)
    up_narrow[:, 2 * rank :] = odd_rows[...].astype(jnp.bfloat16)

    def up_copy(group):
        return pltpu.make_async_copy(
            up_narrow.at[pl.ds(group * count, count), :],
            out.at[group, pl.ds(per_group * rank, count), :],
            up_sems.at[group],
        )

    def up_start(group, carry):
        up_copy(group).start()
        return carry

    def up_wait(group, carry):
        up_copy(group).wait()
        return carry

    lax.fori_loop(0, groups, up_start, 0)
    lax.fori_loop(0, groups * per_group, wait, 0)
    lax.fori_loop(0, groups, up_wait, 0)


def make_messages(wanted, down, up, shard_width):
    groups, choices = wanted.shape
    rank, depth = down.shape[1:]
    halves = depth // HALF
    count = shard_width * choices * rank // HALF
    rows = choices * rank * halves + count
    column = jnp.transpose(wanted).reshape(choices * groups, 1)
    return pl.pallas_call(
        send_kernel,
        out_shape=jax.ShapeDtypeStruct((groups, rows, HALF), jnp.bfloat16),
        in_specs=[
            pl.BlockSpec(memory_space=pltpu.SMEM),
            pl.BlockSpec(memory_space=pltpu.VMEM),
            pl.BlockSpec(memory_space=pl.ANY),
            pl.BlockSpec(memory_space=pltpu.VMEM),
        ],
        out_specs=pl.BlockSpec(memory_space=pl.ANY),
        scratch_shapes=[
            pltpu.VMEM((groups * count, 2 * rank), jnp.float32),
            pltpu.VMEM((groups * count, 2 * rank), jnp.float32),
            pltpu.VMEM((groups * count, HALF), jnp.bfloat16),
            pltpu.SemaphoreType.DMA((groups * choices * halves,)),
            pltpu.SemaphoreType.DMA((groups,)),
        ],
        name="make_messages",
    )(wanted, column, down, up)


def base_kernel(tokens_refs, weight, out):
    total = jnp.zeros(out.shape, jnp.float32)
    for i, part in enumerate(tokens_refs):
        total += jnp.dot(
            part[...], weight[0, i * HALF : (i + 1) * HALF, :], preferred_element_type=jnp.float32
        )

    @pl.when(pl.program_id(0) == 0)
    def _():
        out[...] = total

    @pl.when(pl.program_id(0) > 0)
    def _():
        out[...] += total


def base_product(tokens, weight, lines, plane):
    rows = tokens.shape[0]
    width = weight.shape[2]

    def token_spec(z):
        def index(n):
            x, place = n // plane, lax.rem(n, plane)
            return (0, (z * plane + place) * 2 + x)

        return pl.BlockSpec((rows, HALF), index)

    def kernel(*refs):
        base_kernel(refs[:lines], refs[lines], refs[lines + 1])

    return pl.pallas_call(
        kernel,
        grid=(weight.shape[0],),
        out_shape=jax.ShapeDtypeStruct((rows, width), jnp.float32),
        in_specs=[token_spec(z) for z in range(lines)]
        + [pl.BlockSpec((1, lines * HALF, width), lambda n: (n, 0, 0))],
        out_specs=pl.BlockSpec((rows, width), lambda n: (0, 0)),
        compiler_params=pltpu.CompilerParams(vmem_limit_bytes=32 * MIB),
        cost_estimate=pl.CostEstimate(
            flops=2 * rows * tokens.shape[1] * width,
            bytes_accessed=2 * tokens.size + 2 * weight.size + 4 * rows * width,
            transcendentals=0,
        ),
        name="base_product",
    )(*([tokens] * lines), weight)


def adapt_kernel(tokens, down, up, mask, base, out, shrink):
    step = pl.program_id(0)
    sources = down.shape[0]
    pair = mask.shape[1]
    halves = tokens.shape[1] // (sources * HALF)
    total = jnp.zeros(shrink.shape, jnp.float32)
    for source in range(sources):
        for half in range(halves):
            column = (source * halves + half) * HALF
            total += lax.dot_general(
                tokens[:, column : column + HALF],
                down[source, half * pair : (half + 1) * pair, :],
                (((1,), (1,)), ((), ())),
                preferred_element_type=jnp.float32,
            )

    @pl.when(step == 0)
    def _():
        shrink[...] = total

    @pl.when(step > 0)
    def _():
        shrink[...] += total

    @pl.when(step == pl.num_programs(0) - 1)
    def _():
        picked = (shrink[...] * mask[...]).astype(jnp.bfloat16)
        got = up[...].reshape(up.shape[0] * up.shape[1], HALF)
        width = out.shape[1]
        value = lax.broadcasted_iota(jnp.int32, (width, got.shape[0]), 0)
        row = lax.broadcasted_iota(jnp.int32, (width, got.shape[0]), 1)
        wide = jnp.zeros((width, pair), jnp.float32)
        for i in range(HALF // pair):
            place = (value == row * (HALF // pair) + i).astype(jnp.float32).astype(jnp.bfloat16)
            wide += jnp.dot(
                place, got[:, i * pair : (i + 1) * pair], preferred_element_type=jnp.float32
            )
        delta = lax.dot_general(
            picked,
            wide.astype(jnp.bfloat16),
            (((1,), (1,)), ((), ())),
            preferred_element_type=jnp.float32,
        )
        out[...] = (base[...] + delta).astype(out.dtype)


def adapt(tokens, messages, mask, base, halves):
    rows, width = base.shape
    pair = mask.shape[1]
    groups, length = messages.shape[:2]
    count = length - halves * pair
    steps = 8
    per_step = groups // steps
    return pl.pallas_call(
        adapt_kernel,
        grid=(steps,),
        out_shape=jax.ShapeDtypeStruct((rows, width), jnp.bfloat16),
        in_specs=[
            pl.BlockSpec((rows, tokens.shape[1] // steps), lambda n: (0, n)),
            pl.BlockSpec((per_step, halves * pair, HALF), lambda n: (n, 0, 0)),
            pl.BlockSpec((groups, count, HALF), lambda n: (0, halves * pair // count, 0)),
            pl.BlockSpec((rows, pair), lambda n: (0, 0)),
            pl.BlockSpec((rows, width), lambda n: (0, 0)),
        ],
        out_specs=pl.BlockSpec((rows, width), lambda n: (0, 0)),
        scratch_shapes=[pltpu.VMEM((rows, pair), jnp.float32)],
        compiler_params=pltpu.CompilerParams(vmem_limit_bytes=32 * MIB),
        cost_estimate=pl.CostEstimate(
            flops=2 * rows * tokens.shape[1] * pair,
            bytes_accessed=2 * tokens.size + 2 * messages.size + 6 * rows * width,
            transcendentals=0,
        ),
        name="adapt",
    )(tokens, messages, messages, mask, base)


def row_slots(lengths, slots, rows):
    ends = jnp.cumsum(lengths)
    starts = ends - lengths
    position = jnp.arange(rows, dtype=jnp.int32)[:, None]
    member = (position >= starts[None, :]) & (position < ends[None, :])
    return jnp.sum(jnp.where(member, slots[None, :], 0), axis=1)


def body(
    lines,
    tokens,
    base_weight,
    adapter_down,
    adapter_up,
    request_lengths,
    group_adapters,
    request_slot,
):
    store = ("line", "plane", "core")
    rank = adapter_down.shape[2]
    choices = group_adapters.shape[1]
    depth, width = base_weight.shape
    group = lax.axis_index(store)
    own_half = lax.dynamic_slice_in_dim(base_weight, lax.axis_index("parts") * HALF, HALF, 0)
    along = lax.all_gather(own_half, "line", axis=0, tiled=True)
    gathered = lax.all_gather(along, ("parts", "plane", "core"), axis=0, tiled=False)
    shard_width = adapter_up.shape[1]
    messages = make_messages(
        group_adapters,
        jnp.swapaxes(adapter_down, 1, 2),
        jnp.transpose(adapter_up, (1, 2, 0)).reshape(shard_width * rank, adapter_up.shape[0]),
        shard_width,
    )
    arrived = lax.all_to_all(messages, store, split_axis=0, concat_axis=0, tiled=True)
    slots = lax.dynamic_index_in_dim(request_slot, group, 0, keepdims=False)
    slot_of_row = row_slots(request_lengths[0], slots, tokens.shape[0])
    lane_slot = jnp.arange(choices * rank, dtype=jnp.int32)[None, :] // rank
    mask = (slot_of_row[:, None] == lane_slot).astype(jnp.float32)
    base = base_product(tokens, gathered, lines, gathered.shape[0] // 2)
    return adapt(tokens, arrived, mask, base, depth // HALF)


def plain_body(
    tokens, base_weight, adapter_down, adapter_up, request_lengths, group_adapters, request_slot
):
    store = ("line", "plane", "core")
    rank = adapter_down.shape[2]
    choices = group_adapters.shape[1]
    group = lax.axis_index(store)
    wanted = jnp.transpose(group_adapters)
    slots = lax.dynamic_index_in_dim(request_slot, group, 0, keepdims=False)
    slot_of_row = row_slots(request_lengths[0], slots, tokens.shape[0])
    lane_slot = jnp.arange(choices * rank, dtype=jnp.int32)[None, :] // rank
    mask = (slot_of_row[:, None] == lane_slot).astype(jnp.float32)
    exchange = functools.partial(
        lax.all_to_all, axis_name=store, split_axis=1, concat_axis=1, tiled=True
    )
    down = exchange(jnp.take(adapter_down, wanted, axis=0))
    up = exchange(jnp.take(adapter_up, wanted, axis=0))
    weight = lax.all_gather(base_weight, store, axis=0, tiled=True)
    down = down.reshape(choices, tokens.shape[1], rank)
    up = up.reshape(choices, base_weight.shape[1], rank)
    base = jnp.dot(tokens, weight, preferred_element_type=jnp.float32)
    shrink = jnp.einsum("td,kdr->tkr", tokens, down, preferred_element_type=jnp.float32)
    picked = (shrink.reshape(mask.shape) * mask).astype(jnp.bfloat16)
    picked = picked.reshape(shrink.shape)
    delta = jnp.einsum("tkr,kvr->tv", picked, up, preferred_element_type=jnp.float32)
    return (base + delta).astype(jnp.bfloat16)


def solution(mesh):
    parts, size = mesh.shape["parts"], mesh.shape["store"]
    chips = size // 2
    plane = 1
    while 4 * plane * plane <= chips:
        plane *= 2
    lines = chips // plane
    names = ("parts", "line", "plane", "core")
    split = Mesh(mesh.devices.reshape(parts, lines, plane, 2), names)
    store = names[1:]

    def run(tokens, base_weight, *rest):
        large = parts == 2 and base_weight.shape[0] // size == 2 * HALF
        return jax.shard_map(
            functools.partial(body, lines) if large else plain_body,
            mesh=split,
            in_specs=(
                P(names, None),
                P(store, None),
                P(None, store, None),
                P(None, store, None),
                P(names, None),
                P("parts", None),
                P("parts", None),
            ),
            out_specs=P(names, None),
            check_vma=False,
        )(tokens, base_weight, *rest)

    return run
```

```python
import functools

import jax
import jax.numpy as jnp
from jax import lax
from jax.experimental import pallas as pl
from jax.experimental.pallas import tpu as pltpu
from jax.sharding import Mesh
from jax.sharding import PartitionSpec as P

HALF = 256
MIB = 1024 * 1024
AXES = ("parts", "line", "plane", "core")


def send_kernel(wanted, down, up, out, pick, even_rows, odd_rows, sems):
    choices, groups = wanted.shape
    rank = down.shape[1]
    halves = down.shape[2] // HALF
    copies = []
    for group in range(groups):
        for choice in range(choices):
            for half in range(halves):
                copy = pltpu.make_async_copy(
                    down.at[wanted[choice, group], :, pl.ds(half * HALF, HALF)],
                    out.at[group, pl.ds((half * choices + choice) * rank, rank), :],
                    sems.at[len(copies)],
                )
                copy.start()
                copies.append(copy)

    ids = lax.broadcasted_iota(jnp.int32, (1, up.shape[1]), 1)
    for choice in range(choices):
        for group in range(groups):
            here = (ids == wanted[choice, group]).astype(jnp.float32)
            pick[pl.ds(choice * groups + group, 1), :] = here
    rows = lax.dot_general(
        pick[...].astype(jnp.bfloat16),
        up[...],
        (((1,), (1,)), ((), ())),
        preferred_element_type=jnp.float32,
    )
    first, second = rows[:groups], rows[groups:]
    low = lax.broadcasted_iota(jnp.int32, (groups, 2 * rank), 1) < rank
    count = even_rows.shape[0] // groups
    for i in range(count):
        a = first[:, 2 * rank * i : 2 * rank * (i + 1)]
        b = second[:, 2 * rank * i : 2 * rank * (i + 1)]
        even_rows[pl.ds(i, groups, stride=count), :] = jnp.where(low, a, pltpu.roll(b, rank, 1))
        odd_rows[pl.ds(i, groups, stride=count), :] = jnp.where(low, pltpu.roll(a, rank, 1), b)
    start = choices * halves * rank
    for group in range(groups):
        own = pl.ds(group * count, count)
        out[group, start:, : 2 * rank] = even_rows[own, :].astype(jnp.bfloat16)
        out[group, start:, 2 * rank :] = odd_rows[own, :].astype(jnp.bfloat16)
    for copy in copies:
        copy.wait()


def make_messages(wanted, down, up, shard_width):
    choices, groups = wanted.shape
    rank, depth = down.shape[1:]
    halves = depth // HALF
    count = shard_width * choices * rank // HALF
    rows = choices * rank * halves + count
    return pl.pallas_call(
        send_kernel,
        out_shape=jax.ShapeDtypeStruct((groups, rows, HALF), jnp.bfloat16),
        in_specs=[
            pl.BlockSpec(memory_space=pltpu.SMEM),
            pl.BlockSpec(memory_space=pl.ANY),
            pl.BlockSpec(memory_space=pltpu.VMEM),
        ],
        out_specs=pl.BlockSpec(memory_space=pltpu.VMEM),
        scratch_shapes=[
            pltpu.VMEM((choices * groups, up.shape[1]), jnp.float32),
            pltpu.VMEM((groups * count, 2 * rank), jnp.float32),
            pltpu.VMEM((groups * count, 2 * rank), jnp.float32),
            pltpu.SemaphoreType.DMA((groups * choices * halves,)),
        ],
        compiler_params=pltpu.CompilerParams(vmem_limit_bytes=56 * MIB),
        name="make_messages",
    )(wanted, down, up)


def base_product(tokens, blocks):
    rows, depth = tokens.shape
    width = blocks[0][1].shape[1]
    count = len(blocks)
    masks = [mask for mask, _ in blocks]

    def kernel(*refs):
        tokens_ref, parts, out = refs[0], refs[1 : 1 + count], refs[1 + count]
        left, right, left_sems, right_sems = refs[2 + count :]
        place = [lax.axis_index(name) for name in AXES]
        copies = []
        for n, mask in enumerate(masks):
            x, z, y, core = [i ^ bit for i, bit in zip(place, mask)]
            column = pl.multiple_of((((z * 2 + y) * 2 + core) * 2 + x) * HALF, HALF)
            pair = (
                pltpu.make_async_copy(
                    tokens_ref.at[:, pl.ds(column, HALF)], left.at[n], left_sems.at[n]
                ),
                pltpu.make_async_copy(parts[n], right.at[n], right_sems.at[n]),
            )
            for copy in pair:
                copy.start()
            copies.append(pair)
        for n in range(0, count, 2):
            for pair in copies[n : n + 2]:
                for copy in pair:
                    copy.wait()
            total = jnp.dot(left[n], right[n], preferred_element_type=jnp.float32)
            total += jnp.dot(left[n + 1], right[n + 1], preferred_element_type=jnp.float32)
            if n == 0:
                out[...] = total
            else:
                out[...] += total

    return pl.pallas_call(
        kernel,
        out_shape=jax.ShapeDtypeStruct((rows, width), jnp.float32),
        in_specs=[pl.BlockSpec(memory_space=pl.ANY)] * (1 + count),
        out_specs=pl.BlockSpec(memory_space=pltpu.VMEM),
        scratch_shapes=[
            pltpu.VMEM((count, rows, HALF), jnp.bfloat16),
            pltpu.VMEM((count, HALF, width), jnp.bfloat16),
            pltpu.SemaphoreType.DMA((count,)),
            pltpu.SemaphoreType.DMA((count,)),
        ],
        compiler_params=pltpu.CompilerParams(vmem_limit_bytes=56 * MIB),
        cost_estimate=pl.CostEstimate(
            flops=2 * rows * depth * width,
            bytes_accessed=2 * rows * depth + 2 * depth * width + 4 * rows * width,
            transcendentals=0,
        ),
        name="base_product",
    )(tokens, *[block for _, block in blocks])


def adapt_kernel(halves, tokens, messages, mask, base, out, held, sems):
    groups, length = messages.shape[:2]
    pair = mask.shape[1]
    width = out.shape[1]
    depth = halves * HALF
    copies = []
    for source in range(groups):
        copy = pltpu.make_async_copy(
            tokens.at[:, pl.ds(source * depth, depth)], held.at[source], sems.at[source]
        )
        copy.start()
        copies.append(copy)

    start = halves * pair
    got = messages[:, start:, :].reshape(groups * (length - start), HALF)
    value = lax.broadcasted_iota(jnp.int32, (width, got.shape[0]), 0)
    row = lax.broadcasted_iota(jnp.int32, (width, got.shape[0]), 1)
    wide = jnp.zeros((width, pair), jnp.float32)
    for i in range(HALF // pair):
        place = (value == row * (HALF // pair) + i).astype(jnp.float32).astype(jnp.bfloat16)
        wide += jnp.dot(
            place, got[:, i * pair : (i + 1) * pair], preferred_element_type=jnp.float32
        )
    wide = wide.astype(jnp.bfloat16)

    shrink = jnp.zeros(mask.shape, jnp.float32)
    for source in range(groups):
        copies[source].wait()
        down = jnp.concatenate(
            [messages[source, half * pair : (half + 1) * pair, :] for half in range(halves)], axis=1
        )
        shrink += lax.dot_general(
            held[source], down, (((1,), (1,)), ((), ())), preferred_element_type=jnp.float32
        )
    picked = (shrink * mask[...]).astype(jnp.bfloat16)
    delta = lax.dot_general(
        picked, wide, (((1,), (1,)), ((), ())), preferred_element_type=jnp.float32
    )
    out[...] = (base[...] + delta).astype(out.dtype)


def adapt(tokens, messages, mask, base, halves):
    rows, width = base.shape
    groups = messages.shape[0]
    return pl.pallas_call(
        functools.partial(adapt_kernel, halves),
        out_shape=jax.ShapeDtypeStruct((rows, width), jnp.bfloat16),
        in_specs=[pl.BlockSpec(memory_space=pl.ANY)] + [pl.BlockSpec(memory_space=pltpu.VMEM)] * 3,
        out_specs=pl.BlockSpec(memory_space=pltpu.VMEM),
        scratch_shapes=[
            pltpu.VMEM((groups, rows, halves * HALF), jnp.bfloat16),
            pltpu.SemaphoreType.DMA((groups,)),
        ],
        compiler_params=pltpu.CompilerParams(vmem_limit_bytes=56 * MIB),
        cost_estimate=pl.CostEstimate(
            flops=2 * rows * tokens.shape[1] * mask.shape[1],
            bytes_accessed=2 * tokens.size + 2 * messages.size + 6 * rows * width,
            transcendentals=0,
        ),
        name="adapt",
    )(tokens, messages, mask, base)


def row_slots(lengths, slots, rows):
    ends = jnp.cumsum(lengths)
    starts = ends - lengths
    position = jnp.arange(rows, dtype=jnp.int32)[:, None]
    member = (position >= starts[None, :]) & (position < ends[None, :])
    return jnp.sum(jnp.where(member, slots[None, :], 0), axis=1)


def swap(block, axis, bit):
    size = lax.axis_size(axis)
    return lax.ppermute(block, axis, [(i, i ^ bit) for i in range(size)])


def gather_rows(base_weight):
    x = lax.axis_index("parts")
    own = lax.dynamic_slice_in_dim(base_weight, x * HALF, HALF, 0)
    other = lax.dynamic_slice_in_dim(base_weight, (1 - x) * HALF, HALF, 0)
    blocks = {(0, 0, 0, 0): own}
    blocks[0, 1, 0, 0] = swap(own, "line", 1)
    blocks[0, 2, 0, 0] = swap(own, "line", 2)
    blocks[0, 3, 0, 0] = swap(blocks[0, 2, 0, 0], "line", 1)
    for z in range(4):
        blocks[0, z, 1, 0] = swap(blocks[0, z, 0, 0], "plane", 1)
    for z in range(4):
        for y in range(2):
            source = blocks[0, z, y, 0]
            blocks[1, z, y, 0] = other if z == y == 0 else swap(source, "parts", 1)
    for (x, z, y, _), block in list(blocks.items()):
        blocks[x, z, y, 1] = swap(block, "core", 1)
    return list(blocks.items())


def body(
    tokens, base_weight, adapter_down, adapter_up, request_lengths, group_adapters, request_slot
):
    store = AXES[1:]
    rank = adapter_down.shape[2]
    choices = group_adapters.shape[1]
    depth = base_weight.shape[0]
    group = lax.axis_index(store)
    shard_width = adapter_up.shape[1]
    messages = make_messages(
        jnp.transpose(group_adapters),
        jnp.swapaxes(adapter_down, 1, 2),
        jnp.transpose(adapter_up, (1, 2, 0)).reshape(shard_width * rank, adapter_up.shape[0]),
        shard_width,
    )
    arrived = lax.all_to_all(messages, store, split_axis=0, concat_axis=0, tiled=True)
    blocks = gather_rows(base_weight)
    slots = lax.dynamic_index_in_dim(request_slot, group, 0, keepdims=False)
    slot_of_row = row_slots(request_lengths[0], slots, tokens.shape[0])
    lane_slot = jnp.arange(choices * rank, dtype=jnp.int32)[None, :] // rank
    mask = (slot_of_row[:, None] == lane_slot).astype(jnp.float32)
    base = base_product(tokens, blocks)
    return adapt(tokens, arrived, mask, base, depth // HALF)


def plain_body(
    tokens, base_weight, adapter_down, adapter_up, request_lengths, group_adapters, request_slot
):
    store = AXES[1:]
    rank = adapter_down.shape[2]
    choices = group_adapters.shape[1]
    group = lax.axis_index(store)
    wanted = jnp.transpose(group_adapters)
    slots = lax.dynamic_index_in_dim(request_slot, group, 0, keepdims=False)
    slot_of_row = row_slots(request_lengths[0], slots, tokens.shape[0])
    lane_slot = jnp.arange(choices * rank, dtype=jnp.int32)[None, :] // rank
    mask = (slot_of_row[:, None] == lane_slot).astype(jnp.float32)
    exchange = functools.partial(
        lax.all_to_all, axis_name=store, split_axis=1, concat_axis=1, tiled=True
    )
    down = exchange(jnp.take(adapter_down, wanted, axis=0))
    up = exchange(jnp.take(adapter_up, wanted, axis=0))
    weight = lax.all_gather(base_weight, store, axis=0, tiled=True)
    down = down.reshape(choices, tokens.shape[1], rank)
    up = up.reshape(choices, base_weight.shape[1], rank)
    base = jnp.dot(tokens, weight, preferred_element_type=jnp.float32)
    shrink = jnp.einsum("td,kdr->tkr", tokens, down, preferred_element_type=jnp.float32)
    picked = (shrink.reshape(mask.shape) * mask).astype(jnp.bfloat16)
    picked = picked.reshape(shrink.shape)
    delta = jnp.einsum("tkr,kvr->tv", picked, up, preferred_element_type=jnp.float32)
    return (base + delta).astype(jnp.bfloat16)


def solution(mesh):
    parts, size = mesh.shape["parts"], mesh.shape["store"]
    chips = size // 2
    plane = 1
    while 4 * plane * plane <= chips:
        plane *= 2
    lines = chips // plane
    split = Mesh(mesh.devices.reshape(parts, lines, plane, 2), AXES)
    store = AXES[1:]

    def run(tokens, base_weight, *rest):
        small = (parts, lines, plane) == (2, 4, 2) and base_weight.shape[0] // size == 2 * HALF
        return jax.shard_map(
            body if small else plain_body,
            mesh=split,
            in_specs=(
                P(AXES, None),
                P(store, None),
                P(None, store, None),
                P(None, store, None),
                P(AXES, None),
                P("parts", None),
                P("parts", None),
            ),
            out_specs=P(AXES, None),
            check_vma=False,
        )(tokens, base_weight, *rest)

    return run
```

```python
import functools

import jax
import jax.numpy as jnp
from jax import lax
from jax.experimental import pallas as pl
from jax.experimental.pallas import tpu as pltpu
from jax.sharding import Mesh
from jax.sharding import PartitionSpec as P

HALF = 256
DEEP = 4
MIB = 1024 * 1024
AXES = ("parts", "line", "plane", "core")


def send_kernel(wanted, down, up, out, pick, even_rows, odd_rows, sems):
    choices, groups = wanted.shape
    rank = down.shape[1]
    halves = down.shape[2] // HALF
    copies = []
    for group in range(groups):
        for choice in range(choices):
            for half in range(halves):
                copy = pltpu.make_async_copy(
                    down.at[wanted[choice, group], :, pl.ds(half * HALF, HALF)],
                    out.at[group, pl.ds((half * choices + choice) * rank, rank), :],
                    sems.at[len(copies)],
                )
                copy.start()
                copies.append(copy)

    ids = lax.broadcasted_iota(jnp.int32, (1, up.shape[1]), 1)
    for choice in range(choices):
        for group in range(groups):
            here = (ids == wanted[choice, group]).astype(jnp.float32)
            pick[pl.ds(choice * groups + group, 1), :] = here
    rows = lax.dot_general(
        pick[...].astype(jnp.bfloat16),
        up[...],
        (((1,), (1,)), ((), ())),
        preferred_element_type=jnp.float32,
    )
    first, second = rows[:groups], rows[groups:]
    low = lax.broadcasted_iota(jnp.int32, (groups, 2 * rank), 1) < rank
    count = even_rows.shape[0] // groups
    for i in range(count):
        a = first[:, 2 * rank * i : 2 * rank * (i + 1)]
        b = second[:, 2 * rank * i : 2 * rank * (i + 1)]
        even_rows[pl.ds(i, groups, stride=count), :] = jnp.where(low, a, pltpu.roll(b, rank, 1))
        odd_rows[pl.ds(i, groups, stride=count), :] = jnp.where(low, pltpu.roll(a, rank, 1), b)
    start = choices * halves * rank
    for group in range(groups):
        own = pl.ds(group * count, count)
        out[group, start:, : 2 * rank] = even_rows[own, :].astype(jnp.bfloat16)
        out[group, start:, 2 * rank :] = odd_rows[own, :].astype(jnp.bfloat16)
    for copy in copies:
        copy.wait()


def make_messages(wanted, down, up, shard_width):
    choices, groups = wanted.shape
    rank, depth = down.shape[1:]
    halves = depth // HALF
    count = shard_width * choices * rank // HALF
    rows = choices * rank * halves + count
    return pl.pallas_call(
        send_kernel,
        out_shape=jax.ShapeDtypeStruct((groups, rows, HALF), jnp.bfloat16),
        in_specs=[
            pl.BlockSpec(memory_space=pltpu.SMEM),
            pl.BlockSpec(memory_space=pl.ANY),
            pl.BlockSpec(memory_space=pltpu.VMEM),
        ],
        out_specs=pl.BlockSpec(memory_space=pltpu.VMEM),
        scratch_shapes=[
            pltpu.VMEM((choices * groups, up.shape[1]), jnp.float32),
            pltpu.VMEM((groups * count, 2 * rank), jnp.float32),
            pltpu.VMEM((groups * count, 2 * rank), jnp.float32),
            pltpu.SemaphoreType.DMA((groups * choices * halves,)),
        ],
        compiler_params=pltpu.CompilerParams(vmem_limit_bytes=56 * MIB),
        name="make_messages",
    )(wanted, down, up)


def base_product(tokens, blocks):
    rows, depth = tokens.shape
    width = blocks[0][1].shape[1]
    count = len(blocks)
    masks = [mask for mask, _ in blocks]

    def kernel(*refs):
        tokens_ref, parts, out = refs[0], refs[1 : 1 + count], refs[1 + count]
        left, right, left_sems, right_sems = refs[2 + count :]
        place = [lax.axis_index(name) for name in AXES]
        copies = []
        for n, mask in enumerate(masks):
            x, z, y, core = [i ^ bit for i, bit in zip(place, mask)]
            column = pl.multiple_of((((z * 2 + y) * 2 + core) * 2 + x) * HALF, HALF)
            slot, inner = n // DEEP, pl.ds(n % DEEP * HALF, HALF)
            pair = (
                pltpu.make_async_copy(
                    tokens_ref.at[:, pl.ds(column, HALF)], left.at[slot, :, inner], left_sems.at[n]
                ),
                pltpu.make_async_copy(parts[n], right.at[slot, inner, :], right_sems.at[n]),
            )
            for copy in pair:
                copy.start()
            copies.append(pair)
        for n in range(count // DEEP):
            for pair in copies[n * DEEP : (n + 1) * DEEP]:
                for copy in pair:
                    copy.wait()
            total = jnp.dot(left[n], right[n], preferred_element_type=jnp.float32)
            if n == 0:
                out[...] = total
            else:
                out[...] += total

    return pl.pallas_call(
        kernel,
        out_shape=jax.ShapeDtypeStruct((rows, width), jnp.float32),
        in_specs=[pl.BlockSpec(memory_space=pl.ANY)] * (1 + count),
        out_specs=pl.BlockSpec(memory_space=pltpu.VMEM),
        scratch_shapes=[
            pltpu.VMEM((count // DEEP, rows, DEEP * HALF), jnp.bfloat16),
            pltpu.VMEM((count // DEEP, DEEP * HALF, width), jnp.bfloat16),
            pltpu.SemaphoreType.DMA((count,)),
            pltpu.SemaphoreType.DMA((count,)),
        ],
        compiler_params=pltpu.CompilerParams(vmem_limit_bytes=56 * MIB),
        cost_estimate=pl.CostEstimate(
            flops=2 * rows * depth * width,
            bytes_accessed=2 * rows * depth + 2 * depth * width + 4 * rows * width,
            transcendentals=0,
        ),
        name="base_product",
    )(tokens, *[block for _, block in blocks])


def adapt_kernel(halves, tokens, messages, mask, base, out, held, got, kept, start, wide, *sems):
    groups, length = messages.shape[:2]
    pair = mask.shape[1]
    depth = halves * HALF
    left_sems, right_sems, base_sem, mask_sem = sems
    copies = []
    for source in range(groups):
        two = (
            pltpu.make_async_copy(messages.at[source], got.at[source], right_sems.at[source]),
            pltpu.make_async_copy(
                tokens.at[:, pl.ds(source * depth, depth)], held.at[source], left_sems.at[source]
            ),
        )
        for copy in two:
            copy.start()
        copies.append(two)
    last = (
        pltpu.make_async_copy(mask, kept, mask_sem),
        pltpu.make_async_copy(base, start, base_sem),
    )
    for copy in last:
        copy.start()

    shrink = jnp.zeros(mask.shape, jnp.float32)
    for source in range(groups):
        for copy in copies[source]:
            copy.wait()
        down = jnp.concatenate(
            [got[source, half * pair : (half + 1) * pair, :] for half in range(halves)], axis=1
        )
        shrink += lax.dot_general(
            held[source], down, (((1,), (1,)), ((), ())), preferred_element_type=jnp.float32
        )
    ups = got[:, halves * pair :, :].astype(jnp.float32)
    ups = ups.reshape(groups * (length - halves * pair), HALF)
    step = HALF // pair
    for i in range(step):
        wide[pl.ds(i, ups.shape[0], stride=step), :] = ups[:, i * pair : (i + 1) * pair]
    for copy in last:
        copy.wait()
    picked = (shrink * kept[...]).astype(jnp.bfloat16)
    delta = lax.dot_general(
        picked,
        wide[...].astype(jnp.bfloat16),
        (((1,), (1,)), ((), ())),
        preferred_element_type=jnp.float32,
    )
    out[...] = (start[...] + delta).astype(out.dtype)


def adapt(tokens, messages, mask, base, halves):
    rows, width = base.shape
    groups = messages.shape[0]
    return pl.pallas_call(
        functools.partial(adapt_kernel, halves),
        out_shape=jax.ShapeDtypeStruct((rows, width), jnp.bfloat16),
        in_specs=[pl.BlockSpec(memory_space=pl.ANY)] * 4,
        out_specs=pl.BlockSpec(memory_space=pltpu.VMEM),
        scratch_shapes=[
            pltpu.VMEM((groups, rows, halves * HALF), jnp.bfloat16),
            pltpu.VMEM(messages.shape, jnp.bfloat16),
            pltpu.VMEM(mask.shape, jnp.float32),
            pltpu.VMEM(base.shape, jnp.float32),
            pltpu.VMEM((width, mask.shape[1]), jnp.float32),
            pltpu.SemaphoreType.DMA((groups,)),
            pltpu.SemaphoreType.DMA((groups,)),
            pltpu.SemaphoreType.DMA,
            pltpu.SemaphoreType.DMA,
        ],
        compiler_params=pltpu.CompilerParams(vmem_limit_bytes=56 * MIB),
        cost_estimate=pl.CostEstimate(
            flops=2 * rows * tokens.shape[1] * mask.shape[1],
            bytes_accessed=2 * tokens.size + 2 * messages.size + 6 * rows * width,
            transcendentals=0,
        ),
        name="adapt",
    )(tokens, messages, mask, base)


def after(value, *others):
    def kernel(*refs):
        pass

    return pl.pallas_call(
        kernel,
        out_shape=jax.ShapeDtypeStruct(value.shape, value.dtype),
        in_specs=[pl.BlockSpec(memory_space=pl.ANY)] * (1 + len(others)),
        out_specs=pl.BlockSpec(memory_space=pl.ANY),
        input_output_aliases={0: 0},
        name="after",
    )(value, *others)


def row_slots(lengths, slots, rows):
    ends = jnp.cumsum(lengths)
    starts = ends - lengths
    position = jnp.arange(rows, dtype=jnp.int32)[:, None]
    member = (position >= starts[None, :]) & (position < ends[None, :])
    return jnp.sum(jnp.where(member, slots[None, :], 0), axis=1)


def swap(block, axis, bit):
    size = lax.axis_size(axis)
    return lax.ppermute(block, axis, [(i, i ^ bit) for i in range(size)])


def gather_rows(base_weight):
    x = lax.axis_index("parts")
    own = lax.dynamic_slice_in_dim(base_weight, x * HALF, HALF, 0)
    other = lax.dynamic_slice_in_dim(base_weight, (1 - x) * HALF, HALF, 0)
    blocks = {(0, 0, 0, 0): own}
    blocks[0, 1, 0, 0] = swap(own, "line", 1)
    blocks[0, 2, 0, 0] = swap(own, "line", 2)
    blocks[0, 3, 0, 0] = swap(blocks[0, 2, 0, 0], "line", 1)
    for z in range(4):
        blocks[0, z, 1, 0] = swap(blocks[0, z, 0, 0], "plane", 1)
    for z in range(4):
        for y in range(2):
            source = blocks[0, z, y, 0]
            blocks[1, z, y, 0] = other if z == y == 0 else swap(source, "parts", 1)
    for (x, z, y, _), block in list(blocks.items()):
        blocks[x, z, y, 1] = swap(block, "core", 1)
    return blocks


def body(
    tokens, base_weight, adapter_down, adapter_up, request_lengths, group_adapters, request_slot
):
    store = AXES[1:]
    rank = adapter_down.shape[2]
    choices = group_adapters.shape[1]
    depth = base_weight.shape[0]
    group = lax.axis_index(store)
    shard_width = adapter_up.shape[1]
    messages = make_messages(
        jnp.transpose(group_adapters),
        jnp.swapaxes(adapter_down, 1, 2),
        jnp.transpose(adapter_up, (1, 2, 0)).reshape(shard_width * rank, adapter_up.shape[0]),
        shard_width,
    )
    blocks = gather_rows(base_weight)
    messages = after(messages, blocks[0, 1, 0, 0])
    arrived = lax.all_to_all(messages, store, split_axis=0, concat_axis=0, tiled=True)
    slots = lax.dynamic_index_in_dim(request_slot, group, 0, keepdims=False)
    slot_of_row = row_slots(request_lengths[0], slots, tokens.shape[0])
    lane_slot = jnp.arange(choices * rank, dtype=jnp.int32)[None, :] // rank
    mask = (slot_of_row[:, None] == lane_slot).astype(jnp.float32)
    base = base_product(tokens, list(blocks.items()))
    return adapt(tokens, arrived, mask, base, depth // HALF)


def plain_body(
    tokens, base_weight, adapter_down, adapter_up, request_lengths, group_adapters, request_slot
):
    store = AXES[1:]
    rank = adapter_down.shape[2]
    choices = group_adapters.shape[1]
    group = lax.axis_index(store)
    wanted = jnp.transpose(group_adapters)
    slots = lax.dynamic_index_in_dim(request_slot, group, 0, keepdims=False)
    slot_of_row = row_slots(request_lengths[0], slots, tokens.shape[0])
    lane_slot = jnp.arange(choices * rank, dtype=jnp.int32)[None, :] // rank
    mask = (slot_of_row[:, None] == lane_slot).astype(jnp.float32)
    exchange = functools.partial(
        lax.all_to_all, axis_name=store, split_axis=1, concat_axis=1, tiled=True
    )
    down = exchange(jnp.take(adapter_down, wanted, axis=0))
    up = exchange(jnp.take(adapter_up, wanted, axis=0))
    weight = lax.all_gather(base_weight, store, axis=0, tiled=True)
    down = down.reshape(choices, tokens.shape[1], rank)
    up = up.reshape(choices, base_weight.shape[1], rank)
    base = jnp.dot(tokens, weight, preferred_element_type=jnp.float32)
    shrink = jnp.einsum("td,kdr->tkr", tokens, down, preferred_element_type=jnp.float32)
    picked = (shrink.reshape(mask.shape) * mask).astype(jnp.bfloat16)
    picked = picked.reshape(shrink.shape)
    delta = jnp.einsum("tkr,kvr->tv", picked, up, preferred_element_type=jnp.float32)
    return (base + delta).astype(jnp.bfloat16)


def solution(mesh):
    parts, size = mesh.shape["parts"], mesh.shape["store"]
    chips = size // 2
    plane = 1
    while 4 * plane * plane <= chips:
        plane *= 2
    lines = chips // plane
    split = Mesh(mesh.devices.reshape(parts, lines, plane, 2), AXES)
    store = AXES[1:]

    def run(tokens, base_weight, *rest):
        small = (parts, lines, plane) == (2, 4, 2) and base_weight.shape[0] // size == 2 * HALF
        return jax.shard_map(
            body if small else plain_body,
            mesh=split,
            in_specs=(
                P(AXES, None),
                P(store, None),
                P(None, store, None),
                P(None, store, None),
                P(AXES, None),
                P("parts", None),
                P("parts", None),
            ),
            out_specs=P(AXES, None),
            check_vma=False,
        )(tokens, base_weight, *rest)

    return run
```

```python
import functools

import jax
import jax.numpy as jnp
from jax import lax
from jax.experimental import pallas as pl
from jax.experimental.pallas import tpu as pltpu
from jax.sharding import Mesh
from jax.sharding import PartitionSpec as P

HALF = 256
DEEP = 4
MIB = 1024 * 1024
AXES = ("parts", "line", "plane", "core")


def in_vmem(value):
    return pltpu.with_memory_space_constraint(value, pltpu.VMEM)


def store_index():
    return (lax.axis_index("line") * 2 + lax.axis_index("plane")) * 2 + lax.axis_index("core")


def send_kernel(groups, wanted, down, up, *refs):
    outs, (pick, even_rows, odd_rows, sems) = refs[:groups], refs[groups:]
    choices = wanted.shape[0]
    rank = down.shape[1]
    halves = down.shape[2] // HALF
    me = store_index()
    copies = []
    for k in range(groups):
        for choice in range(choices):
            for half in range(halves):
                copy = pltpu.make_async_copy(
                    down.at[wanted[choice, me ^ k], :, pl.ds(half * HALF, HALF)],
                    outs[k].at[pl.ds((half * choices + choice) * rank, rank), :],
                    sems.at[len(copies)],
                )
                copy.start()
                copies.append(copy)

    ids = lax.broadcasted_iota(jnp.int32, (1, up.shape[1]), 1)
    for choice in range(choices):
        for k in range(groups):
            here = (ids == wanted[choice, me ^ k]).astype(jnp.float32)
            pick[pl.ds(choice * groups + k, 1), :] = here
    rows = lax.dot_general(
        pick[...].astype(jnp.bfloat16),
        up[...],
        (((1,), (1,)), ((), ())),
        preferred_element_type=jnp.float32,
    )
    first, second = rows[:groups], rows[groups:]
    low = lax.broadcasted_iota(jnp.int32, (groups, 2 * rank), 1) < rank
    count = even_rows.shape[0] // groups
    for i in range(count):
        a = first[:, 2 * rank * i : 2 * rank * (i + 1)]
        b = second[:, 2 * rank * i : 2 * rank * (i + 1)]
        even_rows[pl.ds(i, groups, stride=count), :] = jnp.where(low, a, pltpu.roll(b, rank, 1))
        odd_rows[pl.ds(i, groups, stride=count), :] = jnp.where(low, pltpu.roll(a, rank, 1), b)
    start = choices * halves * rank
    for k in range(groups):
        own = pl.ds(k * count, count)
        outs[k][start:, : 2 * rank] = even_rows[own, :].astype(jnp.bfloat16)
        outs[k][start:, 2 * rank :] = odd_rows[own, :].astype(jnp.bfloat16)
    for copy in copies:
        copy.wait()


def make_messages(wanted, down, up, shard_width):
    choices, groups = wanted.shape
    rank, depth = down.shape[1:]
    halves = depth // HALF
    count = shard_width * choices * rank // HALF
    rows = choices * rank * halves + count
    return pl.pallas_call(
        functools.partial(send_kernel, groups),
        out_shape=[pltpu.VMEM((rows, HALF), jnp.bfloat16)] * groups,
        in_specs=[
            pl.BlockSpec(memory_space=pltpu.SMEM),
            pl.BlockSpec(memory_space=pl.ANY),
            pl.BlockSpec(memory_space=pltpu.VMEM),
        ],
        out_specs=[pl.BlockSpec(memory_space=pltpu.VMEM)] * groups,
        scratch_shapes=[
            pltpu.VMEM((choices * groups, up.shape[1]), jnp.float32),
            pltpu.VMEM((groups * count, 2 * rank), jnp.float32),
            pltpu.VMEM((groups * count, 2 * rank), jnp.float32),
            pltpu.SemaphoreType.DMA((groups * choices * halves,)),
        ],
        compiler_params=pltpu.CompilerParams(vmem_limit_bytes=16 * MIB),
        name="make_messages",
    )(wanted, down, up)


def base_product(tokens, blocks):
    rows, depth = tokens.shape
    width = blocks[0][1].shape[1]
    count = len(blocks)
    masks = [mask for mask, _ in blocks]

    def kernel(tokens_ref, *refs):
        parts, out = refs[:count], refs[count]
        place = [lax.axis_index(name) for name in AXES]
        for n in range(0, count, DEEP):
            left, right = [], []
            for mask, part in zip(masks[n : n + DEEP], parts[n : n + DEEP]):
                x, z, y, core = [i ^ bit for i, bit in zip(place, mask)]
                column = pl.multiple_of((((z * 2 + y) * 2 + core) * 2 + x) * HALF, HALF)
                left.append(tokens_ref[:, pl.ds(column, HALF)])
                right.append(part[...])
            total = jnp.dot(
                jnp.concatenate(left, axis=1),
                jnp.concatenate(right, axis=0),
                preferred_element_type=jnp.float32,
            )
            if n == 0:
                out[...] = total
            else:
                out[...] += total

    return pl.pallas_call(
        kernel,
        out_shape=pltpu.VMEM((rows, width), jnp.float32),
        in_specs=[pl.BlockSpec(memory_space=pltpu.VMEM)] * (1 + count),
        out_specs=pl.BlockSpec(memory_space=pltpu.VMEM),
        compiler_params=pltpu.CompilerParams(vmem_limit_bytes=16 * MIB),
        cost_estimate=pl.CostEstimate(
            flops=2 * rows * depth * width,
            bytes_accessed=2 * rows * depth + 2 * depth * width + 4 * rows * width,
            transcendentals=0,
        ),
        name="base_product",
    )(in_vmem(tokens), *[in_vmem(block) for _, block in blocks])


def adapt_kernel(tokens, mask, base, *refs):
    *messages, out, ups, wide = refs
    pair = mask.shape[1]
    depth = tokens.shape[1] // len(messages)
    halves = depth // HALF
    step = HALF // pair
    me = store_index()
    shrink = jnp.zeros(mask.shape, jnp.float32)
    for k, message in enumerate(messages):
        source = me ^ k
        column = pl.multiple_of(source * depth, depth)
        down = jnp.concatenate(
            [message[half * pair : (half + 1) * pair, :] for half in range(halves)], axis=1
        )
        shrink += lax.dot_general(
            tokens[:, pl.ds(column, depth)],
            down,
            (((1,), (1,)), ((), ())),
            preferred_element_type=jnp.float32,
        )
        up = message[halves * pair :, :].astype(jnp.float32)
        count = up.shape[0]
        for i in range(step):
            ups[k, pl.ds(i, count, stride=step), :] = up[:, i * pair : (i + 1) * pair]
        own = pl.ds(pl.multiple_of(source * count * step, count * step), count * step)
        wide[own, :] = ups[k].astype(jnp.bfloat16)
    picked = (shrink * mask[...]).astype(jnp.bfloat16)
    delta = lax.dot_general(
        picked, wide[...], (((1,), (1,)), ((), ())), preferred_element_type=jnp.float32
    )
    out[...] = (base[...] + delta).astype(out.dtype)


def adapt(tokens, messages, mask, base):
    rows, width = base.shape
    groups = len(messages)
    pair = mask.shape[1]
    return pl.pallas_call(
        adapt_kernel,
        out_shape=jax.ShapeDtypeStruct((rows, width), jnp.bfloat16),
        in_specs=[pl.BlockSpec(memory_space=pltpu.VMEM)] * (3 + groups),
        out_specs=pl.BlockSpec(memory_space=pltpu.VMEM),
        scratch_shapes=[
            pltpu.VMEM((groups, width // groups, pair), jnp.float32),
            pltpu.VMEM((width, pair), jnp.bfloat16),
        ],
        compiler_params=pltpu.CompilerParams(vmem_limit_bytes=16 * MIB),
        cost_estimate=pl.CostEstimate(
            flops=2 * rows * tokens.shape[1] * pair,
            bytes_accessed=2 * tokens.size + 2 * groups * messages[0].size + 6 * rows * width,
            transcendentals=0,
        ),
        name="adapt",
    )(*[in_vmem(value) for value in (tokens, mask, base, *messages)])


def after(value, *others):
    def kernel(*refs):
        pass

    return pl.pallas_call(
        kernel,
        out_shape=pltpu.VMEM(value.shape, value.dtype),
        in_specs=[pl.BlockSpec(memory_space=pl.ANY)] * (1 + len(others)),
        out_specs=pl.BlockSpec(memory_space=pl.ANY),
        input_output_aliases={0: 0},
        compiler_params=pltpu.CompilerParams(vmem_limit_bytes=MIB),
        name="after",
    )(*[in_vmem(other) for other in (value, *others)])


def row_slots(lengths, slots, rows):
    ends = jnp.cumsum(lengths)
    starts = ends - lengths
    position = jnp.arange(rows, dtype=jnp.int32)[:, None]
    member = (position >= starts[None, :]) & (position < ends[None, :])
    return jnp.sum(jnp.where(member, slots[None, :], 0), axis=1)


def swap(block, axis, bit):
    size = lax.axis_size(axis)
    return lax.ppermute(block, axis, [(i, i ^ bit) for i in range(size)])


def gather_rows(base_weight):
    x = lax.axis_index("parts")
    own = lax.dynamic_slice_in_dim(base_weight, x * HALF, HALF, 0)
    other = lax.dynamic_slice_in_dim(base_weight, (1 - x) * HALF, HALF, 0)
    blocks = {(0, 0, 0, 0): own}
    blocks[0, 1, 0, 0] = swap(own, "line", 1)
    blocks[0, 2, 0, 0] = swap(own, "line", 2)
    blocks[0, 3, 0, 0] = swap(blocks[0, 2, 0, 0], "line", 1)
    for z in range(4):
        blocks[0, z, 1, 0] = swap(blocks[0, z, 0, 0], "plane", 1)
    for z in range(4):
        for y in range(2):
            source = blocks[0, z, y, 0]
            blocks[1, z, y, 0] = other if z == y == 0 else swap(source, "parts", 1)
    for (x, z, y, _), block in list(blocks.items()):
        blocks[x, z, y, 1] = swap(block, "core", 1)
    return blocks


def exchange(messages, first):
    store = AXES[1:]
    groups = len(messages)

    def send(k, *others):
        pairs = [(i, i ^ k) for i in range(groups)]
        return lax.ppermute(after(messages[k], *others), store, pairs)

    arrived = {0: messages[0]}
    across = [k for k in range(1, groups) if k >= groups // 2]
    near = [k for k in range(1, groups) if k < groups // 2]
    for n, k in enumerate(across):
        arrived[k] = send(k, arrived[across[n - 2]] if n >= 2 else first)
    for n, k in enumerate(near):
        arrived[k] = send(k, arrived[across[n]])
    return [arrived[k] for k in range(groups)]


def body(
    tokens, base_weight, adapter_down, adapter_up, request_lengths, group_adapters, request_slot
):
    rank = adapter_down.shape[2]
    choices = group_adapters.shape[1]
    group = store_index()
    shard_width = adapter_up.shape[1]
    messages = make_messages(
        jnp.transpose(group_adapters),
        jnp.swapaxes(adapter_down, 1, 2),
        jnp.transpose(adapter_up, (1, 2, 0)).reshape(shard_width * rank, adapter_up.shape[0]),
        shard_width,
    )
    blocks = gather_rows(base_weight)
    arrived = exchange(messages, blocks[0, 1, 0, 0])
    slots = lax.dynamic_index_in_dim(request_slot, group, 0, keepdims=False)
    slot_of_row = row_slots(request_lengths[0], slots, tokens.shape[0])
    lane_slot = jnp.arange(choices * rank, dtype=jnp.int32)[None, :] // rank
    mask = (slot_of_row[:, None] == lane_slot).astype(jnp.float32)
    base = base_product(tokens, list(blocks.items()))
    return adapt(tokens, arrived, mask, base)


def plain_body(
    tokens, base_weight, adapter_down, adapter_up, request_lengths, group_adapters, request_slot
):
    store = AXES[1:]
    rank = adapter_down.shape[2]
    choices = group_adapters.shape[1]
    group = lax.axis_index(store)
    wanted = jnp.transpose(group_adapters)
    slots = lax.dynamic_index_in_dim(request_slot, group, 0, keepdims=False)
    slot_of_row = row_slots(request_lengths[0], slots, tokens.shape[0])
    lane_slot = jnp.arange(choices * rank, dtype=jnp.int32)[None, :] // rank
    mask = (slot_of_row[:, None] == lane_slot).astype(jnp.float32)
    exchange = functools.partial(
        lax.all_to_all, axis_name=store, split_axis=1, concat_axis=1, tiled=True
    )
    down = exchange(jnp.take(adapter_down, wanted, axis=0))
    up = exchange(jnp.take(adapter_up, wanted, axis=0))
    weight = lax.all_gather(base_weight, store, axis=0, tiled=True)
    down = down.reshape(choices, tokens.shape[1], rank)
    up = up.reshape(choices, base_weight.shape[1], rank)
    base = jnp.dot(tokens, weight, preferred_element_type=jnp.float32)
    shrink = jnp.einsum("td,kdr->tkr", tokens, down, preferred_element_type=jnp.float32)
    picked = (shrink.reshape(mask.shape) * mask).astype(jnp.bfloat16)
    picked = picked.reshape(shrink.shape)
    delta = jnp.einsum("tkr,kvr->tv", picked, up, preferred_element_type=jnp.float32)
    return (base + delta).astype(jnp.bfloat16)


def solution(mesh):
    parts, size = mesh.shape["parts"], mesh.shape["store"]
    chips = size // 2
    plane = 1
    while 4 * plane * plane <= chips:
        plane *= 2
    lines = chips // plane
    split = Mesh(mesh.devices.reshape(parts, lines, plane, 2), AXES)
    store = AXES[1:]

    def run(tokens, base_weight, *rest):
        small = (parts, lines, plane) == (2, 4, 2) and base_weight.shape[0] // size == 2 * HALF
        return jax.shard_map(
            body if small else plain_body,
            mesh=split,
            in_specs=(
                P(AXES, None),
                P(store, None),
                P(None, store, None),
                P(None, store, None),
                P(AXES, None),
                P("parts", None),
                P("parts", None),
            ),
            out_specs=P(AXES, None),
            check_vma=False,
        )(tokens, base_weight, *rest)

    return run
```

```python
import functools

import jax
import jax.numpy as jnp
from jax import lax
from jax.experimental import pallas as pl
from jax.experimental.pallas import tpu as pltpu
from jax.sharding import Mesh
from jax.sharding import PartitionSpec as P

HALF = 256
MIB = 1024 * 1024
AXES = ("parts", "line", "plane", "core")


def in_vmem(value):
    return pltpu.with_memory_space_constraint(value, pltpu.VMEM)


def in_hbm(value):
    return pltpu.with_memory_space_constraint(value, pltpu.HBM)


def store_index():
    return (lax.axis_index("line") * 2 + lax.axis_index("plane")) * 2 + lax.axis_index("core")


def send_kernel(groups, wanted, down, up, *refs):
    outs, (table, pick, even_rows, odd_rows, table_sem, sems) = refs[:groups], refs[groups:]
    choices = wanted.shape[0]
    rank = down.shape[1]
    halves = down.shape[2] // HALF
    me = store_index()
    copies = []
    for k in range(groups):
        for choice in range(choices):
            for half in range(halves):
                copy = pltpu.make_async_copy(
                    down.at[wanted[choice, me ^ k], :, pl.ds(half * HALF, HALF)],
                    outs[k].at[pl.ds((half * choices + choice) * rank, rank), :],
                    sems.at[len(copies)],
                )
                copy.start()
                copies.append(copy)
    table_copy = pltpu.make_async_copy(up, table, table_sem)
    table_copy.start()

    ids = lax.broadcasted_iota(jnp.int32, (1, up.shape[1]), 1)
    for choice in range(choices):
        for k in range(groups):
            here = (ids == wanted[choice, me ^ k]).astype(jnp.float32)
            pick[pl.ds(choice * groups + k, 1), :] = here
    table_copy.wait()
    rows = lax.dot_general(
        pick[...].astype(jnp.bfloat16),
        table[...],
        (((1,), (1,)), ((), ())),
        preferred_element_type=jnp.float32,
    )
    first, second = rows[:groups], rows[groups:]
    low = lax.broadcasted_iota(jnp.int32, (groups, 2 * rank), 1) < rank
    count = even_rows.shape[0] // groups
    for i in range(count):
        a = first[:, 2 * rank * i : 2 * rank * (i + 1)]
        b = second[:, 2 * rank * i : 2 * rank * (i + 1)]
        even_rows[pl.ds(i, groups, stride=count), :] = jnp.where(low, a, pltpu.roll(b, rank, 1))
        odd_rows[pl.ds(i, groups, stride=count), :] = jnp.where(low, pltpu.roll(a, rank, 1), b)
    start = choices * halves * rank
    for k in range(groups):
        own = pl.ds(k * count, count)
        outs[k][start:, : 2 * rank] = even_rows[own, :].astype(jnp.bfloat16)
        outs[k][start:, 2 * rank :] = odd_rows[own, :].astype(jnp.bfloat16)
    for copy in copies:
        copy.wait()


def make_messages(wanted, down, up, shard_width):
    choices, groups = wanted.shape
    rank, depth = down.shape[1:]
    halves = depth // HALF
    count = shard_width * choices * rank // HALF
    rows = choices * rank * halves + count
    return pl.pallas_call(
        functools.partial(send_kernel, groups),
        out_shape=[pltpu.VMEM((rows, HALF), jnp.bfloat16)] * groups,
        in_specs=[
            pl.BlockSpec(memory_space=pltpu.SMEM),
            pl.BlockSpec(memory_space=pltpu.HBM),
            pl.BlockSpec(memory_space=pltpu.HBM),
        ],
        out_specs=[pl.BlockSpec(memory_space=pltpu.VMEM)] * groups,
        scratch_shapes=[
            pltpu.VMEM(up.shape, up.dtype),
            pltpu.VMEM((choices * groups, up.shape[1]), jnp.float32),
            pltpu.VMEM((groups * count, 2 * rank), jnp.float32),
            pltpu.VMEM((groups * count, 2 * rank), jnp.float32),
            pltpu.SemaphoreType.DMA,
            pltpu.SemaphoreType.DMA((groups * choices * halves,)),
        ],
        compiler_params=pltpu.CompilerParams(vmem_limit_bytes=16 * MIB),
        name="make_messages",
    )(wanted, in_hbm(down), in_hbm(up))


def base_product(tokens, bundles, start=None):
    rows, depth = tokens.shape
    width = bundles[0][1].shape[1]
    count = len(bundles)
    total_rows = sum(bundle.shape[0] for _, bundle in bundles)

    def kernel(tokens_ref, *refs):
        parts, out = refs[:count], refs[-1]
        place = dict(zip(AXES, [lax.axis_index(name) for name in AXES]))
        first = start is None
        for (masks, _), part in zip(bundles, parts):
            left = []
            for x, z, y, core in masks:
                z, y, core = place["line"] ^ z, place["plane"] ^ y, place["core"] ^ core
                owner = (z * 2 + y) * 2 + core
                if x is None:
                    column, size = pl.multiple_of(owner * 2 * HALF, 2 * HALF), 2 * HALF
                else:
                    column = pl.multiple_of((owner * 2 + (place["parts"] ^ x)) * HALF, HALF)
                    size = HALF
                left.append(tokens_ref[:, pl.ds(column, size)])
            total = jnp.dot(
                jnp.concatenate(left, axis=1), part[...], preferred_element_type=jnp.float32
            )
            if first:
                out[...] = total if start is None else refs[count][...] + total
            else:
                out[...] += total
            first = False

    def kernel_with_start(tokens_ref, *refs):
        refs[-1][...] = refs[count][...]
        kernel(tokens_ref, *refs)

    extra = [] if start is None else [start]
    return pl.pallas_call(
        kernel if start is None else kernel_with_start,
        out_shape=pltpu.VMEM((rows, width), jnp.float32),
        in_specs=[pl.BlockSpec(memory_space=pltpu.VMEM)] * (1 + count + len(extra)),
        out_specs=pl.BlockSpec(memory_space=pltpu.VMEM),
        compiler_params=pltpu.CompilerParams(vmem_limit_bytes=16 * MIB),
        cost_estimate=pl.CostEstimate(
            flops=2 * rows * total_rows * width,
            bytes_accessed=2 * rows * total_rows + 2 * total_rows * width + 4 * rows * width,
            transcendentals=0,
        ),
        name="base_product",
    )(*[in_vmem(value) for value in (tokens, *[bundle for _, bundle in bundles], *extra)])


def adapt_kernel(tokens, mask, base, *refs):
    *messages, out, ups, wide = refs
    pair = mask.shape[1]
    depth = tokens.shape[1] // len(messages)
    halves = depth // HALF
    step = HALF // pair
    me = store_index()
    shrink = jnp.zeros(mask.shape, jnp.float32)
    for k, message in enumerate(messages):
        source = me ^ k
        column = pl.multiple_of(source * depth, depth)
        down = jnp.concatenate(
            [message[half * pair : (half + 1) * pair, :] for half in range(halves)], axis=1
        )
        shrink += lax.dot_general(
            tokens[:, pl.ds(column, depth)],
            down,
            (((1,), (1,)), ((), ())),
            preferred_element_type=jnp.float32,
        )
        up = message[halves * pair :, :].astype(jnp.float32)
        count = up.shape[0]
        for i in range(step):
            ups[k, pl.ds(i, count, stride=step), :] = up[:, i * pair : (i + 1) * pair]
        own = pl.ds(pl.multiple_of(source * count * step, count * step), count * step)
        wide[own, :] = ups[k].astype(jnp.bfloat16)
    picked = (shrink * mask[...]).astype(jnp.bfloat16)
    delta = lax.dot_general(
        picked, wide[...], (((1,), (1,)), ((), ())), preferred_element_type=jnp.float32
    )
    out[...] = (base[...] + delta).astype(out.dtype)


def adapt(tokens, messages, mask, base):
    rows, width = base.shape
    groups = len(messages)
    pair = mask.shape[1]
    return pl.pallas_call(
        adapt_kernel,
        out_shape=jax.ShapeDtypeStruct((rows, width), jnp.bfloat16),
        in_specs=[pl.BlockSpec(memory_space=pltpu.VMEM)] * (3 + groups),
        out_specs=pl.BlockSpec(memory_space=pltpu.VMEM),
        scratch_shapes=[
            pltpu.VMEM((groups, width // groups, pair), jnp.float32),
            pltpu.VMEM((width, pair), jnp.bfloat16),
        ],
        compiler_params=pltpu.CompilerParams(vmem_limit_bytes=16 * MIB),
        cost_estimate=pl.CostEstimate(
            flops=2 * rows * tokens.shape[1] * pair,
            bytes_accessed=2 * tokens.size + 2 * groups * messages[0].size + 6 * rows * width,
            transcendentals=0,
        ),
        name="adapt",
    )(*[in_vmem(value) for value in (tokens, mask, base, *messages)])


def after(value, *others):
    def kernel(*refs):
        pass

    return pl.pallas_call(
        kernel,
        out_shape=pltpu.VMEM(value.shape, value.dtype),
        in_specs=[pl.BlockSpec(memory_space=pl.ANY)] * (1 + len(others)),
        out_specs=pl.BlockSpec(memory_space=pl.ANY),
        input_output_aliases={0: 0},
        compiler_params=pltpu.CompilerParams(vmem_limit_bytes=MIB),
        name="after",
    )(*[in_vmem(other) for other in (value, *others)])


def bundle(blocks):
    size, width = blocks[0].shape

    def kernel(*refs):
        for n, ref in enumerate(refs[:-1]):
            refs[-1][n * size : (n + 1) * size, :] = ref[...]

    return pl.pallas_call(
        kernel,
        out_shape=pltpu.VMEM((size * len(blocks), width), blocks[0].dtype),
        in_specs=[pl.BlockSpec(memory_space=pltpu.VMEM)] * len(blocks),
        out_specs=pl.BlockSpec(memory_space=pltpu.VMEM),
        compiler_params=pltpu.CompilerParams(vmem_limit_bytes=2 * MIB),
        name="bundle",
    )(*[in_vmem(block) for block in blocks])


def load_rows(base_weight):
    def kernel(weight, whole, half, sems):
        x = lax.axis_index("parts")
        own = pltpu.make_async_copy(weight.at[pl.ds(x * HALF, HALF), :], half, sems.at[0])
        rest = pltpu.make_async_copy(weight, whole, sems.at[1])
        own.start()
        rest.start()
        own.wait()
        rest.wait()

    return pl.pallas_call(
        kernel,
        out_shape=[
            pltpu.VMEM(base_weight.shape, base_weight.dtype),
            pltpu.VMEM((HALF, base_weight.shape[1]), base_weight.dtype),
        ],
        in_specs=[pl.BlockSpec(memory_space=pltpu.HBM)],
        out_specs=[pl.BlockSpec(memory_space=pltpu.VMEM)] * 2,
        scratch_shapes=[pltpu.SemaphoreType.DMA((2,))],
        compiler_params=pltpu.CompilerParams(vmem_limit_bytes=2 * MIB),
        name="load_rows",
    )(in_hbm(base_weight))


def row_mask(lengths, slots, rows, choices, rank):
    requests = lengths.shape[1]

    def kernel(lengths_ref, slots_ref, out):
        group = store_index()
        position = lax.broadcasted_iota(jnp.int32, out.shape, 0)
        lane_slot = lax.broadcasted_iota(jnp.int32, out.shape, 1) // rank
        chosen = jnp.full(out.shape, slots_ref[group, 0], jnp.int32)
        begin = lengths_ref[0, 0]
        for request in range(1, requests):
            change = slots_ref[group, request] - slots_ref[group, request - 1]
            chosen += jnp.where(position >= begin, change, 0)
            begin += lengths_ref[0, request]
        out[...] = (chosen == lane_slot).astype(jnp.float32)

    return pl.pallas_call(
        kernel,
        out_shape=pltpu.VMEM((rows, choices * rank), jnp.float32),
        in_specs=[pl.BlockSpec(memory_space=pltpu.SMEM)] * 2,
        out_specs=pl.BlockSpec(memory_space=pltpu.VMEM),
        compiler_params=pltpu.CompilerParams(vmem_limit_bytes=2 * MIB),
        name="row_mask",
    )(lengths, slots)


def row_slots(lengths, slots, rows):
    ends = jnp.cumsum(lengths)
    starts = ends - lengths
    position = jnp.arange(rows, dtype=jnp.int32)[:, None]
    member = (position >= starts[None, :]) & (position < ends[None, :])
    return jnp.sum(jnp.where(member, slots[None, :], 0), axis=1)


def swap(block, axis, bit):
    size = lax.axis_size(axis)
    return lax.ppermute(block, axis, [(i, i ^ bit) for i in range(size)])


def gather_rows(base_weight):
    whole, own = load_rows(base_weight)
    z1 = swap(own, "line", 1)
    z2 = swap(own, "line", 2)
    y0 = swap(own, "plane", 1)
    z3 = swap(z2, "line", 1)
    y1 = swap(z1, "plane", 1)
    y23 = swap(bundle([z2, z3]), "plane", 1)
    sent = [
        ([(1, 0), (0, 1)], bundle([z1, y0])),
        ([(2, 0), (1, 1)], bundle([z2, y1])),
        ([(3, 0)], z3),
        ([(2, 1), (3, 1)], y23),
    ]
    bundles = [([(None, 0, 0, 0)], whole), ([(None, 0, 0, 1)], swap(whole, "core", 1))]
    for places, block in sent:
        for x, held in enumerate([block, swap(block, "parts", 1)]):
            for core, got in enumerate([held, swap(held, "core", 1)]):
                bundles.append(([(x, z, y, core) for z, y in places], got))
    return bundles, z1


def exchange(messages, first):
    store = AXES[1:]
    groups = len(messages)

    def send(k, *others):
        pairs = [(i, i ^ k) for i in range(groups)]
        return lax.ppermute(after(messages[k], *others), store, pairs)

    arrived = {0: messages[0]}
    across = [k for k in range(1, groups) if k >= groups // 2]
    near = [k for k in range(1, groups) if k < groups // 2]
    for n, k in enumerate(across):
        arrived[k] = send(k, arrived[across[n - 2]] if n >= 2 else first)
    for n, k in enumerate(near):
        arrived[k] = send(k, arrived[across[n]])
    return [arrived[k] for k in range(groups)]


def body(
    tokens, base_weight, adapter_down, adapter_up, request_lengths, group_adapters, request_slot
):
    rank = adapter_down.shape[2]
    choices = group_adapters.shape[1]
    shard_width = adapter_up.shape[1]
    messages = make_messages(
        jnp.transpose(group_adapters),
        jnp.swapaxes(adapter_down, 1, 2),
        jnp.transpose(adapter_up, (1, 2, 0)).reshape(shard_width * rank, adapter_up.shape[0]),
        shard_width,
    )
    bundles, first = gather_rows(base_weight)
    arrived = exchange(messages, first)
    mask = row_mask(request_lengths, request_slot, tokens.shape[0], choices, rank)
    base = base_product(tokens, bundles)
    return adapt(tokens, arrived, mask, base)


def plain_body(
    tokens, base_weight, adapter_down, adapter_up, request_lengths, group_adapters, request_slot
):
    store = AXES[1:]
    rank = adapter_down.shape[2]
    choices = group_adapters.shape[1]
    group = lax.axis_index(store)
    wanted = jnp.transpose(group_adapters)
    slots = lax.dynamic_index_in_dim(request_slot, group, 0, keepdims=False)
    slot_of_row = row_slots(request_lengths[0], slots, tokens.shape[0])
    lane_slot = jnp.arange(choices * rank, dtype=jnp.int32)[None, :] // rank
    mask = (slot_of_row[:, None] == lane_slot).astype(jnp.float32)
    exchange = functools.partial(
        lax.all_to_all, axis_name=store, split_axis=1, concat_axis=1, tiled=True
    )
    down = exchange(jnp.take(adapter_down, wanted, axis=0))
    up = exchange(jnp.take(adapter_up, wanted, axis=0))
    weight = lax.all_gather(base_weight, store, axis=0, tiled=True)
    down = down.reshape(choices, tokens.shape[1], rank)
    up = up.reshape(choices, base_weight.shape[1], rank)
    base = jnp.dot(tokens, weight, preferred_element_type=jnp.float32)
    shrink = jnp.einsum("td,kdr->tkr", tokens, down, preferred_element_type=jnp.float32)
    picked = (shrink.reshape(mask.shape) * mask).astype(jnp.bfloat16)
    picked = picked.reshape(shrink.shape)
    delta = jnp.einsum("tkr,kvr->tv", picked, up, preferred_element_type=jnp.float32)
    return (base + delta).astype(jnp.bfloat16)


def solution(mesh):
    parts, size = mesh.shape["parts"], mesh.shape["store"]
    chips = size // 2
    plane = 1
    while 4 * plane * plane <= chips:
        plane *= 2
    lines = chips // plane
    split = Mesh(mesh.devices.reshape(parts, lines, plane, 2), AXES)
    store = AXES[1:]

    def run(tokens, base_weight, *rest):
        small = (parts, lines, plane) == (2, 4, 2) and base_weight.shape[0] // size == 2 * HALF
        return jax.shard_map(
            body if small else plain_body,
            mesh=split,
            in_specs=(
                P(AXES, None),
                P(store, None),
                P(None, store, None),
                P(None, store, None),
                P(AXES, None),
                P("parts", None),
                P("parts", None),
            ),
            out_specs=P(AXES, None),
            check_vma=False,
        )(tokens, base_weight, *rest)

    return run
```

```python
import functools

import jax
import jax.numpy as jnp
from jax import lax
from jax.experimental import pallas as pl
from jax.experimental.pallas import tpu as pltpu
from jax.sharding import Mesh
from jax.sharding import PartitionSpec as P

HALF = 256
MIB = 1024 * 1024
AXES = ("parts", "line", "plane", "core")


def in_vmem(value):
    return pltpu.with_memory_space_constraint(value, pltpu.VMEM)


def in_hbm(value):
    return pltpu.with_memory_space_constraint(value, pltpu.HBM)


def store_index():
    return (lax.axis_index("line") * 2 + lax.axis_index("plane")) * 2 + lax.axis_index("core")


ROUNDS = ((4, 1), (2, 6), (5, 3), (7, 7))


def message_targets(round_):
    chip, core = store_index() // 2, lax.axis_index("core")
    own = jnp.where(core == 0, *ROUNDS[round_])
    other = jnp.where(core == 0, *ROUNDS[round_][::-1])
    return [(chip ^ own) * 2, (chip ^ own) * 2 + 1], [(chip ^ other) * 2, (chip ^ other) * 2 + 1]


def send_kernel(rounds, wanted, down, up, weight, *refs):
    outs, whole, half = refs[: 2 * rounds + 1], refs[2 * rounds + 1], refs[2 * rounds + 2]
    table, pick, even_rows, odd_rows, table_sem, sems = refs[2 * rounds + 3 :]
    choices, groups = wanted.shape
    rank = down.shape[1]
    halves = down.shape[2] // HALF
    length = outs[0].shape[0] // 2
    me = store_index()
    places = []
    for n in range(rounds):
        own, other = message_targets(n)
        places += [(own[i], outs[2 * n], i) for i in range(2)]
        places += [(other[i], outs[2 * n + 1], i) for i in range(2)]
    places += [(me, outs[-1], 0), (me ^ 1, outs[-1], 1)]
    copies = []

    def begin(source, target):
        copy = pltpu.make_async_copy(source, target, sems.at[len(copies)])
        copy.start()
        copies.append(copy)

    begin(weight.at[pl.ds(lax.axis_index("parts") * HALF, HALF), :], half)
    begin(weight, whole)
    for target, out, i in places:
        for choice in range(choices):
            adapter = wanted[choice, target]
            for part in range(halves):
                start = i * length + (part * choices + choice) * rank
                begin(
                    down.at[adapter, :, pl.ds(part * HALF, HALF)], out.at[pl.ds(start, rank), :]
                )
    table_copy = pltpu.make_async_copy(up, table, table_sem)
    table_copy.start()

    ids = lax.broadcasted_iota(jnp.int32, (1, up.shape[1]), 1)
    for choice in range(choices):
        for group in range(groups):
            here = (ids == wanted[choice, group]).astype(jnp.float32)
            pick[pl.ds(choice * groups + group, 1), :] = here
    table_copy.wait()
    rows = lax.dot_general(
        pick[...].astype(jnp.bfloat16),
        table[...],
        (((1,), (1,)), ((), ())),
        preferred_element_type=jnp.float32,
    )
    first, second = rows[:groups], rows[groups:]
    low = lax.broadcasted_iota(jnp.int32, (groups, 2 * rank), 1) < rank
    count = even_rows.shape[0] // groups
    for i in range(count):
        a = first[:, 2 * rank * i : 2 * rank * (i + 1)]
        b = second[:, 2 * rank * i : 2 * rank * (i + 1)]
        even_rows[pl.ds(i, groups, stride=count), :] = jnp.where(low, a, pltpu.roll(b, rank, 1))
        odd_rows[pl.ds(i, groups, stride=count), :] = jnp.where(low, pltpu.roll(a, rank, 1), b)
    for target, out, i in places:
        own = pl.ds(pl.multiple_of(target * count, count), count)
        to = pl.ds((i + 1) * length - count, count)
        out[to, : 2 * rank] = even_rows[own, :].astype(jnp.bfloat16)
        out[to, 2 * rank :] = odd_rows[own, :].astype(jnp.bfloat16)
    for copy in copies:
        copy.wait()


def make_messages(wanted, down, up, weight, shard_width):
    choices, groups = wanted.shape
    rank, depth = down.shape[1:]
    halves = depth // HALF
    count = shard_width * choices * rank // HALF
    length = choices * rank * halves + count
    rounds = len(ROUNDS)
    *messages, local, whole, half = pl.pallas_call(
        functools.partial(send_kernel, rounds),
        out_shape=[pltpu.VMEM((2 * length, HALF), jnp.bfloat16)] * (2 * rounds + 1)
        + [
            pltpu.VMEM(weight.shape, weight.dtype),
            pltpu.VMEM((HALF, weight.shape[1]), weight.dtype),
        ],
        in_specs=[pl.BlockSpec(memory_space=pltpu.SMEM)]
        + [pl.BlockSpec(memory_space=pltpu.HBM)] * 3,
        out_specs=[pl.BlockSpec(memory_space=pltpu.VMEM)] * (2 * rounds + 3),
        scratch_shapes=[
            pltpu.VMEM(up.shape, up.dtype),
            pltpu.VMEM((choices * groups, up.shape[1]), jnp.float32),
            pltpu.VMEM((groups * count, 2 * rank), jnp.float32),
            pltpu.VMEM((groups * count, 2 * rank), jnp.float32),
            pltpu.SemaphoreType.DMA,
            pltpu.SemaphoreType.DMA(((4 * rounds + 2) * choices * halves + 2,)),
        ],
        compiler_params=pltpu.CompilerParams(vmem_limit_bytes=16 * MIB),
        name="make_messages",
    )(wanted, *[in_hbm(value) for value in (down, up, weight)])
    return messages[::2], messages[1::2], local, whole, half


def base_product(tokens, bundles, start=None):
    rows, depth = tokens.shape
    width = bundles[0][1].shape[1]
    count = len(bundles)
    total_rows = sum(bundle.shape[0] for _, bundle in bundles)

    def kernel(tokens_ref, *refs):
        parts, out = refs[:count], refs[-1]
        place = dict(zip(AXES, [lax.axis_index(name) for name in AXES]))
        first = True
        for (masks, _), part in zip(bundles, parts):
            left = []
            for x, z, y, core in masks:
                z, y, core = place["line"] ^ z, place["plane"] ^ y, place["core"] ^ core
                owner = (z * 2 + y) * 2 + core
                if x is None:
                    column, size = pl.multiple_of(owner * 2 * HALF, 2 * HALF), 2 * HALF
                else:
                    column = pl.multiple_of((owner * 2 + (place["parts"] ^ x)) * HALF, HALF)
                    size = HALF
                left.append(tokens_ref[:, pl.ds(column, size)])
            total = jnp.dot(
                jnp.concatenate(left, axis=1), part[...], preferred_element_type=jnp.float32
            )
            if first:
                out[...] = total if start is None else refs[count][...] + total
            else:
                out[...] += total
            first = False

    extra = [] if start is None else [start]
    return pl.pallas_call(
        kernel,
        out_shape=pltpu.VMEM((rows, width), jnp.float32),
        in_specs=[pl.BlockSpec(memory_space=pltpu.VMEM)] * (1 + count + len(extra)),
        out_specs=pl.BlockSpec(memory_space=pltpu.VMEM),
        compiler_params=pltpu.CompilerParams(vmem_limit_bytes=16 * MIB),
        cost_estimate=pl.CostEstimate(
            flops=2 * rows * total_rows * width,
            bytes_accessed=2 * rows * total_rows + 2 * total_rows * width + 4 * rows * width,
            transcendentals=0,
        ),
        name="base_product",
    )(*[in_vmem(value) for value in (tokens, *[bundle for _, bundle in bundles], *extra)])


def adapt_kernel(rounds, tokens, mask, base, *refs):
    across, handed = refs[:rounds], refs[rounds : 2 * rounds]
    local, swapped, out, ups, wide = refs[2 * rounds :]
    length = local.shape[0] // 2
    pair = mask.shape[1]
    step = HALF // pair
    groups = wide.shape[0] * step // ups.shape[0] // 2
    depth = tokens.shape[1] // groups
    halves = depth // HALF
    core = lax.axis_index("core")
    chip = store_index() // 2

    def at(ref, place):
        return ref[pl.ds(pl.multiple_of(place * length, 16), length), :]

    messages = [(chip * 2 + core, at(local, 0)), (chip * 2 + 1 - core, swapped[-length:, :])]
    for n in range(rounds):
        own, other = jnp.where(core == 0, *ROUNDS[n]), jnp.where(core == 0, *ROUNDS[n][::-1])
        if ROUNDS[n][0] != ROUNDS[n][1]:
            for i in range(2):
                messages.append(((chip ^ own) * 2 + (core ^ i), at(across[n], 2 * i + core)))
                messages.append(((chip ^ other) * 2 + (core ^ 1 ^ i), at(handed[n], i)))
        else:
            for i in range(2):
                both = at(across[n], 2 * i + core) + at(handed[n], 1 - i)
                messages.append(((chip ^ own) * 2 + (core ^ i), both))

    shrink = jnp.zeros(mask.shape, jnp.float32)
    for source, message in messages:
        column = pl.multiple_of(source * depth, depth)
        down = jnp.concatenate(
            [message[half * pair : (half + 1) * pair, :] for half in range(halves)], axis=1
        )
        shrink += lax.dot_general(
            tokens[:, pl.ds(column, depth)],
            down,
            (((1,), (1,)), ((), ())),
            preferred_element_type=jnp.float32,
        )
        up = message[halves * pair :, :].astype(jnp.float32)
        count = up.shape[0]
        for i in range(step):
            ups[pl.ds(i, count, stride=step), :] = up[:, i * pair : (i + 1) * pair]
        own = pl.ds(pl.multiple_of(source * count * step, count * step), count * step)
        wide[own, :] = ups[...].astype(jnp.bfloat16)
    picked = (shrink * mask[...]).astype(jnp.bfloat16)
    delta = lax.dot_general(
        picked, wide[...], (((1,), (1,)), ((), ())), preferred_element_type=jnp.float32
    )
    out[...] = (base[...] + delta).astype(out.dtype)


def adapt(tokens, across, handed, local, swapped, mask, base, shard_width):
    rows, width = base.shape
    pair = mask.shape[1]
    values = (tokens, mask, base, *across, *handed, local, swapped)
    return pl.pallas_call(
        functools.partial(adapt_kernel, len(across)),
        out_shape=jax.ShapeDtypeStruct((rows, width), jnp.bfloat16),
        in_specs=[pl.BlockSpec(memory_space=pltpu.VMEM)] * len(values),
        out_specs=pl.BlockSpec(memory_space=pltpu.VMEM),
        scratch_shapes=[
            pltpu.VMEM((shard_width, pair), jnp.float32),
            pltpu.VMEM((width, pair), jnp.bfloat16),
        ],
        compiler_params=pltpu.CompilerParams(vmem_limit_bytes=16 * MIB),
        cost_estimate=pl.CostEstimate(
            flops=2 * rows * tokens.shape[1] * pair,
            bytes_accessed=2 * tokens.size + 2 * tokens.shape[1] * pair + 6 * rows * width,
            transcendentals=0,
        ),
        name="adapt",
    )(*[in_vmem(value) for value in values])


def bundle(pieces, others=()):
    pieces = [piece if isinstance(piece, tuple) else (piece, None, piece.shape[0]) for piece in pieces]
    count = len(pieces)
    width, dtype = pieces[0][0].shape[1], pieces[0][0].dtype

    def kernel(*refs):
        place = 0
        for ref, (_, begin, size) in zip(refs[:count], pieces):
            first = 0 if begin is None else begin()
            refs[-1][place : place + size, :] = ref[pl.ds(first, size), :]
            place += size

    values = [array for array, _, _ in pieces] + list(others)
    return pl.pallas_call(
        kernel,
        out_shape=pltpu.VMEM((sum(size for _, _, size in pieces), width), dtype),
        in_specs=[pl.BlockSpec(memory_space=pltpu.VMEM)] * len(values),
        out_specs=pl.BlockSpec(memory_space=pltpu.VMEM),
        compiler_params=pltpu.CompilerParams(vmem_limit_bytes=2 * MIB),
        name="bundle",
    )(*[in_vmem(value) for value in values])


def row_mask(lengths, slots, rows, choices, rank):
    requests = lengths.shape[1]

    def kernel(lengths_ref, slots_ref, out):
        group = store_index()
        position = lax.broadcasted_iota(jnp.int32, out.shape, 0)
        lane_slot = lax.broadcasted_iota(jnp.int32, out.shape, 1) // rank
        chosen = jnp.full(out.shape, slots_ref[group, 0], jnp.int32)
        begin = lengths_ref[0, 0]
        for request in range(1, requests):
            change = slots_ref[group, request] - slots_ref[group, request - 1]
            chosen += jnp.where(position >= begin, change, 0)
            begin += lengths_ref[0, request]
        out[...] = (chosen == lane_slot).astype(jnp.float32)

    return pl.pallas_call(
        kernel,
        out_shape=pltpu.VMEM((rows, choices * rank), jnp.float32),
        in_specs=[pl.BlockSpec(memory_space=pltpu.SMEM)] * 2,
        out_specs=pl.BlockSpec(memory_space=pltpu.VMEM),
        compiler_params=pltpu.CompilerParams(vmem_limit_bytes=2 * MIB),
        name="row_mask",
    )(lengths, slots)


def row_slots(lengths, slots, rows):
    ends = jnp.cumsum(lengths)
    starts = ends - lengths
    position = jnp.arange(rows, dtype=jnp.int32)[:, None]
    member = (position >= starts[None, :]) & (position < ends[None, :])
    return jnp.sum(jnp.where(member, slots[None, :], 0), axis=1)


def swap(block, axis, bit):
    size = lax.axis_size(axis)
    return lax.ppermute(block, axis, [(i, i ^ bit) for i in range(size)])


def gather_rows(whole, own):
    z2 = swap(own, "line", 2)
    z1 = swap(own, "line", 1)
    y0 = swap(own, "plane", 1)
    z3 = swap(z2, "line", 1)
    y1 = swap(bundle([z1], [y0]), "plane", 1)
    y23 = swap(bundle([z2, z3], [y1]), "plane", 1)
    y2, y3 = (y23, lambda: 0, HALF), (y23, lambda: HALF, HALF)
    bundles = [([(None, 0, 0, 0)], whole), ([(None, 0, 0, 1)], swap(whole, "core", 1))]
    before = []
    for places, blocks in (
        ([(1, 0), (0, 1)], [z1, y0]),
        ([(2, 0), (1, 1)], [z2, y1]),
        ([(3, 0), (2, 1)], [z3, y2]),
        ([(3, 1)], [y3]),
    ):
        sent = bundle(blocks, before)
        got = swap(sent, "parts", 1)
        both = [(x, z, y) for x in range(2) for z, y in places]
        other = swap(bundle([sent, got]), "core", 1)
        bundles.append(([(0, z, y, 0) for z, y in places], sent))
        bundles.append(([(1, z, y, 0) for z, y in places], got))
        bundles.append(([(x, z, y, 1) for x, z, y in both], other))
        before = [got]
    return bundles, z2


def exchange(mine, theirs, local, first):
    length = local.shape[0] // 2
    size = 2 * lax.axis_size("line") * lax.axis_size("plane")
    early = swap(theirs[0], "core", 1)
    later = swap(bundle([*theirs[1:], (local, lambda: length, length)]), "core", 1)
    across, handed = [], []
    before = [[], [first]]
    for n, masks in enumerate(ROUNDS):
        if n == 0:
            got = early
        else:
            got = (later, functools.partial(int, (n - 1) * 2 * length), 2 * length)
        payload = bundle([mine[n], got], before[n])
        cores = (0, 1) if masks[0] != masks[1] else (1,)
        pairs = [
            (chip * 2 + core, (chip ^ masks[core]) * 2 + core)
            for chip in range(size // 2)
            for core in cores
        ]
        across.append(lax.ppermute(payload, AXES[1:], pairs))
        before.append([across[n]])

        def place(i):
            return pl.multiple_of((2 * i + 1 - lax.axis_index("core")) * length, 16)

        parts = [(across[n], functools.partial(place, i), length) for i in range(2)]
        handed.append(swap(bundle(parts), "core", 1))
    return across, handed, later


def body(
    tokens, base_weight, adapter_down, adapter_up, request_lengths, group_adapters, request_slot
):
    rank = adapter_down.shape[2]
    choices = group_adapters.shape[1]
    shard_width = adapter_up.shape[1]
    mine, theirs, local, whole, half = make_messages(
        jnp.transpose(group_adapters),
        jnp.swapaxes(adapter_down, 1, 2),
        jnp.transpose(adapter_up, (1, 2, 0)).reshape(shard_width * rank, adapter_up.shape[0]),
        base_weight,
        shard_width,
    )
    bundles, first = gather_rows(whole, half)
    across, handed, swapped = exchange(mine, theirs, local, first)
    mask = row_mask(request_lengths, request_slot, tokens.shape[0], choices, rank)
    base = base_product(tokens, bundles[:9])
    base = base_product(tokens, bundles[9:], base)
    return adapt(tokens, across, handed, local, swapped, mask, base, shard_width)


def plain_body(
    tokens, base_weight, adapter_down, adapter_up, request_lengths, group_adapters, request_slot
):
    store = AXES[1:]
    rank = adapter_down.shape[2]
    choices = group_adapters.shape[1]
    group = lax.axis_index(store)
    wanted = jnp.transpose(group_adapters)
    slots = lax.dynamic_index_in_dim(request_slot, group, 0, keepdims=False)
    slot_of_row = row_slots(request_lengths[0], slots, tokens.shape[0])
    lane_slot = jnp.arange(choices * rank, dtype=jnp.int32)[None, :] // rank
    mask = (slot_of_row[:, None] == lane_slot).astype(jnp.float32)
    exchange = functools.partial(
        lax.all_to_all, axis_name=store, split_axis=1, concat_axis=1, tiled=True
    )
    down = exchange(jnp.take(adapter_down, wanted, axis=0))
    up = exchange(jnp.take(adapter_up, wanted, axis=0))
    weight = lax.all_gather(base_weight, store, axis=0, tiled=True)
    down = down.reshape(choices, tokens.shape[1], rank)
    up = up.reshape(choices, base_weight.shape[1], rank)
    base = jnp.dot(tokens, weight, preferred_element_type=jnp.float32)
    shrink = jnp.einsum("td,kdr->tkr", tokens, down, preferred_element_type=jnp.float32)
    picked = (shrink.reshape(mask.shape) * mask).astype(jnp.bfloat16)
    picked = picked.reshape(shrink.shape)
    delta = jnp.einsum("tkr,kvr->tv", picked, up, preferred_element_type=jnp.float32)
    return (base + delta).astype(jnp.bfloat16)


def solution(mesh):
    parts, size = mesh.shape["parts"], mesh.shape["store"]
    chips = size // 2
    plane = 1
    while 4 * plane * plane <= chips:
        plane *= 2
    lines = chips // plane
    split = Mesh(mesh.devices.reshape(parts, lines, plane, 2), AXES)
    store = AXES[1:]

    def run(tokens, base_weight, *rest):
        small = (parts, lines, plane) == (2, 4, 2) and base_weight.shape[0] // size == 2 * HALF
        return jax.shard_map(
            body if small else plain_body,
            mesh=split,
            in_specs=(
                P(AXES, None),
                P(store, None),
                P(None, store, None),
                P(None, store, None),
                P(AXES, None),
                P("parts", None),
                P("parts", None),
            ),
            out_specs=P(AXES, None),
            check_vma=False,
        )(tokens, base_weight, *rest)

    return run
```

```python
import functools

import jax
import jax.numpy as jnp
from jax import lax
from jax.experimental import pallas as pl
from jax.experimental.pallas import tpu as pltpu
from jax.sharding import Mesh
from jax.sharding import PartitionSpec as P

HALF = 256
MIB = 1024 * 1024
COST = 4
AXES = ("parts", "line", "plane", "core")


def in_vmem(value):
    return pltpu.with_memory_space_constraint(value, pltpu.VMEM)


def in_hbm(value):
    return pltpu.with_memory_space_constraint(value, pltpu.HBM)


def store_index():
    return (lax.axis_index("line") * 2 + lax.axis_index("plane")) * 2 + lax.axis_index("core")


DIRECT_FIRST, DIRECT_LAST, DIRECT_NEAR = 4, 7, 1
ROUNDS = ((2, 6), (5, 3))


def direct_targets(mask):
    return [store_index() ^ (2 * mask + i) for i in range(2)]


def round_targets(masks, core):
    chip = store_index() // 2
    mask = jnp.where(core == 0, *masks)
    return [(chip ^ mask) * 2 + i for i in range(2)]


def send_kernel(targets_of, wanted, down, up, weight, *refs):
    targets = targets_of()
    *outs, whole, half = refs[:-6]
    table, pick, even_rows, odd_rows, table_sem, sems = refs[-6:]
    choices = wanted.shape[0]
    rank = down.shape[1]
    halves = down.shape[2] // HALF
    padded = pick.shape[0] // choices
    count = even_rows.shape[0] // padded
    length = choices * halves * rank + count
    copies = []

    def begin(source, target):
        copy = pltpu.make_async_copy(source, target, sems.at[len(copies)])
        copy.start()
        copies.append(copy)

    begin(weight.at[pl.ds(lax.axis_index("parts") * HALF, HALF), :], half)
    begin(weight, whole)
    places = []
    for out, target in targets:
        places.append((outs[out], sum(place[0] is outs[out] for place in places) * length))
        for choice in range(choices):
            adapter = wanted[choice, target]
            for part in range(halves):
                start = places[-1][1] + (part * choices + choice) * rank
                begin(
                    down.at[adapter, :, pl.ds(part * HALF, HALF)],
                    outs[out].at[pl.ds(start, rank), :],
                )
    table_copy = pltpu.make_async_copy(up, table, table_sem)
    table_copy.start()

    ids = lax.broadcasted_iota(jnp.int32, (1, up.shape[1]), 1)
    pick[...] = jnp.zeros_like(pick)
    for choice in range(choices):
        for n, (_, target) in enumerate(targets):
            here = (ids == wanted[choice, target]).astype(jnp.float32)
            pick[pl.ds(choice * padded + n, 1), :] = here
    table_copy.wait()
    rows = lax.dot_general(
        pick[...].astype(jnp.bfloat16),
        table[...],
        (((1,), (1,)), ((), ())),
        preferred_element_type=jnp.float32,
    )
    first, second = rows[:padded], rows[padded:]
    low = lax.broadcasted_iota(jnp.int32, (padded, 2 * rank), 1) < rank
    for i in range(count):
        a = first[:, 2 * rank * i : 2 * rank * (i + 1)]
        b = second[:, 2 * rank * i : 2 * rank * (i + 1)]
        even_rows[pl.ds(i, padded, stride=count), :] = jnp.where(low, a, pltpu.roll(b, rank, 1))
        odd_rows[pl.ds(i, padded, stride=count), :] = jnp.where(low, pltpu.roll(a, rank, 1), b)
    for n, (out, start) in enumerate(places):
        own = pl.ds(n * count, count)
        to = pl.ds(start + length - count, count)
        out[to, : 2 * rank] = even_rows[own, :].astype(jnp.bfloat16)
        out[to, 2 * rank :] = odd_rows[own, :].astype(jnp.bfloat16)
    for copy in copies:
        copy.wait()


def make_messages(wanted, down, up, weight, shard_width, counts, targets_of, cost, others=()):
    choices = wanted.shape[0]
    rank, depth = down.shape[1:]
    halves = depth // HALF
    count = shard_width * choices * rank // HALF
    length = choices * rank * halves + count
    padded = -(-sum(counts) // 8) * 8

    def kernel(*refs):
        send_kernel(targets_of, *refs[:4], *refs[4 + len(others) :])

    *messages, whole, half = pl.pallas_call(
        kernel,
        out_shape=[pltpu.VMEM((n * length, HALF), jnp.bfloat16) for n in counts]
        + [
            pltpu.VMEM(weight.shape, weight.dtype),
            pltpu.VMEM((HALF, weight.shape[1]), weight.dtype),
        ],
        in_specs=[pl.BlockSpec(memory_space=pltpu.SMEM)]
        + [pl.BlockSpec(memory_space=pltpu.HBM)] * 3
        + [pl.BlockSpec(memory_space=pltpu.VMEM)] * len(others),
        out_specs=[pl.BlockSpec(memory_space=pltpu.VMEM)] * (len(counts) + 2),
        scratch_shapes=[
            pltpu.VMEM(up.shape, up.dtype),
            pltpu.VMEM((choices * padded, up.shape[1]), jnp.float32),
            pltpu.VMEM((padded * count, 2 * rank), jnp.float32),
            pltpu.VMEM((padded * count, 2 * rank), jnp.float32),
            pltpu.SemaphoreType.DMA,
            pltpu.SemaphoreType.DMA((sum(counts) * choices * halves + 2,)),
        ],
        compiler_params=pltpu.CompilerParams(vmem_limit_bytes=16 * MIB),
        cost_estimate=pl.CostEstimate(
            flops=0, bytes_accessed=4 * cost * sum(counts) * length * HALF, transcendentals=0
        ),
        name="make_messages",
    )(
        wanted,
        *[in_hbm(value) for value in (down, up, weight)],
        *[in_vmem(other) for other in others],
    )
    return messages, whole, half


def base_product(tokens, bundles, start=None):
    rows, depth = tokens.shape
    width = bundles[0][1].shape[1]
    count = len(bundles)
    total_rows = sum(bundle.shape[0] for _, bundle in bundles)

    def kernel(tokens_ref, *refs):
        parts, out = refs[:count], refs[-1]
        place = dict(zip(AXES, [lax.axis_index(name) for name in AXES]))
        first = True
        for (masks, _), part in zip(bundles, parts):
            left = []
            for x, z, y, core in masks:
                z, y, core = place["line"] ^ z, place["plane"] ^ y, place["core"] ^ core
                owner = (z * 2 + y) * 2 + core
                if x is None:
                    column, size = pl.multiple_of(owner * 2 * HALF, 2 * HALF), 2 * HALF
                else:
                    column = pl.multiple_of((owner * 2 + (place["parts"] ^ x)) * HALF, HALF)
                    size = HALF
                left.append(tokens_ref[:, pl.ds(column, size)])
            total = jnp.dot(
                jnp.concatenate(left, axis=1), part[...], preferred_element_type=jnp.float32
            )
            if first:
                out[...] = total if start is None else refs[count][...] + total
            else:
                out[...] += total
            first = False

    extra = [] if start is None else [start]
    return pl.pallas_call(
        kernel,
        out_shape=pltpu.VMEM((rows, width), jnp.float32),
        in_specs=[pl.BlockSpec(memory_space=pltpu.VMEM)] * (1 + count + len(extra)),
        out_specs=pl.BlockSpec(memory_space=pltpu.VMEM),
        compiler_params=pltpu.CompilerParams(vmem_limit_bytes=16 * MIB),
        cost_estimate=pl.CostEstimate(
            flops=2 * rows * total_rows * width,
            bytes_accessed=2 * rows * total_rows + 2 * total_rows * width + 4 * rows * width,
            transcendentals=0,
        ),
        name="base_product",
    )(*[in_vmem(value) for value in (tokens, *[bundle for _, bundle in bundles], *extra)])


def shrink_part(sources, length, tokens, messages, wide, ups):
    pair = wide.shape[1]
    step = HALF // pair
    groups = wide.shape[0] // ups.shape[0]
    depth = tokens.shape[1] // groups
    halves = depth // HALF
    total = None
    for n, start, source in sources():
        begin = start if isinstance(start, int) else pl.multiple_of(start, 16)
        message = messages[n][pl.ds(begin, length), :]
        column = pl.multiple_of(source * depth, depth)
        down = jnp.concatenate(
            [message[half * pair : (half + 1) * pair, :] for half in range(halves)], axis=1
        )
        part = lax.dot_general(
            tokens[:, pl.ds(column, depth)],
            down,
            (((1,), (1,)), ((), ())),
            preferred_element_type=jnp.float32,
        )
        total = part if total is None else total + part
        up = message[halves * pair :, :].astype(jnp.float32)
        count = up.shape[0]
        for i in range(step):
            ups[pl.ds(i, count, stride=step), :] = up[:, i * pair : (i + 1) * pair]
        own = pl.ds(pl.multiple_of(source * count * step, count * step), count * step)
        wide[own, :] = ups[...].astype(jnp.bfloat16)
    return total


def adapt_cost(tokens, pair, share):
    return pl.CostEstimate(
        flops=int(4 * tokens.size * pair * share),
        bytes_accessed=int(2 * tokens.size * share),
        transcendentals=0,
    )


def adapt_begin(tokens, messages, sources, length, pair, shard_width, width, share):
    rows = tokens.shape[0]
    count = len(messages)

    def kernel(tokens_ref, *refs):
        shrink, wide, ups = refs[count:]
        wide[...] = jnp.zeros_like(wide)
        shrink[...] = shrink_part(sources, length, tokens_ref, refs[:count], wide, ups)

    return pl.pallas_call(
        kernel,
        out_shape=[
            pltpu.VMEM((rows, pair), jnp.float32),
            pltpu.VMEM((width, pair), jnp.bfloat16),
        ],
        in_specs=[pl.BlockSpec(memory_space=pltpu.VMEM)] * (1 + count),
        out_specs=[pl.BlockSpec(memory_space=pltpu.VMEM)] * 2,
        scratch_shapes=[pltpu.VMEM((shard_width, pair), jnp.float32)],
        compiler_params=pltpu.CompilerParams(vmem_limit_bytes=16 * MIB),
        cost_estimate=adapt_cost(tokens, pair, share),
        name="adapt_begin",
    )(*[in_vmem(value) for value in (tokens, *messages)])


def adapt_end(tokens, messages, sources, length, mask, base, begun, shard_width, share):
    rows, width = base.shape
    pair = mask.shape[1]
    count = len(messages)

    def kernel(tokens_ref, mask_ref, base_ref, shrunk, widened, *refs):
        out, wide, ups = refs[count:]
        wide[...] = widened[...]
        shrink = shrunk[...]
        shrink += shrink_part(sources, length, tokens_ref, refs[:count], wide, ups)
        picked = (shrink * mask_ref[...]).astype(jnp.bfloat16)
        delta = lax.dot_general(
            picked, wide[...], (((1,), (1,)), ((), ())), preferred_element_type=jnp.float32
        )
        out[...] = (base_ref[...] + delta).astype(out.dtype)

    values = (tokens, mask, base, *begun, *messages)
    return pl.pallas_call(
        kernel,
        out_shape=jax.ShapeDtypeStruct((rows, width), jnp.bfloat16),
        in_specs=[pl.BlockSpec(memory_space=pltpu.VMEM)] * len(values),
        out_specs=pl.BlockSpec(memory_space=pltpu.VMEM),
        scratch_shapes=[
            pltpu.VMEM((width, pair), jnp.bfloat16),
            pltpu.VMEM((shard_width, pair), jnp.float32),
        ],
        compiler_params=pltpu.CompilerParams(vmem_limit_bytes=16 * MIB),
        cost_estimate=adapt_cost(tokens, pair, share),
        name="adapt_end",
    )(*[in_vmem(value) for value in values])


def after(value, *others):
    def kernel(*refs):
        pass

    return pl.pallas_call(
        kernel,
        out_shape=pltpu.VMEM(value.shape, value.dtype),
        in_specs=[pl.BlockSpec(memory_space=pl.ANY)] * (1 + len(others)),
        out_specs=pl.BlockSpec(memory_space=pl.ANY),
        input_output_aliases={0: 0},
        compiler_params=pltpu.CompilerParams(vmem_limit_bytes=MIB),
        name="after",
    )(*[in_vmem(other) for other in (value, *others)])


def bundle(pieces, others=()):
    pieces = [piece if isinstance(piece, tuple) else (piece, None, piece.shape[0]) for piece in pieces]
    count = len(pieces)
    width, dtype = pieces[0][0].shape[1], pieces[0][0].dtype

    def kernel(*refs):
        place = 0
        for ref, (_, begin, size) in zip(refs[:count], pieces):
            first = 0 if begin is None else begin()
            refs[-1][place : place + size, :] = ref[pl.ds(first, size), :]
            place += size

    values = [array for array, _, _ in pieces] + list(others)
    return pl.pallas_call(
        kernel,
        out_shape=pltpu.VMEM((sum(size for _, _, size in pieces), width), dtype),
        in_specs=[pl.BlockSpec(memory_space=pltpu.VMEM)] * len(values),
        out_specs=pl.BlockSpec(memory_space=pltpu.VMEM),
        compiler_params=pltpu.CompilerParams(vmem_limit_bytes=2 * MIB),
        name="bundle",
    )(*[in_vmem(value) for value in values])


def row_mask(lengths, slots, rows, choices, rank):
    requests = lengths.shape[1]

    def kernel(lengths_ref, slots_ref, out):
        group = store_index()
        position = lax.broadcasted_iota(jnp.int32, out.shape, 0)
        lane_slot = lax.broadcasted_iota(jnp.int32, out.shape, 1) // rank
        chosen = jnp.full(out.shape, slots_ref[group, 0], jnp.int32)
        begin = lengths_ref[0, 0]
        for request in range(1, requests):
            change = slots_ref[group, request] - slots_ref[group, request - 1]
            chosen += jnp.where(position >= begin, change, 0)
            begin += lengths_ref[0, request]
        out[...] = (chosen == lane_slot).astype(jnp.float32)

    return pl.pallas_call(
        kernel,
        out_shape=pltpu.VMEM((rows, choices * rank), jnp.float32),
        in_specs=[pl.BlockSpec(memory_space=pltpu.SMEM)] * 2,
        out_specs=pl.BlockSpec(memory_space=pltpu.VMEM),
        compiler_params=pltpu.CompilerParams(vmem_limit_bytes=2 * MIB),
        name="row_mask",
    )(lengths, slots)


def row_slots(lengths, slots, rows):
    ends = jnp.cumsum(lengths)
    starts = ends - lengths
    position = jnp.arange(rows, dtype=jnp.int32)[:, None]
    member = (position >= starts[None, :]) & (position < ends[None, :])
    return jnp.sum(jnp.where(member, slots[None, :], 0), axis=1)


def swap(block, axis, bit):
    size = lax.axis_size(axis)
    return lax.ppermute(block, axis, [(i, i ^ bit) for i in range(size)])


def gather_rows(whole, half, paces, plane_pace):
    z2 = swap(half, "line", 2)
    z1 = swap(half, "line", 1)
    y0 = swap(half, "plane", 1)
    z3 = swap(bundle([z2], [z1]), "line", 1)
    y1 = swap(bundle([z1], [y0, *plane_pace]), "plane", 1)
    y23 = swap(bundle([z2, z3], [y1]), "plane", 1)
    y2, y3 = (y23, lambda: 0, HALF), (y23, lambda: HALF, HALF)
    bundles = [([(None, 0, 0, 0)], whole), ([(None, 0, 0, 1)], swap(whole, "core", 1))]
    before = []
    for n, (places, blocks) in enumerate(
        (
            ([(1, 0), (0, 1)], [z1, y0]),
            ([(2, 0), (1, 1)], [z2, y1]),
            ([(3, 0), (2, 1)], [z3, y2]),
            ([(3, 1)], [y3]),
        )
    ):
        sent = bundle(blocks, before + paces[n])
        got = swap(sent, "parts", 1)
        bundles.append(([(0, z, y, 0) for z, y in places], sent))
        bundles.append(([(1, z, y, 0) for z, y in places], got))

        def from_core(*others, places=places, held=(sent, got)):
            masks = [(x, z, y, 1) for x in range(2) for z, y in places]
            return masks, swap(bundle(held, others), "core", 1)

        if n < 3:
            bundles.append(from_core())
        before = [got]
    return bundles, from_core


def send_chip(mask, messages, *others):
    size = 2 * lax.axis_size("line") * lax.axis_size("plane")
    payload = after(messages, *others) if others else messages
    return lax.ppermute(payload, AXES[1:], [(i, i ^ (2 * mask)) for i in range(size)])


def hand_on(*arrived):
    length = arrived[0].shape[0] // 2

    return swap(bundle([(pair, lambda: length, length) for pair in arrived]), "core", 1)


def send_round(masks, mine, theirs, *others):
    size = 2 * lax.axis_size("line") * lax.axis_size("plane")
    length = mine.shape[0] // 2
    pairs = [
        (chip * 2 + core, (chip ^ masks[core]) * 2 + core)
        for chip in range(size // 2)
        for core in range(2)
    ]
    got = lax.ppermute(bundle([mine, theirs], others), AXES[1:], pairs)

    def place(i):
        return pl.multiple_of((2 * i + 1 - lax.axis_index("core")) * length, 16)

    parts = [(got, functools.partial(place, i), length) for i in range(2)]
    return got, swap(bundle(parts), "core", 1)


def body(
    tokens, base_weight, adapter_down, adapter_up, request_lengths, group_adapters, request_slot
):
    rank = adapter_down.shape[2]
    choices = group_adapters.shape[1]
    width = base_weight.shape[1]
    shard_width = adapter_up.shape[1]
    mask = row_mask(request_lengths, request_slot, tokens.shape[0], choices, rank)
    operands = (
        jnp.transpose(group_adapters),
        jnp.swapaxes(adapter_down, 1, 2),
        jnp.transpose(adapter_up, (1, 2, 0)).reshape(shard_width * rank, adapter_up.shape[0]),
        base_weight,
        shard_width,
    )

    def first_targets():
        return [(0, target) for target in direct_targets(DIRECT_FIRST)]

    def other_targets():
        core = lax.axis_index("core")
        targets = [(0, target) for target in direct_targets(DIRECT_LAST)]
        targets += [(1, target) for target in direct_targets(DIRECT_NEAR)]
        for n, masks in enumerate(ROUNDS):
            targets += [(2 + n, target) for target in round_targets(masks, core)]
        for masks in ROUNDS:
            targets += [(4, target) for target in round_targets(masks, 1 - core)]
        me = store_index()
        return targets + [(4, me ^ 1), (5, me)]

    (pair_first,), whole, half = make_messages(*operands, (2,), first_targets, 1)
    (pair_last, pair_near, mine_a, mine_b, theirs, local), _, _ = make_messages(
        *operands, (2, 2, 2, 2, 5, 1), other_targets, COST, [half]
    )
    length = local.shape[0]

    got_first = send_chip(DIRECT_FIRST, pair_first)
    swapped = swap(theirs, "core", 1)
    got_a, handed_a = send_round(ROUNDS[0], mine_a, (swapped, lambda: 0, 2 * length))
    got_near = send_chip(DIRECT_NEAR, pair_near, got_first)
    handed_first = hand_on(got_first, got_near)
    got_b, handed_b = send_round(
        ROUNDS[1], mine_b, (swapped, lambda: 2 * length, 2 * length), got_first, mask
    )
    paces = [[], [], [got_a], [got_b, handed_first]]
    bundles, last_rows = gather_rows(whole, half, paces, [got_first])
    base = base_product(tokens, bundles[:4])
    base = base_product(tokens, bundles[4:7], base)
    got_last = send_chip(DIRECT_LAST, pair_last, got_a, base)
    handed_last = hand_on(got_last)
    bundles.append(last_rows(got_last))
    base = base_product(tokens, bundles[7:10], base)
    base = base_product(tokens, bundles[10:], base)

    def round_sources(masks, first):
        core, chip = lax.axis_index("core"), store_index() // 2
        own, other = jnp.where(core == 0, *masks), jnp.where(core == 0, *masks[::-1])
        places = []
        for i in range(2):
            places.append((first, (2 * i + core) * length, (chip ^ own) * 2 + (core ^ i)))
            places.append((first + 1, i * length, (chip ^ other) * 2 + (core ^ 1 ^ i)))
        return places

    def direct_sources(mask, n, handed, start):
        core, chip = lax.axis_index("core"), store_index() // 2
        source = (chip ^ mask) * 2
        return [(n, 0, source + core), (handed, start, source + 1 - core)]

    def begin_sources():
        me = store_index()
        places = [(0, 0, me), (1, 4 * length, me ^ 1)]
        places += direct_sources(DIRECT_FIRST, 2, 4, 0)
        places += direct_sources(DIRECT_NEAR, 3, 4, length)
        return places + round_sources(ROUNDS[0], 5)

    def end_sources():
        return round_sources(ROUNDS[1], 0) + direct_sources(DIRECT_LAST, 2, 3, 0)

    begun = adapt_begin(
        tokens,
        (local, swapped, got_first, got_near, handed_first, got_a, handed_a),
        begin_sources,
        length,
        choices * rank,
        shard_width,
        width,
        0.6,
    )
    return adapt_end(
        tokens,
        (got_b, handed_b, got_last, handed_last),
        end_sources,
        length,
        mask,
        base,
        begun,
        shard_width,
        0.4,
    )


def plain_body(
    tokens, base_weight, adapter_down, adapter_up, request_lengths, group_adapters, request_slot
):
    store = AXES[1:]
    rank = adapter_down.shape[2]
    choices = group_adapters.shape[1]
    group = lax.axis_index(store)
    wanted = jnp.transpose(group_adapters)
    slots = lax.dynamic_index_in_dim(request_slot, group, 0, keepdims=False)
    slot_of_row = row_slots(request_lengths[0], slots, tokens.shape[0])
    lane_slot = jnp.arange(choices * rank, dtype=jnp.int32)[None, :] // rank
    mask = (slot_of_row[:, None] == lane_slot).astype(jnp.float32)
    exchange = functools.partial(
        lax.all_to_all, axis_name=store, split_axis=1, concat_axis=1, tiled=True
    )
    down = exchange(jnp.take(adapter_down, wanted, axis=0))
    up = exchange(jnp.take(adapter_up, wanted, axis=0))
    weight = lax.all_gather(base_weight, store, axis=0, tiled=True)
    down = down.reshape(choices, tokens.shape[1], rank)
    up = up.reshape(choices, base_weight.shape[1], rank)
    base = jnp.dot(tokens, weight, preferred_element_type=jnp.float32)
    shrink = jnp.einsum("td,kdr->tkr", tokens, down, preferred_element_type=jnp.float32)
    picked = (shrink.reshape(mask.shape) * mask).astype(jnp.bfloat16)
    picked = picked.reshape(shrink.shape)
    delta = jnp.einsum("tkr,kvr->tv", picked, up, preferred_element_type=jnp.float32)
    return (base + delta).astype(jnp.bfloat16)


def solution(mesh):
    parts, size = mesh.shape["parts"], mesh.shape["store"]
    chips = size // 2
    plane = 1
    while 4 * plane * plane <= chips:
        plane *= 2
    lines = chips // plane
    split = Mesh(mesh.devices.reshape(parts, lines, plane, 2), AXES)
    store = AXES[1:]

    def run(tokens, base_weight, *rest):
        small = (parts, lines, plane) == (2, 4, 2) and base_weight.shape[0] // size == 2 * HALF
        return jax.shard_map(
            body if small else plain_body,
            mesh=split,
            in_specs=(
                P(AXES, None),
                P(store, None),
                P(None, store, None),
                P(None, store, None),
                P(AXES, None),
                P("parts", None),
                P("parts", None),
            ),
            out_specs=P(AXES, None),
            check_vma=False,
        )(tokens, base_weight, *rest)

    return run
```

```python
import functools

import jax
import jax.numpy as jnp
from jax import lax
from jax.experimental import pallas as pl
from jax.experimental.pallas import tpu as pltpu
from jax.sharding import Mesh
from jax.sharding import PartitionSpec as P

HALF = 256
MIB = 1024 * 1024
COST = 4
AXES = ("parts", "line", "plane", "core")


def in_vmem(value):
    return pltpu.with_memory_space_constraint(value, pltpu.VMEM)


def in_hbm(value):
    return pltpu.with_memory_space_constraint(value, pltpu.HBM)


def store_index():
    return (lax.axis_index("line") * 2 + lax.axis_index("plane")) * 2 + lax.axis_index("core")


EARLY, LATE = (5,), ()
ROUNDS = ((1, 4), (3, 7), (2, 6))
LAST = ('R1', 'P5')
TIES = {
    "Y2": ("B0", "T2", "X1",),
    "X4": ("T2", "X3", "Y1",),
    "C1": ("X2", "mask",),
    "C2": ("X3",),
    "C3": ("AB",),
    "C4": ("AB", "B1", "F0", "R1", "Y2",),
    "B1": ("R0",),
    "F0": ("Y3",),
    "T1": ("R0", "Y2", "Z3",),
    "T2": ("P5", "Y1", "Z2",),
    "mask": ("B0", "T1", "Y0",),
}


def direct_targets(mask):
    return [store_index() ^ (2 * mask + i) for i in range(2)]


def round_targets(masks, core):
    chip = store_index() // 2
    mask = jnp.where(core == 0, *masks)
    return [(chip ^ mask) * 2 + i for i in range(2)]


def send_kernel(targets_of, wanted, down, up, weight, *refs):
    targets = targets_of()
    *outs, whole, half = refs[:-6]
    table, pick, even_rows, odd_rows, table_sem, sems = refs[-6:]
    choices = wanted.shape[0]
    rank = down.shape[1]
    halves = down.shape[2] // HALF
    padded = pick.shape[0] // choices
    count = even_rows.shape[0] // padded
    length = choices * halves * rank + count
    copies = []

    def begin(source, target):
        copy = pltpu.make_async_copy(source, target, sems.at[len(copies)])
        copy.start()
        copies.append(copy)

    begin(weight.at[pl.ds(lax.axis_index("parts") * HALF, HALF), :], half)
    begin(weight, whole)
    places = []
    for out, target in targets:
        places.append((outs[out], sum(place[0] is outs[out] for place in places) * length))
        for choice in range(choices):
            adapter = wanted[choice, target]
            for part in range(halves):
                start = places[-1][1] + (part * choices + choice) * rank
                begin(
                    down.at[adapter, :, pl.ds(part * HALF, HALF)],
                    outs[out].at[pl.ds(start, rank), :],
                )
    table_copy = pltpu.make_async_copy(up, table, table_sem)
    table_copy.start()

    ids = lax.broadcasted_iota(jnp.int32, (1, up.shape[1]), 1)
    pick[...] = jnp.zeros_like(pick)
    for choice in range(choices):
        for n, (_, target) in enumerate(targets):
            here = (ids == wanted[choice, target]).astype(jnp.float32)
            pick[pl.ds(choice * padded + n, 1), :] = here
    table_copy.wait()
    rows = lax.dot_general(
        pick[...].astype(jnp.bfloat16),
        table[...],
        (((1,), (1,)), ((), ())),
        preferred_element_type=jnp.float32,
    )
    first, second = rows[:padded], rows[padded:]
    low = lax.broadcasted_iota(jnp.int32, (padded, 2 * rank), 1) < rank
    for i in range(count):
        a = first[:, 2 * rank * i : 2 * rank * (i + 1)]
        b = second[:, 2 * rank * i : 2 * rank * (i + 1)]
        even_rows[pl.ds(i, padded, stride=count), :] = jnp.where(low, a, pltpu.roll(b, rank, 1))
        odd_rows[pl.ds(i, padded, stride=count), :] = jnp.where(low, pltpu.roll(a, rank, 1), b)
    for n, (out, start) in enumerate(places):
        own = pl.ds(n * count, count)
        to = pl.ds(start + length - count, count)
        out[to, : 2 * rank] = even_rows[own, :].astype(jnp.bfloat16)
        out[to, 2 * rank :] = odd_rows[own, :].astype(jnp.bfloat16)
    for copy in copies:
        copy.wait()


def make_messages(wanted, down, up, weight, shard_width, counts, targets_of, cost, others=()):
    choices = wanted.shape[0]
    rank, depth = down.shape[1:]
    halves = depth // HALF
    count = shard_width * choices * rank // HALF
    length = choices * rank * halves + count
    padded = -(-sum(counts) // 8) * 8

    def kernel(*refs):
        send_kernel(targets_of, *refs[:4], *refs[4 + len(others) :])

    *messages, whole, half = pl.pallas_call(
        kernel,
        out_shape=[pltpu.VMEM((n * length, HALF), jnp.bfloat16) for n in counts]
        + [
            pltpu.VMEM(weight.shape, weight.dtype),
            pltpu.VMEM((HALF, weight.shape[1]), weight.dtype),
        ],
        in_specs=[pl.BlockSpec(memory_space=pltpu.SMEM)]
        + [pl.BlockSpec(memory_space=pltpu.HBM)] * 3
        + [pl.BlockSpec(memory_space=pltpu.VMEM)] * len(others),
        out_specs=[pl.BlockSpec(memory_space=pltpu.VMEM)] * (len(counts) + 2),
        scratch_shapes=[
            pltpu.VMEM(up.shape, up.dtype),
            pltpu.VMEM((choices * padded, up.shape[1]), jnp.float32),
            pltpu.VMEM((padded * count, 2 * rank), jnp.float32),
            pltpu.VMEM((padded * count, 2 * rank), jnp.float32),
            pltpu.SemaphoreType.DMA,
            pltpu.SemaphoreType.DMA((sum(counts) * choices * halves + 2,)),
        ],
        compiler_params=pltpu.CompilerParams(vmem_limit_bytes=16 * MIB),
        cost_estimate=pl.CostEstimate(
            flops=0, bytes_accessed=4 * cost * sum(counts) * length * HALF, transcendentals=0
        ),
        name="make_messages",
    )(
        wanted,
        *[in_hbm(value) for value in (down, up, weight)],
        *[in_vmem(other) for other in others],
    )
    return messages, whole, half


def base_product(tokens, bundles, start=None, others=()):
    rows, depth = tokens.shape
    width = bundles[0][1].shape[1]
    count = len(bundles)
    total_rows = sum(bundle.shape[0] for _, bundle in bundles)

    def kernel(tokens_ref, *refs):
        parts, out = refs[:count], refs[-1]
        place = dict(zip(AXES, [lax.axis_index(name) for name in AXES]))
        first = True
        for (masks, _), part in zip(bundles, parts):
            left = []
            for x, z, y, core in masks:
                z, y, core = place["line"] ^ z, place["plane"] ^ y, place["core"] ^ core
                owner = (z * 2 + y) * 2 + core
                if x is None:
                    column, size = pl.multiple_of(owner * 2 * HALF, 2 * HALF), 2 * HALF
                else:
                    column = pl.multiple_of((owner * 2 + (place["parts"] ^ x)) * HALF, HALF)
                    size = HALF
                left.append(tokens_ref[:, pl.ds(column, size)])
            total = jnp.dot(
                jnp.concatenate(left, axis=1), part[...], preferred_element_type=jnp.float32
            )
            if first:
                out[...] = total if start is None else refs[count][...] + total
            else:
                out[...] += total
            first = False

    extra = ([] if start is None else [start]) + list(others)
    return pl.pallas_call(
        kernel,
        out_shape=pltpu.VMEM((rows, width), jnp.float32),
        in_specs=[pl.BlockSpec(memory_space=pltpu.VMEM)] * (1 + count + len(extra)),
        out_specs=pl.BlockSpec(memory_space=pltpu.VMEM),
        compiler_params=pltpu.CompilerParams(vmem_limit_bytes=16 * MIB),
        cost_estimate=pl.CostEstimate(
            flops=2 * rows * total_rows * width,
            bytes_accessed=2 * rows * total_rows + 2 * total_rows * width + 4 * rows * width,
            transcendentals=0,
        ),
        name="base_product",
    )(*[in_vmem(value) for value in (tokens, *[bundle for _, bundle in bundles], *extra)])


def shrink_part(sources, length, tokens, messages, wide, ups):
    pair = wide.shape[1]
    step = HALF // pair
    groups = wide.shape[0] // ups.shape[0]
    depth = tokens.shape[1] // groups
    halves = depth // HALF
    total = None
    for n, start, source in sources():
        begin = start if isinstance(start, int) else pl.multiple_of(start, 16)
        message = messages[n][pl.ds(begin, length), :]
        column = pl.multiple_of(source * depth, depth)
        down = jnp.concatenate(
            [message[half * pair : (half + 1) * pair, :] for half in range(halves)], axis=1
        )
        part = lax.dot_general(
            tokens[:, pl.ds(column, depth)],
            down,
            (((1,), (1,)), ((), ())),
            preferred_element_type=jnp.float32,
        )
        total = part if total is None else total + part
        up = message[halves * pair :, :].astype(jnp.float32)
        count = up.shape[0]
        for i in range(step):
            ups[pl.ds(i, count, stride=step), :] = up[:, i * pair : (i + 1) * pair]
        own = pl.ds(pl.multiple_of(source * count * step, count * step), count * step)
        wide[own, :] = ups[...].astype(jnp.bfloat16)
    return total


def adapt_cost(tokens, pair, share):
    return pl.CostEstimate(
        flops=int(4 * tokens.size * pair * share),
        bytes_accessed=int(2 * tokens.size * share),
        transcendentals=0,
    )


def adapt_begin(tokens, messages, sources, length, pair, shard_width, width, share):
    rows = tokens.shape[0]
    count = len(messages)

    def kernel(tokens_ref, *refs):
        shrink, wide, ups = refs[count:]
        wide[...] = jnp.zeros_like(wide)
        shrink[...] = shrink_part(sources, length, tokens_ref, refs[:count], wide, ups)

    return pl.pallas_call(
        kernel,
        out_shape=[
            pltpu.VMEM((rows, pair), jnp.float32),
            pltpu.VMEM((width, pair), jnp.bfloat16),
        ],
        in_specs=[pl.BlockSpec(memory_space=pltpu.VMEM)] * (1 + count),
        out_specs=[pl.BlockSpec(memory_space=pltpu.VMEM)] * 2,
        scratch_shapes=[pltpu.VMEM((shard_width, pair), jnp.float32)],
        compiler_params=pltpu.CompilerParams(vmem_limit_bytes=16 * MIB),
        cost_estimate=adapt_cost(tokens, pair, share),
        name="adapt_begin",
    )(*[in_vmem(value) for value in (tokens, *messages)])


def adapt_end(tokens, messages, sources, length, mask, base, begun, shard_width, share):
    rows, width = base.shape
    pair = mask.shape[1]
    count = len(messages)

    def kernel(tokens_ref, mask_ref, base_ref, shrunk, widened, *refs):
        out, wide, ups = refs[count:]
        wide[...] = widened[...]
        shrink = shrunk[...]
        shrink += shrink_part(sources, length, tokens_ref, refs[:count], wide, ups)
        picked = (shrink * mask_ref[...]).astype(jnp.bfloat16)
        delta = lax.dot_general(
            picked, wide[...], (((1,), (1,)), ((), ())), preferred_element_type=jnp.float32
        )
        out[...] = (base_ref[...] + delta).astype(out.dtype)

    values = (tokens, mask, base, *begun, *messages)
    return pl.pallas_call(
        kernel,
        out_shape=jax.ShapeDtypeStruct((rows, width), jnp.bfloat16),
        in_specs=[pl.BlockSpec(memory_space=pltpu.VMEM)] * len(values),
        out_specs=pl.BlockSpec(memory_space=pltpu.VMEM),
        scratch_shapes=[
            pltpu.VMEM((width, pair), jnp.bfloat16),
            pltpu.VMEM((shard_width, pair), jnp.float32),
        ],
        compiler_params=pltpu.CompilerParams(vmem_limit_bytes=16 * MIB),
        cost_estimate=adapt_cost(tokens, pair, share),
        name="adapt_end",
    )(*[in_vmem(value) for value in values])


def after(value, *others):
    def kernel(*refs):
        pass

    return pl.pallas_call(
        kernel,
        out_shape=pltpu.VMEM(value.shape, value.dtype),
        in_specs=[pl.BlockSpec(memory_space=pl.ANY)] * (1 + len(others)),
        out_specs=pl.BlockSpec(memory_space=pl.ANY),
        input_output_aliases={0: 0},
        compiler_params=pltpu.CompilerParams(vmem_limit_bytes=MIB),
        name="after",
    )(*[in_vmem(other) for other in (value, *others)])


def bundle(pieces, others=()):
    pieces = [piece if isinstance(piece, tuple) else (piece, None, piece.shape[0]) for piece in pieces]
    count = len(pieces)
    width, dtype = pieces[0][0].shape[1], pieces[0][0].dtype

    def kernel(*refs):
        place = 0
        for ref, (_, begin, size) in zip(refs[:count], pieces):
            first = 0 if begin is None else begin()
            refs[-1][place : place + size, :] = ref[pl.ds(first, size), :]
            place += size

    values = [array for array, _, _ in pieces] + list(others)
    return pl.pallas_call(
        kernel,
        out_shape=pltpu.VMEM((sum(size for _, _, size in pieces), width), dtype),
        in_specs=[pl.BlockSpec(memory_space=pltpu.VMEM)] * len(values),
        out_specs=pl.BlockSpec(memory_space=pltpu.VMEM),
        compiler_params=pltpu.CompilerParams(vmem_limit_bytes=2 * MIB),
        name="bundle",
    )(*[in_vmem(value) for value in values])


def row_mask(lengths, slots, rows, choices, rank, others):
    requests = lengths.shape[1]

    def kernel(lengths_ref, slots_ref, *refs):
        out = refs[-1]
        group = store_index()
        position = lax.broadcasted_iota(jnp.int32, out.shape, 0)
        lane_slot = lax.broadcasted_iota(jnp.int32, out.shape, 1) // rank
        chosen = jnp.full(out.shape, slots_ref[group, 0], jnp.int32)
        begin = lengths_ref[0, 0]
        for request in range(1, requests):
            change = slots_ref[group, request] - slots_ref[group, request - 1]
            chosen += jnp.where(position >= begin, change, 0)
            begin += lengths_ref[0, request]
        out[...] = (chosen == lane_slot).astype(jnp.float32)

    return pl.pallas_call(
        kernel,
        out_shape=pltpu.VMEM((rows, choices * rank), jnp.float32),
        in_specs=[pl.BlockSpec(memory_space=pltpu.SMEM)] * 2
        + [pl.BlockSpec(memory_space=pltpu.VMEM)] * len(others),
        out_specs=pl.BlockSpec(memory_space=pltpu.VMEM),
        compiler_params=pltpu.CompilerParams(vmem_limit_bytes=2 * MIB),
        name="row_mask",
    )(lengths, slots, *[in_vmem(other) for other in others])


def row_slots(lengths, slots, rows):
    ends = jnp.cumsum(lengths)
    starts = ends - lengths
    position = jnp.arange(rows, dtype=jnp.int32)[:, None]
    member = (position >= starts[None, :]) & (position < ends[None, :])
    return jnp.sum(jnp.where(member, slots[None, :], 0), axis=1)


def swap(block, axis, bit):
    size = lax.axis_size(axis)
    return lax.ppermute(block, axis, [(i, i ^ bit) for i in range(size)])


def send_pairs(payload, target):
    size = 2 * lax.axis_size("line") * lax.axis_size("plane")
    return lax.ppermute(payload, AXES[1:], [(i, target(i)) for i in range(size)])


ROWS = {
    "Z1": ("line", 1, ["own"]),
    "Z2": ("line", 2, ["own"]),
    "Z3": ("line", 1, ["Z2"]),
    "Y0": ("plane", 1, ["own"]),
    "Y1": ("plane", 1, ["Z1"]),
    "Y2": ("plane", 1, ["Z2"]),
    "Y3": ("plane", 1, ["Z3"]),
    "X1": ("parts", 1, ["Z1", "Y0"]),
    "X2": ("parts", 1, ["Z2", "Y1"]),
    "X3": ("parts", 1, ["Z3", "Y2"]),
    "X4": ("parts", 1, ["Y3"]),
}
PLACES = {name: (int(name[1]), int(name[0] == "Y")) for name in ROWS if name[0] in "ZY"}
STEPS = (("whole", "CW", "S1", "X1"), ("C1", "S2", "X2"), ("C2", "S3", "X3"), ("C3", "S4", "X4", "C4"))


def body(
    tokens, base_weight, adapter_down, adapter_up, request_lengths, group_adapters, request_slot
):
    rank = adapter_down.shape[2]
    choices = group_adapters.shape[1]
    width = base_weight.shape[1]
    shard_width = adapter_up.shape[1]
    pair = choices * rank
    operands = (
        jnp.transpose(group_adapters),
        jnp.swapaxes(adapter_down, 1, 2),
        jnp.transpose(adapter_up, (1, 2, 0)).reshape(shard_width * rank, adapter_up.shape[0]),
        base_weight,
        shard_width,
    )

    def early_targets():
        targets = []
        for n, mask in enumerate(EARLY):
            targets += [(n, target) for target in direct_targets(mask)]
        return targets

    def late_targets():
        core = lax.axis_index("core")
        targets = []
        for n, mask in enumerate(LATE):
            targets += [(n, target) for target in direct_targets(mask)]
        for n, masks in enumerate(ROUNDS):
            targets += [(len(LATE) + n, target) for target in round_targets(masks, core)]
            targets += [
                (len(LATE) + len(ROUNDS) + n, target) for target in round_targets(masks, 1 - core)
            ]
        me = store_index()
        last = len(LATE) + 2 * len(ROUNDS)
        return targets + [(last - 1, me ^ 1), (last, me)]

    early_count = len(EARLY)
    late_counts = (2,) * len(LATE) + (2,) * (2 * len(ROUNDS) - 1) + (3, 1)
    values = {}

    def get(name):
        if name not in values:
            values[name] = make(name)
        return values[name]

    def wait(name):
        return [get(other) for other in TIES.get(name, ())]

    def first_messages():
        messages, whole, half = make_messages(
            *operands, (2,) * early_count, early_targets, 1, wait("early")
        )
        for mask, message in zip(EARLY, messages):
            values[f"pair{mask}"] = message
        values["whole"], values["own"] = whole, half

    def other_messages():
        messages, _, _ = make_messages(
            *operands, late_counts, late_targets, COST, [get("own"), *wait("late")]
        )
        for mask, message in zip(LATE, messages):
            values[f"pair{mask}"] = message
        for n, message in enumerate(messages[len(LATE) :]):
            kind, number = divmod(n, len(ROUNDS))
            values[("mine", "theirs", "local")[kind] + str(number)] = message

    def make(name):
        kind, number = name[0], name[1:]
        if name in ("whole", "own") or name in [f"pair{mask}" for mask in EARLY]:
            first_messages()
            return values[name]
        if name[:4] in ("pair", "mine", "thei", "loca"):
            other_messages()
            return values[name]
        if name in ROWS:
            axis, mask, sources = ROWS[name]
            others = wait(name)
            if kind == "X":
                payload = get("S" + number)
            elif others:
                payload = bundle([get(source) for source in sources], others)
            else:
                payload = get(sources[0])
            return swap(payload, axis, mask)
        if kind == "S":
            return bundle([get(source) for source in ROWS["X" + number][2]], wait("X" + number))
        if name == "CW":
            others = wait(name)
            return swap(bundle([get("whole")], others) if others else get("whole"), "core", 1)
        if kind == "C":
            return swap(bundle([get("S" + number), get("X" + number)], wait(name)), "core", 1)
        if kind == "T":
            return swap(after(get("theirs" + number), *wait(name)), "core", 1)
        if kind == "P":
            message = get("pair" + number)
            others = wait(name)
            payload = after(message, *others) if others else message
            return send_pairs(payload, lambda i: i ^ (2 * int(number)))
        if kind == "H":
            got, length = get("P" + number), get("local0").shape[0]
            return swap(bundle([(got, lambda: length, length)], wait(name)), "core", 1)
        if kind == "R":
            masks, length = ROUNDS[int(number)], get("local0").shape[0]
            theirs = (get("T" + number), lambda: 0, 2 * length)
            payload = bundle([get("mine" + number), theirs], wait(name))
            return send_pairs(payload, lambda i: i ^ (2 * masks[i % 2]))
        if kind == "F":
            got, length = get("R" + number), get("local0").shape[0]

            def place(i):
                return pl.multiple_of((2 * i + 1 - lax.axis_index("core")) * length, 16)

            parts = [(got, functools.partial(place, i), length) for i in range(2)]
            return swap(bundle(parts, wait(name)), "core", 1)
        if name == "mask":
            return row_mask(
                request_lengths, request_slot, tokens.shape[0], choices, rank, wait(name)
            )
        if name == "AB":
            every = [f"P{mask}" for mask in EARLY + LATE] + [f"R{n}" for n in range(len(ROUNDS))]
            buffers, places = arrivals([other for other in every if other not in LAST])

            def sources():
                me = store_index()
                return [(0, 0, me), (1, 2 * length_rows, me ^ 1)] + places(2)

            shrunk, values["second factors"] = adapt_begin(
                tokens,
                (get("local0"), get(f"T{len(ROUNDS) - 1}"), *buffers, *wait(name)),
                sources,
                length_rows,
                pair,
                shard_width,
                width,
                0.6,
            )
            return shrunk
        if kind == "B":
            step = int(number)
            start = get(f"B{step - 1}") if step else None
            bundles = [(masks_of(part), get(part)) for part in STEPS[step]]
            return base_product(tokens, bundles, start, wait(name))
        raise KeyError(name)

    def masks_of(part):
        if part == "whole":
            return [(None, 0, 0, 0)]
        if part == "CW":
            return [(None, 0, 0, 1)]
        places = [PLACES[source] for source in ROWS["X" + part[1]][2]]
        if part[0] == "C":
            return [(x, z, y, 1) for x in range(2) for z, y in places]
        return [(int(part[0] == "X"), z, y, 0) for z, y in places]

    length_rows = base_weight.shape[0] // HALF * pair + shard_width * pair // HALF

    def pair_sources(mask, n):
        core, chip = lax.axis_index("core"), store_index() // 2
        source = (chip ^ mask) * 2
        return [(n, 0, source + core), (n + 1, 0, source + 1 - core)]

    def round_sources(masks, n):
        core, chip = lax.axis_index("core"), store_index() // 2
        own, other = jnp.where(core == 0, *masks), jnp.where(core == 0, *masks[::-1])
        places = []
        for i in range(2):
            places.append((n, (2 * i + core) * length_rows, (chip ^ own) * 2 + (core ^ i)))
            places.append((n + 1, i * length_rows, (chip ^ other) * 2 + (core ^ 1 ^ i)))
        return places

    def arrivals(names):
        buffers = []
        for name in names:
            buffers += [get(name), get(("H" if name[0] == "P" else "F") + name[1:])]

        def sources(offset=0):
            places = []
            for n, name in enumerate(names):
                if name[0] == "P":
                    places += pair_sources(int(name[1:]), offset + 2 * n)
                else:
                    places += round_sources(ROUNDS[int(name[1:])], offset + 2 * n)
            return places

        return buffers, sources

    end_buffers, end_places = arrivals(list(LAST))
    return adapt_end(
        tokens,
        tuple(end_buffers),
        end_places,
        length_rows,
        get("mask"),
        get(f"B{len(STEPS) - 1}"),
        (get("AB"), values["second factors"]),
        shard_width,
        0.4,
    )


def plain_body(
    tokens, base_weight, adapter_down, adapter_up, request_lengths, group_adapters, request_slot
):
    store = AXES[1:]
    rank = adapter_down.shape[2]
    choices = group_adapters.shape[1]
    group = lax.axis_index(store)
    wanted = jnp.transpose(group_adapters)
    slots = lax.dynamic_index_in_dim(request_slot, group, 0, keepdims=False)
    slot_of_row = row_slots(request_lengths[0], slots, tokens.shape[0])
    lane_slot = jnp.arange(choices * rank, dtype=jnp.int32)[None, :] // rank
    mask = (slot_of_row[:, None] == lane_slot).astype(jnp.float32)
    exchange = functools.partial(
        lax.all_to_all, axis_name=store, split_axis=1, concat_axis=1, tiled=True
    )
    down = exchange(jnp.take(adapter_down, wanted, axis=0))
    up = exchange(jnp.take(adapter_up, wanted, axis=0))
    weight = lax.all_gather(base_weight, store, axis=0, tiled=True)
    down = down.reshape(choices, tokens.shape[1], rank)
    up = up.reshape(choices, base_weight.shape[1], rank)
    base = jnp.dot(tokens, weight, preferred_element_type=jnp.float32)
    shrink = jnp.einsum("td,kdr->tkr", tokens, down, preferred_element_type=jnp.float32)
    picked = (shrink.reshape(mask.shape) * mask).astype(jnp.bfloat16)
    picked = picked.reshape(shrink.shape)
    delta = jnp.einsum("tkr,kvr->tv", picked, up, preferred_element_type=jnp.float32)
    return (base + delta).astype(jnp.bfloat16)


def solution(mesh):
    parts, size = mesh.shape["parts"], mesh.shape["store"]
    chips = size // 2
    plane = 1
    while 4 * plane * plane <= chips:
        plane *= 2
    lines = chips // plane
    split = Mesh(mesh.devices.reshape(parts, lines, plane, 2), AXES)
    store = AXES[1:]

    def run(tokens, base_weight, *rest):
        small = (parts, lines, plane) == (2, 4, 2) and base_weight.shape[0] // size == 2 * HALF
        return jax.shard_map(
            body if small else plain_body,
            mesh=split,
            in_specs=(
                P(AXES, None),
                P(store, None),
                P(None, store, None),
                P(None, store, None),
                P(AXES, None),
                P("parts", None),
                P("parts", None),
            ),
            out_specs=P(AXES, None),
            check_vma=False,
        )(tokens, base_weight, *rest)

    return run
```

```python
import functools

import jax
import jax.numpy as jnp
from jax import lax
from jax.experimental import pallas as pl
from jax.experimental.pallas import tpu as pltpu
from jax.sharding import Mesh
from jax.sharding import PartitionSpec as P

HALF = 256
MIB = 1024 * 1024
COST = 1
AXES = ("parts", "line", "plane", "core")


def in_vmem(value):
    return pltpu.with_memory_space_constraint(value, pltpu.VMEM)


def in_hbm(value):
    return pltpu.with_memory_space_constraint(value, pltpu.HBM)


def store_index():
    return (lax.axis_index("line") * 2 + lax.axis_index("plane")) * 2 + lax.axis_index("core")


EARLY, LATE = (), (5,)
ROUNDS = ((1, 4), (3, 7), (2, 6))
SWAPS = ((0,), (1,), (2,))
LAST = ("R1", "P5")
TIES = {
    "Y1": ("local",),
    "Y2": ("B0", "T0", "T2",),
    "C1": ("X2", "mask",),
    "C2": ("X3",),
    "C3": ("AB", "B0", "Y2",),
    "C4": ("AB", "B1", "R1", "Y2",),
    "B0": ("CW", "Y1", "Z1", "Z2",),
    "B1": ("Y2",),
    "B2": ("B1", "T0",),
    "F0": ("Y3",),
    "R2": ("P5",),
    "T1": ("R0", "Y2", "Z3",),
    "T2": ("Y1", "Z2",),
    "mask": ("B0", "T1", "Z2",),
}


def direct_targets(mask):
    return [store_index() ^ (2 * mask + i) for i in range(2)]


def round_targets(masks, core):
    chip = store_index() // 2
    mask = jnp.where(core == 0, *masks)
    return [(chip ^ mask) * 2 + i for i in range(2)]


def send_kernel(targets_of, wanted, down, up, *refs):
    targets = targets_of()
    outs = refs[:-6]
    table, pick, even_rows, odd_rows, table_sem, sems = refs[-6:]
    choices = wanted.shape[0]
    rank = down.shape[1]
    halves = down.shape[2] // HALF
    padded = pick.shape[0] // choices
    count = even_rows.shape[0] // padded
    length = choices * halves * rank + count
    copies = []

    def begin(source, target):
        copy = pltpu.make_async_copy(source, target, sems.at[len(copies)])
        copy.start()
        copies.append(copy)

    places = []
    for out, target in targets:
        places.append((outs[out], sum(place[0] is outs[out] for place in places) * length))
        for choice in range(choices):
            adapter = wanted[choice, target]
            for part in range(halves):
                start = places[-1][1] + (part * choices + choice) * rank
                begin(
                    down.at[adapter, :, pl.ds(part * HALF, HALF)],
                    outs[out].at[pl.ds(start, rank), :],
                )
    table_copy = pltpu.make_async_copy(up, table, table_sem)
    table_copy.start()

    ids = lax.broadcasted_iota(jnp.int32, (1, up.shape[1]), 1)
    pick[...] = jnp.zeros_like(pick)
    for choice in range(choices):
        for n, (_, target) in enumerate(targets):
            here = (ids == wanted[choice, target]).astype(jnp.float32)
            pick[pl.ds(choice * padded + n, 1), :] = here
    table_copy.wait()
    rows = lax.dot_general(
        pick[...].astype(jnp.bfloat16),
        table[...],
        (((1,), (1,)), ((), ())),
        preferred_element_type=jnp.float32,
    )
    first, second = rows[:padded], rows[padded:]
    low = lax.broadcasted_iota(jnp.int32, (padded, 2 * rank), 1) < rank
    for i in range(count):
        a = first[:, 2 * rank * i : 2 * rank * (i + 1)]
        b = second[:, 2 * rank * i : 2 * rank * (i + 1)]
        even_rows[pl.ds(i, padded, stride=count), :] = jnp.where(low, a, pltpu.roll(b, rank, 1))
        odd_rows[pl.ds(i, padded, stride=count), :] = jnp.where(low, pltpu.roll(a, rank, 1), b)
    for n, (out, start) in enumerate(places):
        own = pl.ds(n * count, count)
        to = pl.ds(start + length - count, count)
        out[to, : 2 * rank] = even_rows[own, :].astype(jnp.bfloat16)
        out[to, 2 * rank :] = odd_rows[own, :].astype(jnp.bfloat16)
    for copy in copies:
        copy.wait()


def make_messages(wanted, down, up, shard_width, counts, targets_of, cost, others=()):
    choices = wanted.shape[0]
    rank, depth = down.shape[1:]
    halves = depth // HALF
    count = shard_width * choices * rank // HALF
    length = choices * rank * halves + count
    padded = -(-sum(counts) // 8) * 8

    def kernel(*refs):
        send_kernel(targets_of, *refs[:3], *refs[3 + len(others) :])

    return pl.pallas_call(
        kernel,
        out_shape=[pltpu.VMEM((n * length, HALF), jnp.bfloat16) for n in counts],
        in_specs=[pl.BlockSpec(memory_space=pltpu.SMEM)]
        + [pl.BlockSpec(memory_space=pltpu.HBM)] * 2
        + [pl.BlockSpec(memory_space=pltpu.VMEM)] * len(others),
        out_specs=[pl.BlockSpec(memory_space=pltpu.VMEM)] * len(counts),
        scratch_shapes=[
            pltpu.VMEM(up.shape, up.dtype),
            pltpu.VMEM((choices * padded, up.shape[1]), jnp.float32),
            pltpu.VMEM((padded * count, 2 * rank), jnp.float32),
            pltpu.VMEM((padded * count, 2 * rank), jnp.float32),
            pltpu.SemaphoreType.DMA,
            pltpu.SemaphoreType.DMA((sum(counts) * choices * halves,)),
        ],
        compiler_params=pltpu.CompilerParams(vmem_limit_bytes=16 * MIB),
        cost_estimate=pl.CostEstimate(
            flops=0, bytes_accessed=4 * cost * sum(counts) * length * HALF, transcendentals=0
        ),
        name="make_messages",
    )(wanted, in_hbm(down), in_hbm(up), *[in_vmem(other) for other in others])


def load_rows(weight):
    def kernel(source, whole, half, sems):
        x = lax.axis_index("parts")
        own = pltpu.make_async_copy(source.at[pl.ds(x * HALF, HALF), :], half, sems.at[0])
        rest = pltpu.make_async_copy(source, whole, sems.at[1])
        own.start()
        rest.start()
        own.wait()
        rest.wait()

    return pl.pallas_call(
        kernel,
        out_shape=[
            pltpu.VMEM(weight.shape, weight.dtype),
            pltpu.VMEM((HALF, weight.shape[1]), weight.dtype),
        ],
        in_specs=[pl.BlockSpec(memory_space=pltpu.HBM)],
        out_specs=[pl.BlockSpec(memory_space=pltpu.VMEM)] * 2,
        scratch_shapes=[pltpu.SemaphoreType.DMA((2,))],
        compiler_params=pltpu.CompilerParams(vmem_limit_bytes=2 * MIB),
        name="load_rows",
    )(in_hbm(weight))


def base_product(tokens, bundles, start=None, others=()):
    rows, depth = tokens.shape
    width = bundles[0][1].shape[1]
    count = len(bundles)
    total_rows = sum(bundle.shape[0] for _, bundle in bundles)

    def kernel(tokens_ref, *refs):
        parts, out = refs[:count], refs[-1]
        place = dict(zip(AXES, [lax.axis_index(name) for name in AXES]))
        first = True
        for (masks, _), part in zip(bundles, parts):
            left = []
            for x, z, y, core in masks:
                z, y, core = place["line"] ^ z, place["plane"] ^ y, place["core"] ^ core
                owner = (z * 2 + y) * 2 + core
                if x is None:
                    column, size = pl.multiple_of(owner * 2 * HALF, 2 * HALF), 2 * HALF
                else:
                    column = pl.multiple_of((owner * 2 + (place["parts"] ^ x)) * HALF, HALF)
                    size = HALF
                left.append(tokens_ref[:, pl.ds(column, size)])
            total = jnp.dot(
                jnp.concatenate(left, axis=1), part[...], preferred_element_type=jnp.float32
            )
            if first:
                out[...] = total if start is None else refs[count][...] + total
            else:
                out[...] += total
            first = False

    extra = ([] if start is None else [start]) + list(others)
    return pl.pallas_call(
        kernel,
        out_shape=pltpu.VMEM((rows, width), jnp.float32),
        in_specs=[pl.BlockSpec(memory_space=pltpu.VMEM)] * (1 + count + len(extra)),
        out_specs=pl.BlockSpec(memory_space=pltpu.VMEM),
        compiler_params=pltpu.CompilerParams(vmem_limit_bytes=16 * MIB),
        cost_estimate=pl.CostEstimate(
            flops=2 * rows * total_rows * width,
            bytes_accessed=2 * rows * total_rows + 2 * total_rows * width + 4 * rows * width,
            transcendentals=0,
        ),
        name="base_product",
    )(*[in_vmem(value) for value in (tokens, *[bundle for _, bundle in bundles], *extra)])


def shrink_part(sources, length, tokens, messages, wide, ups):
    pair = wide.shape[1]
    step = HALF // pair
    groups = wide.shape[0] // ups.shape[0]
    depth = tokens.shape[1] // groups
    halves = depth // HALF
    total = None
    for n, start, source in sources():
        begin = start if isinstance(start, int) else pl.multiple_of(start, 16)
        message = messages[n][pl.ds(begin, length), :]
        column = pl.multiple_of(source * depth, depth)
        down = jnp.concatenate(
            [message[half * pair : (half + 1) * pair, :] for half in range(halves)], axis=1
        )
        part = lax.dot_general(
            tokens[:, pl.ds(column, depth)],
            down,
            (((1,), (1,)), ((), ())),
            preferred_element_type=jnp.float32,
        )
        total = part if total is None else total + part
        up = message[halves * pair :, :].astype(jnp.float32)
        count = up.shape[0]
        for i in range(step):
            ups[pl.ds(i, count, stride=step), :] = up[:, i * pair : (i + 1) * pair]
        own = pl.ds(pl.multiple_of(source * count * step, count * step), count * step)
        wide[own, :] = ups[...].astype(jnp.bfloat16)
    return total


def adapt_cost(tokens, pair, share):
    return pl.CostEstimate(
        flops=int(4 * tokens.size * pair * share),
        bytes_accessed=int(2 * tokens.size * share),
        transcendentals=0,
    )


def adapt_begin(tokens, messages, sources, length, pair, shard_width, width, share):
    rows = tokens.shape[0]
    count = len(messages)

    def kernel(tokens_ref, *refs):
        shrink, wide, ups = refs[count:]
        wide[...] = jnp.zeros_like(wide)
        shrink[...] = shrink_part(sources, length, tokens_ref, refs[:count], wide, ups)

    return pl.pallas_call(
        kernel,
        out_shape=[
            pltpu.VMEM((rows, pair), jnp.float32),
            pltpu.VMEM((width, pair), jnp.bfloat16),
        ],
        in_specs=[pl.BlockSpec(memory_space=pltpu.VMEM)] * (1 + count),
        out_specs=[pl.BlockSpec(memory_space=pltpu.VMEM)] * 2,
        scratch_shapes=[pltpu.VMEM((shard_width, pair), jnp.float32)],
        compiler_params=pltpu.CompilerParams(vmem_limit_bytes=16 * MIB),
        cost_estimate=adapt_cost(tokens, pair, share),
        name="adapt_begin",
    )(*[in_vmem(value) for value in (tokens, *messages)])


def adapt_end(tokens, messages, sources, length, mask, base, begun, shard_width, share):
    rows, width = base.shape
    pair = mask.shape[1]
    count = len(messages)

    def kernel(tokens_ref, mask_ref, base_ref, shrunk, widened, *refs):
        out, wide, ups = refs[count:]
        wide[...] = widened[...]
        shrink = shrunk[...]
        shrink += shrink_part(sources, length, tokens_ref, refs[:count], wide, ups)
        picked = (shrink * mask_ref[...]).astype(jnp.bfloat16)
        delta = lax.dot_general(
            picked, wide[...], (((1,), (1,)), ((), ())), preferred_element_type=jnp.float32
        )
        out[...] = (base_ref[...] + delta).astype(out.dtype)

    values = (tokens, mask, base, *begun, *messages)
    return pl.pallas_call(
        kernel,
        out_shape=jax.ShapeDtypeStruct((rows, width), jnp.bfloat16),
        in_specs=[pl.BlockSpec(memory_space=pltpu.VMEM)] * len(values),
        out_specs=pl.BlockSpec(memory_space=pltpu.VMEM),
        scratch_shapes=[
            pltpu.VMEM((width, pair), jnp.bfloat16),
            pltpu.VMEM((shard_width, pair), jnp.float32),
        ],
        compiler_params=pltpu.CompilerParams(vmem_limit_bytes=16 * MIB),
        cost_estimate=adapt_cost(tokens, pair, share),
        name="adapt_end",
    )(*[in_vmem(value) for value in values])


def after(value, *others):
    def kernel(*refs):
        pass

    return pl.pallas_call(
        kernel,
        out_shape=pltpu.VMEM(value.shape, value.dtype),
        in_specs=[pl.BlockSpec(memory_space=pl.ANY)] * (1 + len(others)),
        out_specs=pl.BlockSpec(memory_space=pl.ANY),
        input_output_aliases={0: 0},
        compiler_params=pltpu.CompilerParams(vmem_limit_bytes=MIB),
        name="after",
    )(*[in_vmem(other) for other in (value, *others)])


def bundle(pieces, others=()):
    pieces = [piece if isinstance(piece, tuple) else (piece, None, piece.shape[0]) for piece in pieces]
    count = len(pieces)
    width, dtype = pieces[0][0].shape[1], pieces[0][0].dtype

    def kernel(*refs):
        place = 0
        for ref, (_, begin, size) in zip(refs[:count], pieces):
            first = 0 if begin is None else begin()
            refs[-1][place : place + size, :] = ref[pl.ds(first, size), :]
            place += size

    values = [array for array, _, _ in pieces] + list(others)
    return pl.pallas_call(
        kernel,
        out_shape=pltpu.VMEM((sum(size for _, _, size in pieces), width), dtype),
        in_specs=[pl.BlockSpec(memory_space=pltpu.VMEM)] * len(values),
        out_specs=pl.BlockSpec(memory_space=pltpu.VMEM),
        compiler_params=pltpu.CompilerParams(vmem_limit_bytes=2 * MIB),
        name="bundle",
    )(*[in_vmem(value) for value in values])


def row_mask(lengths, slots, rows, choices, rank, others):
    requests = lengths.shape[1]

    def kernel(lengths_ref, slots_ref, *refs):
        out = refs[-1]
        group = store_index()
        position = lax.broadcasted_iota(jnp.int32, out.shape, 0)
        lane_slot = lax.broadcasted_iota(jnp.int32, out.shape, 1) // rank
        chosen = jnp.full(out.shape, slots_ref[group, 0], jnp.int32)
        begin = lengths_ref[0, 0]
        for request in range(1, requests):
            change = slots_ref[group, request] - slots_ref[group, request - 1]
            chosen += jnp.where(position >= begin, change, 0)
            begin += lengths_ref[0, request]
        out[...] = (chosen == lane_slot).astype(jnp.float32)

    return pl.pallas_call(
        kernel,
        out_shape=pltpu.VMEM((rows, choices * rank), jnp.float32),
        in_specs=[pl.BlockSpec(memory_space=pltpu.SMEM)] * 2
        + [pl.BlockSpec(memory_space=pltpu.VMEM)] * len(others),
        out_specs=pl.BlockSpec(memory_space=pltpu.VMEM),
        compiler_params=pltpu.CompilerParams(vmem_limit_bytes=2 * MIB),
        name="row_mask",
    )(lengths, slots, *[in_vmem(other) for other in others])


def row_slots(lengths, slots, rows):
    ends = jnp.cumsum(lengths)
    starts = ends - lengths
    position = jnp.arange(rows, dtype=jnp.int32)[:, None]
    member = (position >= starts[None, :]) & (position < ends[None, :])
    return jnp.sum(jnp.where(member, slots[None, :], 0), axis=1)


def swap(block, axis, bit):
    size = lax.axis_size(axis)
    return lax.ppermute(block, axis, [(i, i ^ bit) for i in range(size)])


def send_pairs(payload, target):
    size = 2 * lax.axis_size("line") * lax.axis_size("plane")
    return lax.ppermute(payload, AXES[1:], [(i, target(i)) for i in range(size)])


ROWS = {
    "Z1": ("line", 1, ["own"]),
    "Z2": ("line", 2, ["own"]),
    "Z3": ("line", 1, ["Z2"]),
    "Y0": ("plane", 1, ["own"]),
    "Y1": ("plane", 1, ["Z1"]),
    "Y2": ("plane", 1, ["Z2"]),
    "Y3": ("plane", 1, ["Z3"]),
    "X1": ("parts", 1, ["Z1", "Y0"]),
    "X2": ("parts", 1, ["Z2", "Y1"]),
    "X3": ("parts", 1, ["Z3", "Y2"]),
    "X4": ("parts", 1, ["Y3"]),
}
PLACES = {name: (int(name[1]), int(name[0] == "Y")) for name in ROWS if name[0] in "ZY"}
STEPS = (("whole", "CW", "S1", "X1"), ("C1", "S2", "X2"), ("C2", "S3", "X3"), ("C3", "S4", "X4", "C4"))


def body(
    tokens, base_weight, adapter_down, adapter_up, request_lengths, group_adapters, request_slot
):
    rank = adapter_down.shape[2]
    choices = group_adapters.shape[1]
    width = base_weight.shape[1]
    shard_width = adapter_up.shape[1]
    pair = choices * rank
    operands = (
        jnp.transpose(group_adapters),
        jnp.swapaxes(adapter_down, 1, 2),
        jnp.transpose(adapter_up, (1, 2, 0)).reshape(shard_width * rank, adapter_up.shape[0]),
        shard_width,
    )

    def early_targets():
        targets = []
        for n, mask in enumerate(EARLY):
            targets += [(n, target) for target in direct_targets(mask)]
        return targets

    def late_targets():
        core = lax.axis_index("core")
        targets = []
        for n, mask in enumerate(LATE):
            targets += [(n, target) for target in direct_targets(mask)]
        for n, masks in enumerate(ROUNDS):
            targets += [(len(LATE) + n, target) for target in round_targets(masks, core)]
        first = len(LATE) + len(ROUNDS)
        for n, rounds in enumerate(SWAPS):
            for number in rounds:
                targets += [
                    (first + n, target) for target in round_targets(ROUNDS[number], 1 - core)
                ]
        me = store_index()
        last = first + len(SWAPS)
        return targets + [(last - 1, me ^ 1), (last, me)]

    swap_counts = [2 * len(rounds) for rounds in SWAPS]
    swap_counts[-1] += 1
    late_counts = (2,) * (len(LATE) + len(ROUNDS)) + tuple(swap_counts) + (1,)
    values = {}

    def get(name):
        if name not in values:
            values[name] = make(name)
        return values[name]

    def wait(name):
        return [get(other) for other in TIES.get(name, ())]

    def early_messages():
        counts = (2,) * len(EARLY)
        messages = make_messages(*operands, counts, early_targets, 1, wait("early"))
        for mask, message in zip(EARLY, messages):
            values[f"pair{mask}"] = message

    def late_messages():
        messages = make_messages(*operands, late_counts, late_targets, COST, wait("late"))
        names = [f"pair{mask}" for mask in LATE] + [f"mine{n}" for n in range(len(ROUNDS))]
        names += [f"theirs{n}" for n in range(len(SWAPS))] + ["local"]
        values.update(zip(names, messages))

    def make(name):
        kind, number = name[0], name[1:]
        if name in ("whole", "own"):
            values["whole"], values["own"] = load_rows(base_weight)
            return values[name]
        if name in [f"pair{mask}" for mask in EARLY]:
            early_messages()
            return values[name]
        if name[:4] in ("pair", "mine", "thei", "loca"):
            late_messages()
            return values[name]
        if name in ROWS:
            axis, mask, sources = ROWS[name]
            others = wait(name)
            if kind == "X":
                payload = get("S" + number)
            elif others:
                payload = bundle([get(source) for source in sources], others)
            else:
                payload = get(sources[0])
            return swap(payload, axis, mask)
        if kind == "S":
            return bundle([get(source) for source in ROWS["X" + number][2]], wait("X" + number))
        if name == "CW":
            others = wait(name)
            return swap(bundle([get("whole")], others) if others else get("whole"), "core", 1)
        if kind == "C":
            return swap(bundle([get("S" + number), get("X" + number)], wait(name)), "core", 1)
        if kind == "T":
            return swap(after(get("theirs" + number), *wait(name)), "core", 1)
        if kind == "P":
            message = get("pair" + number)
            others = wait(name)
            payload = after(message, *others) if others else message
            return send_pairs(payload, lambda i: i ^ (2 * int(number)))
        if kind == "H":
            got, length = get("P" + number), get("local").shape[0]
            return swap(bundle([(got, lambda: length, length)], wait(name)), "core", 1)
        if kind == "R":
            masks, length = ROUNDS[int(number)], get("local").shape[0]
            group = [n for n, rounds in enumerate(SWAPS) if int(number) in rounds][0]
            begin = SWAPS[group].index(int(number)) * 2 * length
            theirs = (get(f"T{group}"), lambda: begin, 2 * length)
            payload = bundle([get("mine" + number), theirs], wait(name))
            return send_pairs(payload, lambda i: i ^ (2 * masks[i % 2]))
        if kind == "F":
            got, length = get("R" + number), get("local").shape[0]

            def place(i):
                return pl.multiple_of((2 * i + 1 - lax.axis_index("core")) * length, 16)

            parts = [(got, functools.partial(place, i), length) for i in range(2)]
            return swap(bundle(parts, wait(name)), "core", 1)
        if name == "mask":
            return row_mask(
                request_lengths, request_slot, tokens.shape[0], choices, rank, wait(name)
            )
        if name == "AB":
            every = [f"P{mask}" for mask in EARLY + LATE] + [f"R{n}" for n in range(len(ROUNDS))]
            buffers, places = arrivals([other for other in every if other not in LAST])

            def sources():
                me = store_index()
                return [(0, 0, me), (1, 2 * len(SWAPS[-1]) * length_rows, me ^ 1)] + places(2)

            shrunk, values["second factors"] = adapt_begin(
                tokens,
                (get("local"), get(f"T{len(SWAPS) - 1}"), *buffers, *wait(name)),
                sources,
                length_rows,
                pair,
                shard_width,
                width,
                0.6,
            )
            return shrunk
        if kind == "B":
            step = int(number)
            start = get(f"B{step - 1}") if step else None
            bundles = [(masks_of(part), get(part)) for part in STEPS[step]]
            return base_product(tokens, bundles, start, wait(name))
        raise KeyError(name)

    def masks_of(part):
        if part == "whole":
            return [(None, 0, 0, 0)]
        if part == "CW":
            return [(None, 0, 0, 1)]
        places = [PLACES[source] for source in ROWS["X" + part[1]][2]]
        if part[0] == "C":
            return [(x, z, y, 1) for x in range(2) for z, y in places]
        return [(int(part[0] == "X"), z, y, 0) for z, y in places]

    length_rows = base_weight.shape[0] // HALF * pair + shard_width * pair // HALF

    def pair_sources(mask, n):
        core, chip = lax.axis_index("core"), store_index() // 2
        source = (chip ^ mask) * 2
        return [(n, 0, source + core), (n + 1, 0, source + 1 - core)]

    def round_sources(masks, n):
        core, chip = lax.axis_index("core"), store_index() // 2
        own, other = jnp.where(core == 0, *masks), jnp.where(core == 0, *masks[::-1])
        places = []
        for i in range(2):
            places.append((n, (2 * i + core) * length_rows, (chip ^ own) * 2 + (core ^ i)))
            places.append((n + 1, i * length_rows, (chip ^ other) * 2 + (core ^ 1 ^ i)))
        return places

    def arrivals(names):
        buffers = []
        for name in names:
            buffers += [get(name), get(("H" if name[0] == "P" else "F") + name[1:])]

        def sources(offset=0):
            places = []
            for n, name in enumerate(names):
                if name[0] == "P":
                    places += pair_sources(int(name[1:]), offset + 2 * n)
                else:
                    places += round_sources(ROUNDS[int(name[1:])], offset + 2 * n)
            return places

        return buffers, sources

    end_buffers, end_places = arrivals(list(LAST))
    return adapt_end(
        tokens,
        tuple(end_buffers),
        end_places,
        length_rows,
        get("mask"),
        get(f"B{len(STEPS) - 1}"),
        (get("AB"), values["second factors"]),
        shard_width,
        0.4,
    )


def plain_body(
    tokens, base_weight, adapter_down, adapter_up, request_lengths, group_adapters, request_slot
):
    store = AXES[1:]
    rank = adapter_down.shape[2]
    choices = group_adapters.shape[1]
    group = lax.axis_index(store)
    wanted = jnp.transpose(group_adapters)
    slots = lax.dynamic_index_in_dim(request_slot, group, 0, keepdims=False)
    slot_of_row = row_slots(request_lengths[0], slots, tokens.shape[0])
    lane_slot = jnp.arange(choices * rank, dtype=jnp.int32)[None, :] // rank
    mask = (slot_of_row[:, None] == lane_slot).astype(jnp.float32)
    exchange = functools.partial(
        lax.all_to_all, axis_name=store, split_axis=1, concat_axis=1, tiled=True
    )
    down = exchange(jnp.take(adapter_down, wanted, axis=0))
    up = exchange(jnp.take(adapter_up, wanted, axis=0))
    weight = lax.all_gather(base_weight, store, axis=0, tiled=True)
    down = down.reshape(choices, tokens.shape[1], rank)
    up = up.reshape(choices, base_weight.shape[1], rank)
    base = jnp.dot(tokens, weight, preferred_element_type=jnp.float32)
    shrink = jnp.einsum("td,kdr->tkr", tokens, down, preferred_element_type=jnp.float32)
    picked = (shrink.reshape(mask.shape) * mask).astype(jnp.bfloat16)
    picked = picked.reshape(shrink.shape)
    delta = jnp.einsum("tkr,kvr->tv", picked, up, preferred_element_type=jnp.float32)
    return (base + delta).astype(jnp.bfloat16)


def solution(mesh):
    parts, size = mesh.shape["parts"], mesh.shape["store"]
    chips = size // 2
    plane = 1
    while 4 * plane * plane <= chips:
        plane *= 2
    lines = chips // plane
    split = Mesh(mesh.devices.reshape(parts, lines, plane, 2), AXES)
    store = AXES[1:]

    def run(tokens, base_weight, *rest):
        small = (parts, lines, plane) == (2, 4, 2) and base_weight.shape[0] // size == 2 * HALF
        return jax.shard_map(
            body if small else plain_body,
            mesh=split,
            in_specs=(
                P(AXES, None),
                P(store, None),
                P(None, store, None),
                P(None, store, None),
                P(AXES, None),
                P("parts", None),
                P("parts", None),
            ),
            out_specs=P(AXES, None),
            check_vma=False,
        )(tokens, base_weight, *rest)

    return run
```

```python
import functools

import jax
import jax.numpy as jnp
from jax import lax
from jax.experimental import pallas as pl
from jax.experimental.pallas import tpu as pltpu
from jax.sharding import Mesh
from jax.sharding import PartitionSpec as P

HALF = 256
MIB = 1024 * 1024
COST = 1
AXES = ("parts", "line", "plane", "core")


def in_vmem(value):
    return pltpu.with_memory_space_constraint(value, pltpu.VMEM)


def in_hbm(value):
    return pltpu.with_memory_space_constraint(value, pltpu.HBM)


def store_index():
    return (lax.axis_index("line") * 2 + lax.axis_index("plane")) * 2 + lax.axis_index("core")


EARLY, LATE = (), (7,)
ROUNDS = ((1, 4), (5, 2), (3, 6))
SWAPS = ((0,), (1, 2))
LAST = ("R2", "R1")
TIES = {
    "Y1": ("Y0",),
    "Y2": ("B0",),
    "X1": ("Z2", "local", "mask",),
    "X2": ("P7",),
    "X3": ("R0", "X2",),
    "X4": ("R1", "X3",),
    "C4": ("AB", "B1", "R2",),
    "B0": ("CW", "Y1",),
    "B1": ("Y3",),
    "F0": ("R1",),
    "F1": ("AB", "B2",),
    "F2": ("AB", "B2",),
    "R1": ("P7", "R0",),
    "R2": ("P7",),
    "T1": ("T0",),
}


def direct_targets(mask):
    return [store_index() ^ (2 * mask + i) for i in range(2)]


def round_targets(masks, core):
    chip = store_index() // 2
    mask = jnp.where(core == 0, *masks)
    return [(chip ^ mask) * 2 + i for i in range(2)]


def send_kernel(targets_of, wanted, down, up, *refs):
    targets = targets_of()
    outs = refs[:-6]
    table, pick, even_rows, odd_rows, table_sem, sems = refs[-6:]
    choices = wanted.shape[0]
    rank = down.shape[1]
    halves = down.shape[2] // HALF
    padded = pick.shape[0] // choices
    count = even_rows.shape[0] // padded
    length = choices * halves * rank + count
    copies = []

    def begin(source, target):
        copy = pltpu.make_async_copy(source, target, sems.at[len(copies)])
        copy.start()
        copies.append(copy)

    places = []
    for out, target in targets:
        places.append((outs[out], sum(place[0] is outs[out] for place in places) * length))
        for choice in range(choices):
            adapter = wanted[choice, target]
            for part in range(halves):
                start = places[-1][1] + (part * choices + choice) * rank
                begin(
                    down.at[adapter, :, pl.ds(part * HALF, HALF)],
                    outs[out].at[pl.ds(start, rank), :],
                )
    table_copy = pltpu.make_async_copy(up, table, table_sem)
    table_copy.start()

    ids = lax.broadcasted_iota(jnp.int32, (1, up.shape[1]), 1)
    pick[...] = jnp.zeros_like(pick)
    for choice in range(choices):
        for n, (_, target) in enumerate(targets):
            here = (ids == wanted[choice, target]).astype(jnp.float32)
            pick[pl.ds(choice * padded + n, 1), :] = here
    table_copy.wait()
    rows = lax.dot_general(
        pick[...].astype(jnp.bfloat16),
        table[...],
        (((1,), (1,)), ((), ())),
        preferred_element_type=jnp.float32,
    )
    first, second = rows[:padded], rows[padded:]
    low = lax.broadcasted_iota(jnp.int32, (padded, 2 * rank), 1) < rank
    for i in range(count):
        a = first[:, 2 * rank * i : 2 * rank * (i + 1)]
        b = second[:, 2 * rank * i : 2 * rank * (i + 1)]
        even_rows[pl.ds(i, padded, stride=count), :] = jnp.where(low, a, pltpu.roll(b, rank, 1))
        odd_rows[pl.ds(i, padded, stride=count), :] = jnp.where(low, pltpu.roll(a, rank, 1), b)
    for n, (out, start) in enumerate(places):
        own = pl.ds(n * count, count)
        to = pl.ds(start + length - count, count)
        out[to, : 2 * rank] = even_rows[own, :].astype(jnp.bfloat16)
        out[to, 2 * rank :] = odd_rows[own, :].astype(jnp.bfloat16)
    for copy in copies:
        copy.wait()


def make_messages(wanted, down, up, shard_width, counts, targets_of, cost, others=()):
    choices = wanted.shape[0]
    rank, depth = down.shape[1:]
    halves = depth // HALF
    count = shard_width * choices * rank // HALF
    length = choices * rank * halves + count
    padded = -(-sum(counts) // 8) * 8

    def kernel(*refs):
        send_kernel(targets_of, *refs[:3], *refs[3 + len(others) :])

    return pl.pallas_call(
        kernel,
        out_shape=[pltpu.VMEM((n * length, HALF), jnp.bfloat16) for n in counts],
        in_specs=[pl.BlockSpec(memory_space=pltpu.SMEM)]
        + [pl.BlockSpec(memory_space=pltpu.HBM)] * 2
        + [pl.BlockSpec(memory_space=pltpu.VMEM)] * len(others),
        out_specs=[pl.BlockSpec(memory_space=pltpu.VMEM)] * len(counts),
        scratch_shapes=[
            pltpu.VMEM(up.shape, up.dtype),
            pltpu.VMEM((choices * padded, up.shape[1]), jnp.float32),
            pltpu.VMEM((padded * count, 2 * rank), jnp.float32),
            pltpu.VMEM((padded * count, 2 * rank), jnp.float32),
            pltpu.SemaphoreType.DMA,
            pltpu.SemaphoreType.DMA((sum(counts) * choices * halves,)),
        ],
        compiler_params=pltpu.CompilerParams(vmem_limit_bytes=16 * MIB),
        cost_estimate=pl.CostEstimate(
            flops=0, bytes_accessed=4 * cost * sum(counts) * length * HALF, transcendentals=0
        ),
        name="make_messages",
    )(wanted, in_hbm(down), in_hbm(up), *[in_vmem(other) for other in others])


def load_rows(weight):
    def kernel(source, whole, half, sems):
        x = lax.axis_index("parts")
        own = pltpu.make_async_copy(source.at[pl.ds(x * HALF, HALF), :], half, sems.at[0])
        rest = pltpu.make_async_copy(source, whole, sems.at[1])
        own.start()
        rest.start()
        own.wait()
        rest.wait()

    return pl.pallas_call(
        kernel,
        out_shape=[
            pltpu.VMEM(weight.shape, weight.dtype),
            pltpu.VMEM((HALF, weight.shape[1]), weight.dtype),
        ],
        in_specs=[pl.BlockSpec(memory_space=pltpu.HBM)],
        out_specs=[pl.BlockSpec(memory_space=pltpu.VMEM)] * 2,
        scratch_shapes=[pltpu.SemaphoreType.DMA((2,))],
        compiler_params=pltpu.CompilerParams(vmem_limit_bytes=2 * MIB),
        name="load_rows",
    )(in_hbm(weight))


def base_product(tokens, bundles, start=None, others=()):
    rows, depth = tokens.shape
    width = bundles[0][1].shape[1]
    count = len(bundles)
    total_rows = sum(bundle.shape[0] for _, bundle in bundles)

    def kernel(tokens_ref, *refs):
        parts, out = refs[:count], refs[-1]
        place = dict(zip(AXES, [lax.axis_index(name) for name in AXES]))
        first = True
        for (masks, _), part in zip(bundles, parts):
            left = []
            for x, z, y, core in masks:
                z, y, core = place["line"] ^ z, place["plane"] ^ y, place["core"] ^ core
                owner = (z * 2 + y) * 2 + core
                if x is None:
                    column, size = pl.multiple_of(owner * 2 * HALF, 2 * HALF), 2 * HALF
                else:
                    column = pl.multiple_of((owner * 2 + (place["parts"] ^ x)) * HALF, HALF)
                    size = HALF
                left.append(tokens_ref[:, pl.ds(column, size)])
            total = jnp.dot(
                jnp.concatenate(left, axis=1), part[...], preferred_element_type=jnp.float32
            )
            if first:
                out[...] = total if start is None else refs[count][...] + total
            else:
                out[...] += total
            first = False

    extra = ([] if start is None else [start]) + list(others)
    return pl.pallas_call(
        kernel,
        out_shape=pltpu.VMEM((rows, width), jnp.float32),
        in_specs=[pl.BlockSpec(memory_space=pltpu.VMEM)] * (1 + count + len(extra)),
        out_specs=pl.BlockSpec(memory_space=pltpu.VMEM),
        compiler_params=pltpu.CompilerParams(vmem_limit_bytes=16 * MIB),
        cost_estimate=pl.CostEstimate(
            flops=2 * rows * total_rows * width,
            bytes_accessed=2 * rows * total_rows + 2 * total_rows * width + 4 * rows * width,
            transcendentals=0,
        ),
        name="base_product",
    )(*[in_vmem(value) for value in (tokens, *[bundle for _, bundle in bundles], *extra)])


def shrink_part(sources, length, tokens, messages, wide, ups):
    pair = wide.shape[1]
    step = HALF // pair
    groups = wide.shape[0] // ups.shape[0]
    depth = tokens.shape[1] // groups
    halves = depth // HALF
    total = None
    for n, start, source in sources():
        begin = start if isinstance(start, int) else pl.multiple_of(start, 16)
        message = messages[n][pl.ds(begin, length), :]
        column = pl.multiple_of(source * depth, depth)
        down = jnp.concatenate(
            [message[half * pair : (half + 1) * pair, :] for half in range(halves)], axis=1
        )
        part = lax.dot_general(
            tokens[:, pl.ds(column, depth)],
            down,
            (((1,), (1,)), ((), ())),
            preferred_element_type=jnp.float32,
        )
        total = part if total is None else total + part
        up = message[halves * pair :, :].astype(jnp.float32)
        count = up.shape[0]
        for i in range(step):
            ups[pl.ds(i, count, stride=step), :] = up[:, i * pair : (i + 1) * pair]
        own = pl.ds(pl.multiple_of(source * count * step, count * step), count * step)
        wide[own, :] = ups[...].astype(jnp.bfloat16)
    return total


def adapt_cost(tokens, pair, share):
    return pl.CostEstimate(
        flops=int(4 * tokens.size * pair * share),
        bytes_accessed=int(2 * tokens.size * share),
        transcendentals=0,
    )


def adapt_begin(tokens, messages, sources, length, pair, shard_width, width, share):
    rows = tokens.shape[0]
    count = len(messages)

    def kernel(tokens_ref, *refs):
        shrink, wide, ups = refs[count:]
        wide[...] = jnp.zeros_like(wide)
        shrink[...] = shrink_part(sources, length, tokens_ref, refs[:count], wide, ups)

    return pl.pallas_call(
        kernel,
        out_shape=[
            pltpu.VMEM((rows, pair), jnp.float32),
            pltpu.VMEM((width, pair), jnp.bfloat16),
        ],
        in_specs=[pl.BlockSpec(memory_space=pltpu.VMEM)] * (1 + count),
        out_specs=[pl.BlockSpec(memory_space=pltpu.VMEM)] * 2,
        scratch_shapes=[pltpu.VMEM((shard_width, pair), jnp.float32)],
        compiler_params=pltpu.CompilerParams(vmem_limit_bytes=16 * MIB),
        cost_estimate=adapt_cost(tokens, pair, share),
        name="adapt_begin",
    )(*[in_vmem(value) for value in (tokens, *messages)])


def adapt_end(tokens, messages, sources, length, mask, base, begun, shard_width, share):
    rows, width = base.shape
    pair = mask.shape[1]
    count = len(messages)

    def kernel(tokens_ref, mask_ref, base_ref, shrunk, widened, *refs):
        out, wide, ups = refs[count:]
        wide[...] = widened[...]
        shrink = shrunk[...]
        shrink += shrink_part(sources, length, tokens_ref, refs[:count], wide, ups)
        picked = (shrink * mask_ref[...]).astype(jnp.bfloat16)
        delta = lax.dot_general(
            picked, wide[...], (((1,), (1,)), ((), ())), preferred_element_type=jnp.float32
        )
        out[...] = (base_ref[...] + delta).astype(out.dtype)

    values = (tokens, mask, base, *begun, *messages)
    return pl.pallas_call(
        kernel,
        out_shape=jax.ShapeDtypeStruct((rows, width), jnp.bfloat16),
        in_specs=[pl.BlockSpec(memory_space=pltpu.VMEM)] * len(values),
        out_specs=pl.BlockSpec(memory_space=pltpu.VMEM),
        scratch_shapes=[
            pltpu.VMEM((width, pair), jnp.bfloat16),
            pltpu.VMEM((shard_width, pair), jnp.float32),
        ],
        compiler_params=pltpu.CompilerParams(vmem_limit_bytes=16 * MIB),
        cost_estimate=adapt_cost(tokens, pair, share),
        name="adapt_end",
    )(*[in_vmem(value) for value in values])


def after(value, *others):
    def kernel(*refs):
        pass

    return pl.pallas_call(
        kernel,
        out_shape=pltpu.VMEM(value.shape, value.dtype),
        in_specs=[pl.BlockSpec(memory_space=pl.ANY)] * (1 + len(others)),
        out_specs=pl.BlockSpec(memory_space=pl.ANY),
        input_output_aliases={0: 0},
        compiler_params=pltpu.CompilerParams(vmem_limit_bytes=MIB),
        name="after",
    )(*[in_vmem(other) for other in (value, *others)])


def bundle(pieces, others=()):
    pieces = [piece if isinstance(piece, tuple) else (piece, None, piece.shape[0]) for piece in pieces]
    count = len(pieces)
    width, dtype = pieces[0][0].shape[1], pieces[0][0].dtype

    def kernel(*refs):
        place = 0
        for ref, (_, begin, size) in zip(refs[:count], pieces):
            first = 0 if begin is None else begin()
            refs[-1][place : place + size, :] = ref[pl.ds(first, size), :]
            place += size

    values = [array for array, _, _ in pieces] + list(others)
    return pl.pallas_call(
        kernel,
        out_shape=pltpu.VMEM((sum(size for _, _, size in pieces), width), dtype),
        in_specs=[pl.BlockSpec(memory_space=pltpu.VMEM)] * len(values),
        out_specs=pl.BlockSpec(memory_space=pltpu.VMEM),
        compiler_params=pltpu.CompilerParams(vmem_limit_bytes=2 * MIB),
        name="bundle",
    )(*[in_vmem(value) for value in values])


def row_mask(lengths, slots, rows, choices, rank, others):
    requests = lengths.shape[1]

    def kernel(lengths_ref, slots_ref, *refs):
        out = refs[-1]
        group = store_index()
        position = lax.broadcasted_iota(jnp.int32, out.shape, 0)
        lane_slot = lax.broadcasted_iota(jnp.int32, out.shape, 1) // rank
        chosen = jnp.full(out.shape, slots_ref[group, 0], jnp.int32)
        begin = lengths_ref[0, 0]
        for request in range(1, requests):
            change = slots_ref[group, request] - slots_ref[group, request - 1]
            chosen += jnp.where(position >= begin, change, 0)
            begin += lengths_ref[0, request]
        out[...] = (chosen == lane_slot).astype(jnp.float32)

    return pl.pallas_call(
        kernel,
        out_shape=pltpu.VMEM((rows, choices * rank), jnp.float32),
        in_specs=[pl.BlockSpec(memory_space=pltpu.SMEM)] * 2
        + [pl.BlockSpec(memory_space=pltpu.VMEM)] * len(others),
        out_specs=pl.BlockSpec(memory_space=pltpu.VMEM),
        compiler_params=pltpu.CompilerParams(vmem_limit_bytes=2 * MIB),
        name="row_mask",
    )(lengths, slots, *[in_vmem(other) for other in others])


def row_slots(lengths, slots, rows):
    ends = jnp.cumsum(lengths)
    starts = ends - lengths
    position = jnp.arange(rows, dtype=jnp.int32)[:, None]
    member = (position >= starts[None, :]) & (position < ends[None, :])
    return jnp.sum(jnp.where(member, slots[None, :], 0), axis=1)


def swap(block, axis, bit):
    size = lax.axis_size(axis)
    return lax.ppermute(block, axis, [(i, i ^ bit) for i in range(size)])


def send_pairs(payload, target):
    size = 2 * lax.axis_size("line") * lax.axis_size("plane")
    return lax.ppermute(payload, AXES[1:], [(i, target(i)) for i in range(size)])


ROWS = {
    "Z1": ("line", 1, ["own"]),
    "Z2": ("line", 2, ["own"]),
    "Z3": ("line", 1, ["Z2"]),
    "Y0": ("plane", 1, ["own"]),
    "Y1": ("plane", 1, ["Z1"]),
    "Y2": ("plane", 1, ["Z2"]),
    "Y3": ("plane", 1, ["Z3"]),
    "X1": ("parts", 1, ["Z1", "Y0"]),
    "X2": ("parts", 1, ["Z2", "Y1"]),
    "X3": ("parts", 1, ["Z3", "Y2"]),
    "X4": ("parts", 1, ["Y3"]),
}
PLACES = {name: (int(name[1]), int(name[0] == "Y")) for name in ROWS if name[0] in "ZY"}
STEPS = (("whole", "CW", "S1", "X1"), ("C1", "S2", "X2", "S3"), ("C2", "X3", "S4"), ("C3", "X4", "C4"))


def body(
    tokens, base_weight, adapter_down, adapter_up, request_lengths, group_adapters, request_slot
):
    rank = adapter_down.shape[2]
    choices = group_adapters.shape[1]
    width = base_weight.shape[1]
    shard_width = adapter_up.shape[1]
    pair = choices * rank
    operands = (
        jnp.transpose(group_adapters),
        jnp.swapaxes(adapter_down, 1, 2),
        jnp.transpose(adapter_up, (1, 2, 0)).reshape(shard_width * rank, adapter_up.shape[0]),
        shard_width,
    )

    def early_targets():
        targets = []
        for n, mask in enumerate(EARLY):
            targets += [(n, target) for target in direct_targets(mask)]
        return targets

    def late_targets():
        core = lax.axis_index("core")
        targets = []
        for n, mask in enumerate(LATE):
            targets += [(n, target) for target in direct_targets(mask)]
        for n, masks in enumerate(ROUNDS):
            targets += [(len(LATE) + n, target) for target in round_targets(masks, core)]
        first = len(LATE) + len(ROUNDS)
        for n, rounds in enumerate(SWAPS):
            for number in rounds:
                targets += [
                    (first + n, target) for target in round_targets(ROUNDS[number], 1 - core)
                ]
        me = store_index()
        last = first + len(SWAPS)
        return targets + [(last - 1, me ^ 1), (last, me)]

    swap_counts = [2 * len(rounds) for rounds in SWAPS]
    swap_counts[-1] += 1
    late_counts = (2,) * (len(LATE) + len(ROUNDS)) + tuple(swap_counts) + (1,)
    values = {}

    def get(name):
        if name not in values:
            values[name] = make(name)
        return values[name]

    def wait(name):
        return [get(other) for other in TIES.get(name, ())]

    def early_messages():
        counts = (2,) * len(EARLY)
        messages = make_messages(*operands, counts, early_targets, 1, wait("early"))
        for mask, message in zip(EARLY, messages):
            values[f"pair{mask}"] = message

    def late_messages():
        messages = make_messages(*operands, late_counts, late_targets, COST, wait("late"))
        names = [f"pair{mask}" for mask in LATE] + [f"mine{n}" for n in range(len(ROUNDS))]
        names += [f"theirs{n}" for n in range(len(SWAPS))] + ["local"]
        values.update(zip(names, messages))

    def make(name):
        kind, number = name[0], name[1:]
        if name in ("whole", "own"):
            values["whole"], values["own"] = load_rows(base_weight)
            return values[name]
        if name in [f"pair{mask}" for mask in EARLY]:
            early_messages()
            return values[name]
        if name[:4] in ("pair", "mine", "thei", "loca"):
            late_messages()
            return values[name]
        if name in ROWS:
            axis, mask, sources = ROWS[name]
            others = wait(name)
            if kind == "X":
                payload = get("S" + number)
            elif others:
                payload = bundle([get(source) for source in sources], others)
            else:
                payload = get(sources[0])
            return swap(payload, axis, mask)
        if kind == "S":
            return bundle([get(source) for source in ROWS["X" + number][2]], wait("X" + number))
        if name == "CW":
            others = wait(name)
            return swap(bundle([get("whole")], others) if others else get("whole"), "core", 1)
        if kind == "C":
            return swap(bundle([get("S" + number), get("X" + number)], wait(name)), "core", 1)
        if kind == "T":
            return swap(after(get("theirs" + number), *wait(name)), "core", 1)
        if kind == "P":
            message = get("pair" + number)
            others = wait(name)
            payload = after(message, *others) if others else message
            return send_pairs(payload, lambda i: i ^ (2 * int(number)))
        if kind == "H":
            got, length = get("P" + number), get("local").shape[0]
            return swap(bundle([(got, lambda: length, length)], wait(name)), "core", 1)
        if kind == "R":
            masks, length = ROUNDS[int(number)], get("local").shape[0]
            group = [n for n, rounds in enumerate(SWAPS) if int(number) in rounds][0]
            begin = SWAPS[group].index(int(number)) * 2 * length
            theirs = (get(f"T{group}"), lambda: begin, 2 * length)
            payload = bundle([get("mine" + number), theirs], wait(name))
            return send_pairs(payload, lambda i: i ^ (2 * masks[i % 2]))
        if kind == "F":
            got, length = get("R" + number), get("local").shape[0]

            def place(i):
                return pl.multiple_of((2 * i + 1 - lax.axis_index("core")) * length, 16)

            parts = [(got, functools.partial(place, i), length) for i in range(2)]
            return swap(bundle(parts, wait(name)), "core", 1)
        if name == "mask":
            return row_mask(
                request_lengths, request_slot, tokens.shape[0], choices, rank, wait(name)
            )
        if name == "AB":
            every = [f"P{mask}" for mask in EARLY + LATE] + [f"R{n}" for n in range(len(ROUNDS))]
            buffers, places = arrivals([other for other in every if other not in LAST])

            def sources():
                me = store_index()
                return [(0, 0, me), (1, 2 * len(SWAPS[-1]) * length_rows, me ^ 1)] + places(2)

            shrunk, values["second factors"] = adapt_begin(
                tokens,
                (get("local"), get(f"T{len(SWAPS) - 1}"), *buffers, *wait(name)),
                sources,
                length_rows,
                pair,
                shard_width,
                width,
                0.6,
            )
            return shrunk
        if kind == "B":
            step = int(number)
            start = get(f"B{step - 1}") if step else None
            bundles = [(masks_of(part), get(part)) for part in STEPS[step]]
            return base_product(tokens, bundles, start, wait(name))
        raise KeyError(name)

    def masks_of(part):
        if part == "whole":
            return [(None, 0, 0, 0)]
        if part == "CW":
            return [(None, 0, 0, 1)]
        places = [PLACES[source] for source in ROWS["X" + part[1]][2]]
        if part[0] == "C":
            return [(x, z, y, 1) for x in range(2) for z, y in places]
        return [(int(part[0] == "X"), z, y, 0) for z, y in places]

    length_rows = base_weight.shape[0] // HALF * pair + shard_width * pair // HALF

    def pair_sources(mask, n):
        core, chip = lax.axis_index("core"), store_index() // 2
        source = (chip ^ mask) * 2
        return [(n, 0, source + core), (n + 1, 0, source + 1 - core)]

    def round_sources(masks, n):
        core, chip = lax.axis_index("core"), store_index() // 2
        own, other = jnp.where(core == 0, *masks), jnp.where(core == 0, *masks[::-1])
        places = []
        for i in range(2):
            places.append((n, (2 * i + core) * length_rows, (chip ^ own) * 2 + (core ^ i)))
            places.append((n + 1, i * length_rows, (chip ^ other) * 2 + (core ^ 1 ^ i)))
        return places

    def arrivals(names):
        buffers = []
        for name in names:
            buffers += [get(name), get(("H" if name[0] == "P" else "F") + name[1:])]

        def sources(offset=0):
            places = []
            for n, name in enumerate(names):
                if name[0] == "P":
                    places += pair_sources(int(name[1:]), offset + 2 * n)
                else:
                    places += round_sources(ROUNDS[int(name[1:])], offset + 2 * n)
            return places

        return buffers, sources

    end_buffers, end_places = arrivals(list(LAST))
    return adapt_end(
        tokens,
        tuple(end_buffers),
        end_places,
        length_rows,
        get("mask"),
        get(f"B{len(STEPS) - 1}"),
        (get("AB"), values["second factors"]),
        shard_width,
        0.4,
    )


def plain_body(
    tokens, base_weight, adapter_down, adapter_up, request_lengths, group_adapters, request_slot
):
    store = AXES[1:]
    rank = adapter_down.shape[2]
    choices = group_adapters.shape[1]
    group = lax.axis_index(store)
    wanted = jnp.transpose(group_adapters)
    slots = lax.dynamic_index_in_dim(request_slot, group, 0, keepdims=False)
    slot_of_row = row_slots(request_lengths[0], slots, tokens.shape[0])
    lane_slot = jnp.arange(choices * rank, dtype=jnp.int32)[None, :] // rank
    mask = (slot_of_row[:, None] == lane_slot).astype(jnp.float32)
    exchange = functools.partial(
        lax.all_to_all, axis_name=store, split_axis=1, concat_axis=1, tiled=True
    )
    down = exchange(jnp.take(adapter_down, wanted, axis=0))
    up = exchange(jnp.take(adapter_up, wanted, axis=0))
    weight = lax.all_gather(base_weight, store, axis=0, tiled=True)
    down = down.reshape(choices, tokens.shape[1], rank)
    up = up.reshape(choices, base_weight.shape[1], rank)
    base = jnp.dot(tokens, weight, preferred_element_type=jnp.float32)
    shrink = jnp.einsum("td,kdr->tkr", tokens, down, preferred_element_type=jnp.float32)
    picked = (shrink.reshape(mask.shape) * mask).astype(jnp.bfloat16)
    picked = picked.reshape(shrink.shape)
    delta = jnp.einsum("tkr,kvr->tv", picked, up, preferred_element_type=jnp.float32)
    return (base + delta).astype(jnp.bfloat16)


def solution(mesh):
    parts, size = mesh.shape["parts"], mesh.shape["store"]
    chips = size // 2
    plane = 1
    while 4 * plane * plane <= chips:
        plane *= 2
    lines = chips // plane
    split = Mesh(mesh.devices.reshape(parts, lines, plane, 2), AXES)
    store = AXES[1:]

    def run(tokens, base_weight, *rest):
        small = (parts, lines, plane) == (2, 4, 2) and base_weight.shape[0] // size == 2 * HALF
        return jax.shard_map(
            body if small else plain_body,
            mesh=split,
            in_specs=(
                P(AXES, None),
                P(store, None),
                P(None, store, None),
                P(None, store, None),
                P(AXES, None),
                P("parts", None),
                P("parts", None),
            ),
            out_specs=P(AXES, None),
            check_vma=False,
        )(tokens, base_weight, *rest)

    return run
```

```python
import functools

import jax
import jax.numpy as jnp
from jax import lax
from jax.experimental import pallas as pl
from jax.experimental.pallas import tpu as pltpu
from jax.sharding import Mesh
from jax.sharding import PartitionSpec as P

HALF = 256
MIB = 1024 * 1024
COST = 1
AXES = ("parts", "line", "plane", "core")


def in_vmem(value):
    return pltpu.with_memory_space_constraint(value, pltpu.VMEM)


def in_hbm(value):
    return pltpu.with_memory_space_constraint(value, pltpu.HBM)


def store_index():
    return (lax.axis_index("line") * 2 + lax.axis_index("plane")) * 2 + lax.axis_index("core")


EARLY, LATE = (), (4,)
ROUNDS = ((6, 1), (2, 7), (5, 3))
SWAPS = ((0,), (1, 2))
LAST = ("R2", "R1")
TIES = {
    "Y1": ("Y0",),
    "Y2": ("B0",),
    "X1": ("Z2", "local", "mask",),
    "X2": ("P4",),
    "X3": ("R0", "X2",),
    "X4": ("R1", "X3",),
    "C4": ("AB", "B1", "R2",),
    "B1": ("Y3",),
    "F0": ("R1",),
    "F1": ("AB", "B2",),
    "F2": ("AB", "B2",),
    "R1": ("P4", "R0",),
    "R2": ("P4",),
    "T1": ("T0",),
}


def direct_targets(mask):
    return [store_index() ^ (2 * mask + i) for i in range(2)]


def round_targets(masks, core):
    chip = store_index() // 2
    mask = jnp.where(core == 0, *masks)
    return [(chip ^ mask) * 2 + i for i in range(2)]


def send_kernel(targets_of, wanted, down, up, *refs):
    targets = targets_of()
    outs = refs[:-6]
    table, pick, even_rows, odd_rows, table_sem, sems = refs[-6:]
    choices = wanted.shape[0]
    rank = down.shape[1]
    halves = down.shape[2] // HALF
    padded = pick.shape[0] // choices
    count = even_rows.shape[0] // padded
    length = choices * halves * rank + count
    copies = []

    def begin(source, target):
        copy = pltpu.make_async_copy(source, target, sems.at[len(copies)])
        copy.start()
        copies.append(copy)

    places = []
    for out, target in targets:
        places.append((outs[out], sum(place[0] is outs[out] for place in places) * length))
        for choice in range(choices):
            adapter = wanted[choice, target]
            for part in range(halves):
                start = places[-1][1] + (part * choices + choice) * rank
                begin(
                    down.at[adapter, :, pl.ds(part * HALF, HALF)],
                    outs[out].at[pl.ds(start, rank), :],
                )
    table_copy = pltpu.make_async_copy(up, table, table_sem)
    table_copy.start()

    ids = lax.broadcasted_iota(jnp.int32, (1, up.shape[1]), 1)
    pick[...] = jnp.zeros_like(pick)
    for choice in range(choices):
        for n, (_, target) in enumerate(targets):
            here = (ids == wanted[choice, target]).astype(jnp.float32)
            pick[pl.ds(choice * padded + n, 1), :] = here
    table_copy.wait()
    rows = lax.dot_general(
        pick[...].astype(jnp.bfloat16),
        table[...],
        (((1,), (1,)), ((), ())),
        preferred_element_type=jnp.float32,
    )
    first, second = rows[:padded], rows[padded:]
    low = lax.broadcasted_iota(jnp.int32, (padded, 2 * rank), 1) < rank
    for i in range(count):
        a = first[:, 2 * rank * i : 2 * rank * (i + 1)]
        b = second[:, 2 * rank * i : 2 * rank * (i + 1)]
        even_rows[pl.ds(i, padded, stride=count), :] = jnp.where(low, a, pltpu.roll(b, rank, 1))
        odd_rows[pl.ds(i, padded, stride=count), :] = jnp.where(low, pltpu.roll(a, rank, 1), b)
    for n, (out, start) in enumerate(places):
        own = pl.ds(n * count, count)
        to = pl.ds(start + length - count, count)
        out[to, : 2 * rank] = even_rows[own, :].astype(jnp.bfloat16)
        out[to, 2 * rank :] = odd_rows[own, :].astype(jnp.bfloat16)
    for copy in copies:
        copy.wait()


def make_messages(wanted, down, up, shard_width, counts, targets_of, cost, others=()):
    choices = wanted.shape[0]
    rank, depth = down.shape[1:]
    halves = depth // HALF
    count = shard_width * choices * rank // HALF
    length = choices * rank * halves + count
    padded = -(-sum(counts) // 8) * 8

    def kernel(*refs):
        send_kernel(targets_of, *refs[:3], *refs[3 + len(others) :])

    return pl.pallas_call(
        kernel,
        out_shape=[pltpu.VMEM((n * length, HALF), jnp.bfloat16) for n in counts],
        in_specs=[pl.BlockSpec(memory_space=pltpu.SMEM)]
        + [pl.BlockSpec(memory_space=pltpu.HBM)] * 2
        + [pl.BlockSpec(memory_space=pltpu.VMEM)] * len(others),
        out_specs=[pl.BlockSpec(memory_space=pltpu.VMEM)] * len(counts),
        scratch_shapes=[
            pltpu.VMEM(up.shape, up.dtype),
            pltpu.VMEM((choices * padded, up.shape[1]), jnp.float32),
            pltpu.VMEM((padded * count, 2 * rank), jnp.float32),
            pltpu.VMEM((padded * count, 2 * rank), jnp.float32),
            pltpu.SemaphoreType.DMA,
            pltpu.SemaphoreType.DMA((sum(counts) * choices * halves,)),
        ],
        compiler_params=pltpu.CompilerParams(vmem_limit_bytes=16 * MIB),
        cost_estimate=pl.CostEstimate(
            flops=0, bytes_accessed=4 * cost * sum(counts) * length * HALF, transcendentals=0
        ),
        name="make_messages",
    )(wanted, in_hbm(down), in_hbm(up), *[in_vmem(other) for other in others])


def load_rows(weight):
    def kernel(source, whole, half, sems):
        x = lax.axis_index("parts")
        own = pltpu.make_async_copy(source.at[pl.ds(x * HALF, HALF), :], half, sems.at[0])
        rest = pltpu.make_async_copy(source, whole, sems.at[1])
        own.start()
        rest.start()
        own.wait()
        rest.wait()

    return pl.pallas_call(
        kernel,
        out_shape=[
            pltpu.VMEM(weight.shape, weight.dtype),
            pltpu.VMEM((HALF, weight.shape[1]), weight.dtype),
        ],
        in_specs=[pl.BlockSpec(memory_space=pltpu.HBM)],
        out_specs=[pl.BlockSpec(memory_space=pltpu.VMEM)] * 2,
        scratch_shapes=[pltpu.SemaphoreType.DMA((2,))],
        compiler_params=pltpu.CompilerParams(vmem_limit_bytes=2 * MIB),
        name="load_rows",
    )(in_hbm(weight))


def base_product(tokens, bundles, start=None, others=()):
    rows, depth = tokens.shape
    width = bundles[0][1].shape[1]
    count = len(bundles)
    total_rows = sum(bundle.shape[0] for _, bundle in bundles)

    def kernel(tokens_ref, *refs):
        parts, out = refs[:count], refs[-1]
        place = dict(zip(AXES, [lax.axis_index(name) for name in AXES]))
        first = True
        for (masks, _), part in zip(bundles, parts):
            left = []
            for x, z, y, core in masks:
                z, y, core = place["line"] ^ z, place["plane"] ^ y, place["core"] ^ core
                owner = (z * 2 + y) * 2 + core
                if x is None:
                    column, size = pl.multiple_of(owner * 2 * HALF, 2 * HALF), 2 * HALF
                else:
                    column = pl.multiple_of((owner * 2 + (place["parts"] ^ x)) * HALF, HALF)
                    size = HALF
                left.append(tokens_ref[:, pl.ds(column, size)])
            total = jnp.dot(
                jnp.concatenate(left, axis=1), part[...], preferred_element_type=jnp.float32
            )
            if first:
                out[...] = total if start is None else refs[count][...] + total
            else:
                out[...] += total
            first = False

    extra = ([] if start is None else [start]) + list(others)
    return pl.pallas_call(
        kernel,
        out_shape=pltpu.VMEM((rows, width), jnp.float32),
        in_specs=[pl.BlockSpec(memory_space=pltpu.VMEM)] * (1 + count + len(extra)),
        out_specs=pl.BlockSpec(memory_space=pltpu.VMEM),
        compiler_params=pltpu.CompilerParams(vmem_limit_bytes=16 * MIB),
        cost_estimate=pl.CostEstimate(
            flops=2 * rows * total_rows * width,
            bytes_accessed=2 * rows * total_rows + 2 * total_rows * width + 4 * rows * width,
            transcendentals=0,
        ),
        name="base_product",
    )(*[in_vmem(value) for value in (tokens, *[bundle for _, bundle in bundles], *extra)])


def shrink_part(sources, length, tokens, messages, wide, ups):
    pair = wide.shape[1]
    step = HALF // pair
    groups = wide.shape[0] // ups.shape[0]
    depth = tokens.shape[1] // groups
    halves = depth // HALF
    total = None
    for n, start, source in sources():
        begin = start if isinstance(start, int) else pl.multiple_of(start, 16)
        message = messages[n][pl.ds(begin, length), :]
        column = pl.multiple_of(source * depth, depth)
        down = jnp.concatenate(
            [message[half * pair : (half + 1) * pair, :] for half in range(halves)], axis=1
        )
        part = lax.dot_general(
            tokens[:, pl.ds(column, depth)],
            down,
            (((1,), (1,)), ((), ())),
            preferred_element_type=jnp.float32,
        )
        total = part if total is None else total + part
        up = message[halves * pair :, :].astype(jnp.float32)
        count = up.shape[0]
        for i in range(step):
            ups[pl.ds(i, count, stride=step), :] = up[:, i * pair : (i + 1) * pair]
        own = pl.ds(pl.multiple_of(source * count * step, count * step), count * step)
        wide[own, :] = ups[...].astype(jnp.bfloat16)
    return total


def adapt_cost(tokens, pair, share):
    return pl.CostEstimate(
        flops=int(4 * tokens.size * pair * share),
        bytes_accessed=int(2 * tokens.size * share),
        transcendentals=0,
    )


def adapt_begin(tokens, messages, sources, length, pair, shard_width, width, share):
    rows = tokens.shape[0]
    count = len(messages)

    def kernel(tokens_ref, *refs):
        shrink, wide, ups = refs[count:]
        wide[...] = jnp.zeros_like(wide)
        shrink[...] = shrink_part(sources, length, tokens_ref, refs[:count], wide, ups)

    return pl.pallas_call(
        kernel,
        out_shape=[
            pltpu.VMEM((rows, pair), jnp.float32),
            pltpu.VMEM((width, pair), jnp.bfloat16),
        ],
        in_specs=[pl.BlockSpec(memory_space=pltpu.VMEM)] * (1 + count),
        out_specs=[pl.BlockSpec(memory_space=pltpu.VMEM)] * 2,
        scratch_shapes=[pltpu.VMEM((shard_width, pair), jnp.float32)],
        compiler_params=pltpu.CompilerParams(vmem_limit_bytes=16 * MIB),
        cost_estimate=adapt_cost(tokens, pair, share),
        name="adapt_begin",
    )(*[in_vmem(value) for value in (tokens, *messages)])


def adapt_end(tokens, messages, sources, length, mask, base, begun, shard_width, share):
    rows, width = base.shape
    pair = mask.shape[1]
    count = len(messages)

    def kernel(tokens_ref, mask_ref, base_ref, shrunk, widened, *refs):
        out, wide, ups = refs[count:]
        wide[...] = widened[...]
        shrink = shrunk[...]
        shrink += shrink_part(sources, length, tokens_ref, refs[:count], wide, ups)
        picked = (shrink * mask_ref[...]).astype(jnp.bfloat16)
        delta = lax.dot_general(
            picked, wide[...], (((1,), (1,)), ((), ())), preferred_element_type=jnp.float32
        )
        out[...] = (base_ref[...] + delta).astype(out.dtype)

    values = (tokens, mask, base, *begun, *messages)
    return pl.pallas_call(
        kernel,
        out_shape=jax.ShapeDtypeStruct((rows, width), jnp.bfloat16),
        in_specs=[pl.BlockSpec(memory_space=pltpu.VMEM)] * len(values),
        out_specs=pl.BlockSpec(memory_space=pltpu.VMEM),
        scratch_shapes=[
            pltpu.VMEM((width, pair), jnp.bfloat16),
            pltpu.VMEM((shard_width, pair), jnp.float32),
        ],
        compiler_params=pltpu.CompilerParams(vmem_limit_bytes=16 * MIB),
        cost_estimate=adapt_cost(tokens, pair, share),
        name="adapt_end",
    )(*[in_vmem(value) for value in values])


def after(value, *others):
    def kernel(*refs):
        pass

    return pl.pallas_call(
        kernel,
        out_shape=pltpu.VMEM(value.shape, value.dtype),
        in_specs=[pl.BlockSpec(memory_space=pl.ANY)] * (1 + len(others)),
        out_specs=pl.BlockSpec(memory_space=pl.ANY),
        input_output_aliases={0: 0},
        compiler_params=pltpu.CompilerParams(vmem_limit_bytes=MIB),
        name="after",
    )(*[in_vmem(other) for other in (value, *others)])


def bundle(pieces, others=()):
    pieces = [piece if isinstance(piece, tuple) else (piece, None, piece.shape[0]) for piece in pieces]
    count = len(pieces)
    width, dtype = pieces[0][0].shape[1], pieces[0][0].dtype

    def kernel(*refs):
        place = 0
        for ref, (_, begin, size) in zip(refs[:count], pieces):
            first = 0 if begin is None else begin()
            refs[-1][place : place + size, :] = ref[pl.ds(first, size), :]
            place += size

    values = [array for array, _, _ in pieces] + list(others)
    return pl.pallas_call(
        kernel,
        out_shape=pltpu.VMEM((sum(size for _, _, size in pieces), width), dtype),
        in_specs=[pl.BlockSpec(memory_space=pltpu.VMEM)] * len(values),
        out_specs=pl.BlockSpec(memory_space=pltpu.VMEM),
        compiler_params=pltpu.CompilerParams(vmem_limit_bytes=2 * MIB),
        name="bundle",
    )(*[in_vmem(value) for value in values])


def row_mask(lengths, slots, rows, choices, rank, others):
    requests = lengths.shape[1]

    def kernel(lengths_ref, slots_ref, *refs):
        out = refs[-1]
        group = store_index()
        position = lax.broadcasted_iota(jnp.int32, out.shape, 0)
        lane_slot = lax.broadcasted_iota(jnp.int32, out.shape, 1) // rank
        chosen = jnp.full(out.shape, slots_ref[group, 0], jnp.int32)
        begin = lengths_ref[0, 0]
        for request in range(1, requests):
            change = slots_ref[group, request] - slots_ref[group, request - 1]
            chosen += jnp.where(position >= begin, change, 0)
            begin += lengths_ref[0, request]
        out[...] = (chosen == lane_slot).astype(jnp.float32)

    return pl.pallas_call(
        kernel,
        out_shape=pltpu.VMEM((rows, choices * rank), jnp.float32),
        in_specs=[pl.BlockSpec(memory_space=pltpu.SMEM)] * 2
        + [pl.BlockSpec(memory_space=pltpu.VMEM)] * len(others),
        out_specs=pl.BlockSpec(memory_space=pltpu.VMEM),
        compiler_params=pltpu.CompilerParams(vmem_limit_bytes=2 * MIB),
        name="row_mask",
    )(lengths, slots, *[in_vmem(other) for other in others])


def row_slots(lengths, slots, rows):
    ends = jnp.cumsum(lengths)
    starts = ends - lengths
    position = jnp.arange(rows, dtype=jnp.int32)[:, None]
    member = (position >= starts[None, :]) & (position < ends[None, :])
    return jnp.sum(jnp.where(member, slots[None, :], 0), axis=1)


def swap(block, axis, bit):
    size = lax.axis_size(axis)
    return lax.ppermute(block, axis, [(i, i ^ bit) for i in range(size)])


def send_pairs(payload, target):
    size = 2 * lax.axis_size("line") * lax.axis_size("plane")
    return lax.ppermute(payload, AXES[1:], [(i, target(i)) for i in range(size)])


ROWS = {
    "Z1": ("line", 1, ["own"]),
    "Z2": ("line", 2, ["own"]),
    "Z3": ("line", 1, ["Z2"]),
    "Y0": ("plane", 1, ["own"]),
    "Y1": ("plane", 1, ["Z1"]),
    "Y2": ("plane", 1, ["Z2"]),
    "Y3": ("plane", 1, ["Z3"]),
    "X1": ("parts", 1, ["Z1", "Y0"]),
    "X2": ("parts", 1, ["Z2", "Y1"]),
    "X3": ("parts", 1, ["Z3", "Y2"]),
    "X4": ("parts", 1, ["Y3"]),
}
PLACES = {name: (int(name[1]), int(name[0] == "Y")) for name in ROWS if name[0] in "ZY"}
STEPS = (("whole", "CW", "S1", "X1"), ("C1", "S2", "X2", "S3"), ("C2", "X3"), ("C3", "S4", "X4", "C4"))


def body(
    tokens, base_weight, adapter_down, adapter_up, request_lengths, group_adapters, request_slot
):
    rank = adapter_down.shape[2]
    choices = group_adapters.shape[1]
    width = base_weight.shape[1]
    shard_width = adapter_up.shape[1]
    pair = choices * rank
    operands = (
        jnp.transpose(group_adapters),
        jnp.swapaxes(adapter_down, 1, 2),
        jnp.transpose(adapter_up, (1, 2, 0)).reshape(shard_width * rank, adapter_up.shape[0]),
        shard_width,
    )

    def early_targets():
        targets = []
        for n, mask in enumerate(EARLY):
            targets += [(n, target) for target in direct_targets(mask)]
        return targets

    def late_targets():
        core = lax.axis_index("core")
        targets = []
        for n, mask in enumerate(LATE):
            targets += [(n, target) for target in direct_targets(mask)]
        for n, masks in enumerate(ROUNDS):
            targets += [(len(LATE) + n, target) for target in round_targets(masks, core)]
        first = len(LATE) + len(ROUNDS)
        for n, rounds in enumerate(SWAPS):
            for number in rounds:
                targets += [
                    (first + n, target) for target in round_targets(ROUNDS[number], 1 - core)
                ]
        me = store_index()
        last = first + len(SWAPS)
        return targets + [(last - 1, me ^ 1), (last, me)]

    swap_counts = [2 * len(rounds) for rounds in SWAPS]
    swap_counts[-1] += 1
    late_counts = (2,) * (len(LATE) + len(ROUNDS)) + tuple(swap_counts) + (1,)
    values = {}

    def get(name):
        if name not in values:
            values[name] = make(name)
        return values[name]

    def wait(name):
        return [get(other) for other in TIES.get(name, ())]

    def early_messages():
        counts = (2,) * len(EARLY)
        messages = make_messages(*operands, counts, early_targets, 1, wait("early"))
        for mask, message in zip(EARLY, messages):
            values[f"pair{mask}"] = message

    def late_messages():
        messages = make_messages(*operands, late_counts, late_targets, COST, wait("late"))
        names = [f"pair{mask}" for mask in LATE] + [f"mine{n}" for n in range(len(ROUNDS))]
        names += [f"theirs{n}" for n in range(len(SWAPS))] + ["local"]
        values.update(zip(names, messages))

    def make(name):
        kind, number = name[0], name[1:]
        if name in ("whole", "own"):
            values["whole"], values["own"] = load_rows(base_weight)
            return values[name]
        if name in [f"pair{mask}" for mask in EARLY]:
            early_messages()
            return values[name]
        if name[:4] in ("pair", "mine", "thei", "loca"):
            late_messages()
            return values[name]
        if name in ROWS:
            axis, mask, sources = ROWS[name]
            others = wait(name)
            if kind == "X":
                payload = get("S" + number)
            elif others:
                payload = bundle([get(source) for source in sources], others)
            else:
                payload = get(sources[0])
            return swap(payload, axis, mask)
        if kind == "S":
            return bundle([get(source) for source in ROWS["X" + number][2]], wait("X" + number))
        if name == "CW":
            others = wait(name)
            return swap(bundle([get("whole")], others) if others else get("whole"), "core", 1)
        if kind == "C":
            return swap(bundle([get("S" + number), get("X" + number)], wait(name)), "core", 1)
        if kind == "T":
            return swap(after(get("theirs" + number), *wait(name)), "core", 1)
        if kind == "P":
            message = get("pair" + number)
            others = wait(name)
            payload = after(message, *others) if others else message
            return send_pairs(payload, lambda i: i ^ (2 * int(number)))
        if kind == "H":
            got, length = get("P" + number), get("local").shape[0]
            return swap(bundle([(got, lambda: length, length)], wait(name)), "core", 1)
        if kind == "R":
            masks, length = ROUNDS[int(number)], get("local").shape[0]
            group = [n for n, rounds in enumerate(SWAPS) if int(number) in rounds][0]
            begin = SWAPS[group].index(int(number)) * 2 * length
            theirs = (get(f"T{group}"), lambda: begin, 2 * length)
            payload = bundle([get("mine" + number), theirs], wait(name))
            return send_pairs(payload, lambda i: i ^ (2 * masks[i % 2]))
        if kind == "F":
            got, length = get("R" + number), get("local").shape[0]

            def place(i):
                return pl.multiple_of((2 * i + 1 - lax.axis_index("core")) * length, 16)

            parts = [(got, functools.partial(place, i), length) for i in range(2)]
            return swap(bundle(parts, wait(name)), "core", 1)
        if name == "mask":
            return row_mask(
                request_lengths, request_slot, tokens.shape[0], choices, rank, wait(name)
            )
        if name == "AB":
            every = [f"P{mask}" for mask in EARLY + LATE] + [f"R{n}" for n in range(len(ROUNDS))]
            buffers, places = arrivals([other for other in every if other not in LAST])

            def sources():
                me = store_index()
                return [(0, 0, me), (1, 2 * len(SWAPS[-1]) * length_rows, me ^ 1)] + places(2)

            shrunk, values["second factors"] = adapt_begin(
                tokens,
                (get("local"), get(f"T{len(SWAPS) - 1}"), *buffers, *wait(name)),
                sources,
                length_rows,
                pair,
                shard_width,
                width,
                0.6,
            )
            return shrunk
        if kind == "B":
            step = int(number)
            start = get(f"B{step - 1}") if step else None
            bundles = [(masks_of(part), get(part)) for part in STEPS[step]]
            return base_product(tokens, bundles, start, wait(name))
        raise KeyError(name)

    def masks_of(part):
        if part == "whole":
            return [(None, 0, 0, 0)]
        if part == "CW":
            return [(None, 0, 0, 1)]
        places = [PLACES[source] for source in ROWS["X" + part[1]][2]]
        if part[0] == "C":
            return [(x, z, y, 1) for x in range(2) for z, y in places]
        return [(int(part[0] == "X"), z, y, 0) for z, y in places]

    length_rows = base_weight.shape[0] // HALF * pair + shard_width * pair // HALF

    def pair_sources(mask, n):
        core, chip = lax.axis_index("core"), store_index() // 2
        source = (chip ^ mask) * 2
        return [(n, 0, source + core), (n + 1, 0, source + 1 - core)]

    def round_sources(masks, n):
        core, chip = lax.axis_index("core"), store_index() // 2
        own, other = jnp.where(core == 0, *masks), jnp.where(core == 0, *masks[::-1])
        places = []
        for i in range(2):
            places.append((n, (2 * i + core) * length_rows, (chip ^ own) * 2 + (core ^ i)))
            places.append((n + 1, i * length_rows, (chip ^ other) * 2 + (core ^ 1 ^ i)))
        return places

    def arrivals(names):
        buffers = []
        for name in names:
            buffers += [get(name), get(("H" if name[0] == "P" else "F") + name[1:])]

        def sources(offset=0):
            places = []
            for n, name in enumerate(names):
                if name[0] == "P":
                    places += pair_sources(int(name[1:]), offset + 2 * n)
                else:
                    places += round_sources(ROUNDS[int(name[1:])], offset + 2 * n)
            return places

        return buffers, sources

    end_buffers, end_places = arrivals(list(LAST))
    return adapt_end(
        tokens,
        tuple(end_buffers),
        end_places,
        length_rows,
        get("mask"),
        get(f"B{len(STEPS) - 1}"),
        (get("AB"), values["second factors"]),
        shard_width,
        0.4,
    )


def plain_body(
    tokens, base_weight, adapter_down, adapter_up, request_lengths, group_adapters, request_slot
):
    store = AXES[1:]
    rank = adapter_down.shape[2]
    choices = group_adapters.shape[1]
    group = lax.axis_index(store)
    wanted = jnp.transpose(group_adapters)
    slots = lax.dynamic_index_in_dim(request_slot, group, 0, keepdims=False)
    slot_of_row = row_slots(request_lengths[0], slots, tokens.shape[0])
    lane_slot = jnp.arange(choices * rank, dtype=jnp.int32)[None, :] // rank
    mask = (slot_of_row[:, None] == lane_slot).astype(jnp.float32)
    exchange = functools.partial(
        lax.all_to_all, axis_name=store, split_axis=1, concat_axis=1, tiled=True
    )
    down = exchange(jnp.take(adapter_down, wanted, axis=0))
    up = exchange(jnp.take(adapter_up, wanted, axis=0))
    weight = lax.all_gather(base_weight, store, axis=0, tiled=True)
    down = down.reshape(choices, tokens.shape[1], rank)
    up = up.reshape(choices, base_weight.shape[1], rank)
    base = jnp.dot(tokens, weight, preferred_element_type=jnp.float32)
    shrink = jnp.einsum("td,kdr->tkr", tokens, down, preferred_element_type=jnp.float32)
    picked = (shrink.reshape(mask.shape) * mask).astype(jnp.bfloat16)
    picked = picked.reshape(shrink.shape)
    delta = jnp.einsum("tkr,kvr->tv", picked, up, preferred_element_type=jnp.float32)
    return (base + delta).astype(jnp.bfloat16)


def solution(mesh):
    parts, size = mesh.shape["parts"], mesh.shape["store"]
    chips = size // 2
    plane = 1
    while 4 * plane * plane <= chips:
        plane *= 2
    lines = chips // plane
    split = Mesh(mesh.devices.reshape(parts, lines, plane, 2), AXES)
    store = AXES[1:]

    def run(tokens, base_weight, *rest):
        small = (parts, lines, plane) == (2, 4, 2) and base_weight.shape[0] // size == 2 * HALF
        return jax.shard_map(
            body if small else plain_body,
            mesh=split,
            in_specs=(
                P(AXES, None),
                P(store, None),
                P(None, store, None),
                P(None, store, None),
                P(AXES, None),
                P("parts", None),
                P("parts", None),
            ),
            out_specs=P(AXES, None),
            check_vma=False,
        )(tokens, base_weight, *rest)

    return run
```

```python
import functools

import jax
import jax.numpy as jnp
from jax import lax
from jax.experimental import pallas as pl
from jax.experimental.pallas import tpu as pltpu
from jax.sharding import Mesh
from jax.sharding import PartitionSpec as P

HALF = 256
MIB = 1024 * 1024
COST = 1
AXES = ("parts", "line", "plane", "core")


def in_vmem(value):
    return pltpu.with_memory_space_constraint(value, pltpu.VMEM)


def in_hbm(value):
    return pltpu.with_memory_space_constraint(value, pltpu.HBM)


def store_index():
    return (lax.axis_index("line") * 2 + lax.axis_index("plane")) * 2 + lax.axis_index("core")


EARLY, LATE = (), (7,)
ROUNDS = ((1, 4), (6, 2), (3, 5))
SWAPS = ((0,), (1, 2))
LAST = ("R2", "R1")
TIES = {
    "Y1": ("Y0",),
    "Y2": ("B0",),
    "X1": ("Z2", "local", "mask",),
    "X2": ("P7",),
    "X3": ("R0", "X2",),
    "X4": ("R1", "X3",),
    "C4": ("AB", "B1", "R2",),
    "B0": ("CW", "Y1",),
    "B1": ("Y3",),
    "F0": ("R1",),
    "F1": ("AB", "B2",),
    "F2": ("AB", "B2",),
    "R1": ("P7", "R0",),
    "R2": ("P7",),
    "T1": ("T0",),
}


def direct_targets(mask):
    return [store_index() ^ (2 * mask + i) for i in range(2)]


def round_targets(masks, core):
    chip = store_index() // 2
    mask = jnp.where(core == 0, *masks)
    return [(chip ^ mask) * 2 + i for i in range(2)]


def send_kernel(targets_of, wanted, down, up, *refs):
    targets = targets_of()
    outs = refs[:-6]
    table, pick, even_rows, odd_rows, table_sem, sems = refs[-6:]
    choices = wanted.shape[0]
    rank = down.shape[1]
    halves = down.shape[2] // HALF
    padded = pick.shape[0] // choices
    count = even_rows.shape[0] // padded
    length = choices * halves * rank + count
    copies = []

    def begin(source, target):
        copy = pltpu.make_async_copy(source, target, sems.at[len(copies)])
        copy.start()
        copies.append(copy)

    places = []
    for out, target in targets:
        places.append((outs[out], sum(place[0] is outs[out] for place in places) * length))
        for choice in range(choices):
            adapter = wanted[choice, target]
            for part in range(halves):
                start = places[-1][1] + (part * choices + choice) * rank
                begin(
                    down.at[adapter, :, pl.ds(part * HALF, HALF)],
                    outs[out].at[pl.ds(start, rank), :],
                )
    table_copy = pltpu.make_async_copy(up, table, table_sem)
    table_copy.start()

    ids = lax.broadcasted_iota(jnp.int32, (1, up.shape[1]), 1)
    pick[...] = jnp.zeros_like(pick)
    for choice in range(choices):
        for n, (_, target) in enumerate(targets):
            here = (ids == wanted[choice, target]).astype(jnp.float32)
            pick[pl.ds(choice * padded + n, 1), :] = here
    table_copy.wait()
    rows = lax.dot_general(
        pick[...].astype(jnp.bfloat16),
        table[...],
        (((1,), (1,)), ((), ())),
        preferred_element_type=jnp.float32,
    )
    first, second = rows[:padded], rows[padded:]
    low = lax.broadcasted_iota(jnp.int32, (padded, 2 * rank), 1) < rank
    for i in range(count):
        a = first[:, 2 * rank * i : 2 * rank * (i + 1)]
        b = second[:, 2 * rank * i : 2 * rank * (i + 1)]
        even_rows[pl.ds(i, padded, stride=count), :] = jnp.where(low, a, pltpu.roll(b, rank, 1))
        odd_rows[pl.ds(i, padded, stride=count), :] = jnp.where(low, pltpu.roll(a, rank, 1), b)
    for n, (out, start) in enumerate(places):
        own = pl.ds(n * count, count)
        to = pl.ds(start + length - count, count)
        out[to, : 2 * rank] = even_rows[own, :].astype(jnp.bfloat16)
        out[to, 2 * rank :] = odd_rows[own, :].astype(jnp.bfloat16)
    for copy in copies:
        copy.wait()


def make_messages(wanted, down, up, shard_width, counts, targets_of, cost, others=()):
    choices = wanted.shape[0]
    rank, depth = down.shape[1:]
    halves = depth // HALF
    count = shard_width * choices * rank // HALF
    length = choices * rank * halves + count
    padded = -(-sum(counts) // 8) * 8

    def kernel(*refs):
        send_kernel(targets_of, *refs[:3], *refs[3 + len(others) :])

    return pl.pallas_call(
        kernel,
        out_shape=[pltpu.VMEM((n * length, HALF), jnp.bfloat16) for n in counts],
        in_specs=[pl.BlockSpec(memory_space=pltpu.SMEM)]
        + [pl.BlockSpec(memory_space=pltpu.HBM)] * 2
        + [pl.BlockSpec(memory_space=pltpu.VMEM)] * len(others),
        out_specs=[pl.BlockSpec(memory_space=pltpu.VMEM)] * len(counts),
        scratch_shapes=[
            pltpu.VMEM(up.shape, up.dtype),
            pltpu.VMEM((choices * padded, up.shape[1]), jnp.float32),
            pltpu.VMEM((padded * count, 2 * rank), jnp.float32),
            pltpu.VMEM((padded * count, 2 * rank), jnp.float32),
            pltpu.SemaphoreType.DMA,
            pltpu.SemaphoreType.DMA((sum(counts) * choices * halves,)),
        ],
        compiler_params=pltpu.CompilerParams(vmem_limit_bytes=16 * MIB),
        cost_estimate=pl.CostEstimate(
            flops=0, bytes_accessed=4 * cost * sum(counts) * length * HALF, transcendentals=0
        ),
        name="make_messages",
    )(wanted, in_hbm(down), in_hbm(up), *[in_vmem(other) for other in others])


def load_rows(weight):
    def kernel(source, whole, half, sems):
        x = lax.axis_index("parts")
        own = pltpu.make_async_copy(source.at[pl.ds(x * HALF, HALF), :], half, sems.at[0])
        rest = pltpu.make_async_copy(source, whole, sems.at[1])
        own.start()
        rest.start()
        own.wait()
        rest.wait()

    return pl.pallas_call(
        kernel,
        out_shape=[
            pltpu.VMEM(weight.shape, weight.dtype),
            pltpu.VMEM((HALF, weight.shape[1]), weight.dtype),
        ],
        in_specs=[pl.BlockSpec(memory_space=pltpu.HBM)],
        out_specs=[pl.BlockSpec(memory_space=pltpu.VMEM)] * 2,
        scratch_shapes=[pltpu.SemaphoreType.DMA((2,))],
        compiler_params=pltpu.CompilerParams(vmem_limit_bytes=2 * MIB),
        name="load_rows",
    )(in_hbm(weight))


def base_product(tokens, bundles, start=None, others=()):
    rows, depth = tokens.shape
    width = bundles[0][1].shape[1]
    count = len(bundles)
    total_rows = sum(bundle.shape[0] for _, bundle in bundles)

    def kernel(tokens_ref, *refs):
        parts, out = refs[:count], refs[-1]
        place = dict(zip(AXES, [lax.axis_index(name) for name in AXES]))
        first = True
        for (masks, _), part in zip(bundles, parts):
            left = []
            for x, z, y, core in masks:
                z, y, core = place["line"] ^ z, place["plane"] ^ y, place["core"] ^ core
                owner = (z * 2 + y) * 2 + core
                if x is None:
                    column, size = pl.multiple_of(owner * 2 * HALF, 2 * HALF), 2 * HALF
                else:
                    column = pl.multiple_of((owner * 2 + (place["parts"] ^ x)) * HALF, HALF)
                    size = HALF
                left.append(tokens_ref[:, pl.ds(column, size)])
            total = jnp.dot(
                jnp.concatenate(left, axis=1), part[...], preferred_element_type=jnp.float32
            )
            if first:
                out[...] = total if start is None else refs[count][...] + total
            else:
                out[...] += total
            first = False

    extra = ([] if start is None else [start]) + list(others)
    return pl.pallas_call(
        kernel,
        out_shape=pltpu.VMEM((rows, width), jnp.float32),
        in_specs=[pl.BlockSpec(memory_space=pltpu.VMEM)] * (1 + count + len(extra)),
        out_specs=pl.BlockSpec(memory_space=pltpu.VMEM),
        compiler_params=pltpu.CompilerParams(vmem_limit_bytes=16 * MIB),
        cost_estimate=pl.CostEstimate(
            flops=2 * rows * total_rows * width,
            bytes_accessed=2 * rows * total_rows + 2 * total_rows * width + 4 * rows * width,
            transcendentals=0,
        ),
        name="base_product",
    )(*[in_vmem(value) for value in (tokens, *[bundle for _, bundle in bundles], *extra)])


def shrink_part(sources, length, tokens, messages, wide, ups):
    pair = wide.shape[1]
    step = HALF // pair
    groups = wide.shape[0] // ups.shape[0]
    depth = tokens.shape[1] // groups
    halves = depth // HALF
    total = None
    for n, start, source in sources():
        begin = start if isinstance(start, int) else pl.multiple_of(start, 16)
        message = messages[n][pl.ds(begin, length), :]
        column = pl.multiple_of(source * depth, depth)
        down = jnp.concatenate(
            [message[half * pair : (half + 1) * pair, :] for half in range(halves)], axis=1
        )
        part = lax.dot_general(
            tokens[:, pl.ds(column, depth)],
            down,
            (((1,), (1,)), ((), ())),
            preferred_element_type=jnp.float32,
        )
        total = part if total is None else total + part
        up = message[halves * pair :, :].astype(jnp.float32)
        count = up.shape[0]
        for i in range(step):
            ups[pl.ds(i, count, stride=step), :] = up[:, i * pair : (i + 1) * pair]
        own = pl.ds(pl.multiple_of(source * count * step, count * step), count * step)
        wide[own, :] = ups[...].astype(jnp.bfloat16)
    return total


def adapt_cost(tokens, pair, share):
    return pl.CostEstimate(
        flops=int(4 * tokens.size * pair * share),
        bytes_accessed=int(2 * tokens.size * share),
        transcendentals=0,
    )


def adapt_begin(tokens, messages, sources, length, pair, shard_width, width, share):
    rows = tokens.shape[0]
    count = len(messages)

    def kernel(tokens_ref, *refs):
        shrink, wide, ups = refs[count:]
        wide[...] = jnp.zeros_like(wide)
        shrink[...] = shrink_part(sources, length, tokens_ref, refs[:count], wide, ups)

    return pl.pallas_call(
        kernel,
        out_shape=[
            pltpu.VMEM((rows, pair), jnp.float32),
            pltpu.VMEM((width, pair), jnp.bfloat16),
        ],
        in_specs=[pl.BlockSpec(memory_space=pltpu.VMEM)] * (1 + count),
        out_specs=[pl.BlockSpec(memory_space=pltpu.VMEM)] * 2,
        scratch_shapes=[pltpu.VMEM((shard_width, pair), jnp.float32)],
        compiler_params=pltpu.CompilerParams(vmem_limit_bytes=16 * MIB),
        cost_estimate=adapt_cost(tokens, pair, share),
        name="adapt_begin",
    )(*[in_vmem(value) for value in (tokens, *messages)])


def adapt_end(tokens, messages, sources, length, mask, base, begun, shard_width, share):
    rows, width = base.shape
    pair = mask.shape[1]
    count = len(messages)

    def kernel(tokens_ref, mask_ref, base_ref, shrunk, widened, *refs):
        out, wide, ups = refs[count:]
        wide[...] = widened[...]
        shrink = shrunk[...]
        shrink += shrink_part(sources, length, tokens_ref, refs[:count], wide, ups)
        picked = (shrink * mask_ref[...]).astype(jnp.bfloat16)
        delta = lax.dot_general(
            picked, wide[...], (((1,), (1,)), ((), ())), preferred_element_type=jnp.float32
        )
        out[...] = (base_ref[...] + delta).astype(out.dtype)

    values = (tokens, mask, base, *begun, *messages)
    return pl.pallas_call(
        kernel,
        out_shape=jax.ShapeDtypeStruct((rows, width), jnp.bfloat16),
        in_specs=[pl.BlockSpec(memory_space=pltpu.VMEM)] * len(values),
        out_specs=pl.BlockSpec(memory_space=pltpu.VMEM),
        scratch_shapes=[
            pltpu.VMEM((width, pair), jnp.bfloat16),
            pltpu.VMEM((shard_width, pair), jnp.float32),
        ],
        compiler_params=pltpu.CompilerParams(vmem_limit_bytes=16 * MIB),
        cost_estimate=adapt_cost(tokens, pair, share),
        name="adapt_end",
    )(*[in_vmem(value) for value in values])


def after(value, *others):
    def kernel(*refs):
        pass

    return pl.pallas_call(
        kernel,
        out_shape=pltpu.VMEM(value.shape, value.dtype),
        in_specs=[pl.BlockSpec(memory_space=pl.ANY)] * (1 + len(others)),
        out_specs=pl.BlockSpec(memory_space=pl.ANY),
        input_output_aliases={0: 0},
        compiler_params=pltpu.CompilerParams(vmem_limit_bytes=MIB),
        name="after",
    )(*[in_vmem(other) for other in (value, *others)])


def bundle(pieces, others=()):
    pieces = [piece if isinstance(piece, tuple) else (piece, None, piece.shape[0]) for piece in pieces]
    count = len(pieces)
    width, dtype = pieces[0][0].shape[1], pieces[0][0].dtype

    def kernel(*refs):
        place = 0
        for ref, (_, begin, size) in zip(refs[:count], pieces):
            first = 0 if begin is None else begin()
            refs[-1][place : place + size, :] = ref[pl.ds(first, size), :]
            place += size

    values = [array for array, _, _ in pieces] + list(others)
    return pl.pallas_call(
        kernel,
        out_shape=pltpu.VMEM((sum(size for _, _, size in pieces), width), dtype),
        in_specs=[pl.BlockSpec(memory_space=pltpu.VMEM)] * len(values),
        out_specs=pl.BlockSpec(memory_space=pltpu.VMEM),
        compiler_params=pltpu.CompilerParams(vmem_limit_bytes=2 * MIB),
        name="bundle",
    )(*[in_vmem(value) for value in values])


def row_mask(lengths, slots, rows, choices, rank, others):
    requests = lengths.shape[1]

    def kernel(lengths_ref, slots_ref, *refs):
        out = refs[-1]
        group = store_index()
        position = lax.broadcasted_iota(jnp.int32, out.shape, 0)
        lane_slot = lax.broadcasted_iota(jnp.int32, out.shape, 1) // rank
        chosen = jnp.full(out.shape, slots_ref[group, 0], jnp.int32)
        begin = lengths_ref[0, 0]
        for request in range(1, requests):
            change = slots_ref[group, request] - slots_ref[group, request - 1]
            chosen += jnp.where(position >= begin, change, 0)
            begin += lengths_ref[0, request]
        out[...] = (chosen == lane_slot).astype(jnp.float32)

    return pl.pallas_call(
        kernel,
        out_shape=pltpu.VMEM((rows, choices * rank), jnp.float32),
        in_specs=[pl.BlockSpec(memory_space=pltpu.SMEM)] * 2
        + [pl.BlockSpec(memory_space=pltpu.VMEM)] * len(others),
        out_specs=pl.BlockSpec(memory_space=pltpu.VMEM),
        compiler_params=pltpu.CompilerParams(vmem_limit_bytes=2 * MIB),
        name="row_mask",
    )(lengths, slots, *[in_vmem(other) for other in others])


def row_slots(lengths, slots, rows):
    ends = jnp.cumsum(lengths)
    starts = ends - lengths
    position = jnp.arange(rows, dtype=jnp.int32)[:, None]
    member = (position >= starts[None, :]) & (position < ends[None, :])
    return jnp.sum(jnp.where(member, slots[None, :], 0), axis=1)


def swap(block, axis, bit):
    size = lax.axis_size(axis)
    return lax.ppermute(block, axis, [(i, i ^ bit) for i in range(size)])


def send_pairs(payload, target):
    size = 2 * lax.axis_size("line") * lax.axis_size("plane")
    return lax.ppermute(payload, AXES[1:], [(i, target(i)) for i in range(size)])


ROWS = {
    "Z1": ("line", 1, ["own"]),
    "Z2": ("line", 2, ["own"]),
    "Z3": ("line", 1, ["Z2"]),
    "Y0": ("plane", 1, ["own"]),
    "Y1": ("plane", 1, ["Z1"]),
    "Y2": ("plane", 1, ["Z2"]),
    "Y3": ("plane", 1, ["Z3"]),
    "X1": ("parts", 1, ["Z1", "Y0"]),
    "X2": ("parts", 1, ["Z2", "Y1"]),
    "X3": ("parts", 1, ["Z3", "Y2"]),
    "X4": ("parts", 1, ["Y3"]),
}
PLACES = {name: (int(name[1]), int(name[0] == "Y")) for name in ROWS if name[0] in "ZY"}
STEPS = (("whole", "CW", "S1", "X1"), ("C1", "S2", "X2", "S3"), ("C2", "X3", "S4"), ("C3", "X4", "C4"))


def body(
    tokens, base_weight, adapter_down, adapter_up, request_lengths, group_adapters, request_slot
):
    rank = adapter_down.shape[2]
    choices = group_adapters.shape[1]
    width = base_weight.shape[1]
    shard_width = adapter_up.shape[1]
    pair = choices * rank
    operands = (
        jnp.transpose(group_adapters),
        jnp.swapaxes(adapter_down, 1, 2),
        jnp.transpose(adapter_up, (1, 2, 0)).reshape(shard_width * rank, adapter_up.shape[0]),
        shard_width,
    )

    def early_targets():
        targets = []
        for n, mask in enumerate(EARLY):
            targets += [(n, target) for target in direct_targets(mask)]
        return targets

    def late_targets():
        core = lax.axis_index("core")
        targets = []
        for n, mask in enumerate(LATE):
            targets += [(n, target) for target in direct_targets(mask)]
        for n, masks in enumerate(ROUNDS):
            targets += [(len(LATE) + n, target) for target in round_targets(masks, core)]
        first = len(LATE) + len(ROUNDS)
        for n, rounds in enumerate(SWAPS):
            for number in rounds:
                targets += [
                    (first + n, target) for target in round_targets(ROUNDS[number], 1 - core)
                ]
        me = store_index()
        last = first + len(SWAPS)
        return targets + [(last - 1, me ^ 1), (last, me)]

    swap_counts = [2 * len(rounds) for rounds in SWAPS]
    swap_counts[-1] += 1
    late_counts = (2,) * (len(LATE) + len(ROUNDS)) + tuple(swap_counts) + (1,)
    values = {}

    def get(name):
        if name not in values:
            values[name] = make(name)
        return values[name]

    def wait(name):
        return [get(other) for other in TIES.get(name, ())]

    def early_messages():
        counts = (2,) * len(EARLY)
        messages = make_messages(*operands, counts, early_targets, 1, wait("early"))
        for mask, message in zip(EARLY, messages):
            values[f"pair{mask}"] = message

    def late_messages():
        messages = make_messages(*operands, late_counts, late_targets, COST, wait("late"))
        names = [f"pair{mask}" for mask in LATE] + [f"mine{n}" for n in range(len(ROUNDS))]
        names += [f"theirs{n}" for n in range(len(SWAPS))] + ["local"]
        values.update(zip(names, messages))

    def make(name):
        kind, number = name[0], name[1:]
        if name in ("whole", "own"):
            values["whole"], values["own"] = load_rows(base_weight)
            return values[name]
        if name in [f"pair{mask}" for mask in EARLY]:
            early_messages()
            return values[name]
        if name[:4] in ("pair", "mine", "thei", "loca"):
            late_messages()
            return values[name]
        if name in ROWS:
            axis, mask, sources = ROWS[name]
            others = wait(name)
            if kind == "X":
                payload = get("S" + number)
            elif others:
                payload = bundle([get(source) for source in sources], others)
            else:
                payload = get(sources[0])
            return swap(payload, axis, mask)
        if kind == "S":
            return bundle([get(source) for source in ROWS["X" + number][2]], wait("X" + number))
        if name == "CW":
            others = wait(name)
            return swap(bundle([get("whole")], others) if others else get("whole"), "core", 1)
        if kind == "C":
            return swap(bundle([get("S" + number), get("X" + number)], wait(name)), "core", 1)
        if kind == "T":
            return swap(after(get("theirs" + number), *wait(name)), "core", 1)
        if kind == "P":
            message = get("pair" + number)
            others = wait(name)
            payload = after(message, *others) if others else message
            return send_pairs(payload, lambda i: i ^ (2 * int(number)))
        if kind == "H":
            got, length = get("P" + number), get("local").shape[0]
            return swap(bundle([(got, lambda: length, length)], wait(name)), "core", 1)
        if kind == "R":
            masks, length = ROUNDS[int(number)], get("local").shape[0]
            group = [n for n, rounds in enumerate(SWAPS) if int(number) in rounds][0]
            begin = SWAPS[group].index(int(number)) * 2 * length
            theirs = (get(f"T{group}"), lambda: begin, 2 * length)
            payload = bundle([get("mine" + number), theirs], wait(name))
            return send_pairs(payload, lambda i: i ^ (2 * masks[i % 2]))
        if kind == "F":
            got, length = get("R" + number), get("local").shape[0]

            def place(i):
                return pl.multiple_of((2 * i + 1 - lax.axis_index("core")) * length, 16)

            parts = [(got, functools.partial(place, i), length) for i in range(2)]
            return swap(bundle(parts, wait(name)), "core", 1)
        if name == "mask":
            return row_mask(
                request_lengths, request_slot, tokens.shape[0], choices, rank, wait(name)
            )
        if name == "AB":
            every = [f"P{mask}" for mask in EARLY + LATE] + [f"R{n}" for n in range(len(ROUNDS))]
            buffers, places = arrivals([other for other in every if other not in LAST])

            def sources():
                me = store_index()
                return [(0, 0, me), (1, 2 * len(SWAPS[-1]) * length_rows, me ^ 1)] + places(2)

            shrunk, values["second factors"] = adapt_begin(
                tokens,
                (get("local"), get(f"T{len(SWAPS) - 1}"), *buffers, *wait(name)),
                sources,
                length_rows,
                pair,
                shard_width,
                width,
                0.6,
            )
            return shrunk
        if kind == "B":
            step = int(number)
            start = get(f"B{step - 1}") if step else None
            bundles = [(masks_of(part), get(part)) for part in STEPS[step]]
            return base_product(tokens, bundles, start, wait(name))
        raise KeyError(name)

    def masks_of(part):
        if part == "whole":
            return [(None, 0, 0, 0)]
        if part == "CW":
            return [(None, 0, 0, 1)]
        places = [PLACES[source] for source in ROWS["X" + part[1]][2]]
        if part[0] == "C":
            return [(x, z, y, 1) for x in range(2) for z, y in places]
        return [(int(part[0] == "X"), z, y, 0) for z, y in places]

    length_rows = base_weight.shape[0] // HALF * pair + shard_width * pair // HALF

    def pair_sources(mask, n):
        core, chip = lax.axis_index("core"), store_index() // 2
        source = (chip ^ mask) * 2
        return [(n, 0, source + core), (n + 1, 0, source + 1 - core)]

    def round_sources(masks, n):
        core, chip = lax.axis_index("core"), store_index() // 2
        own, other = jnp.where(core == 0, *masks), jnp.where(core == 0, *masks[::-1])
        places = []
        for i in range(2):
            places.append((n, (2 * i + core) * length_rows, (chip ^ own) * 2 + (core ^ i)))
            places.append((n + 1, i * length_rows, (chip ^ other) * 2 + (core ^ 1 ^ i)))
        return places

    def arrivals(names):
        buffers = []
        for name in names:
            buffers += [get(name), get(("H" if name[0] == "P" else "F") + name[1:])]

        def sources(offset=0):
            places = []
            for n, name in enumerate(names):
                if name[0] == "P":
                    places += pair_sources(int(name[1:]), offset + 2 * n)
                else:
                    places += round_sources(ROUNDS[int(name[1:])], offset + 2 * n)
            return places

        return buffers, sources

    end_buffers, end_places = arrivals(list(LAST))
    return adapt_end(
        tokens,
        tuple(end_buffers),
        end_places,
        length_rows,
        get("mask"),
        get(f"B{len(STEPS) - 1}"),
        (get("AB"), values["second factors"]),
        shard_width,
        0.4,
    )


def plain_body(
    tokens, base_weight, adapter_down, adapter_up, request_lengths, group_adapters, request_slot
):
    store = AXES[1:]
    rank = adapter_down.shape[2]
    choices = group_adapters.shape[1]
    group = lax.axis_index(store)
    wanted = jnp.transpose(group_adapters)
    slots = lax.dynamic_index_in_dim(request_slot, group, 0, keepdims=False)
    slot_of_row = row_slots(request_lengths[0], slots, tokens.shape[0])
    lane_slot = jnp.arange(choices * rank, dtype=jnp.int32)[None, :] // rank
    mask = (slot_of_row[:, None] == lane_slot).astype(jnp.float32)
    exchange = functools.partial(
        lax.all_to_all, axis_name=store, split_axis=1, concat_axis=1, tiled=True
    )
    down = exchange(jnp.take(adapter_down, wanted, axis=0))
    up = exchange(jnp.take(adapter_up, wanted, axis=0))
    weight = lax.all_gather(base_weight, store, axis=0, tiled=True)
    down = down.reshape(choices, tokens.shape[1], rank)
    up = up.reshape(choices, base_weight.shape[1], rank)
    base = jnp.dot(tokens, weight, preferred_element_type=jnp.float32)
    shrink = jnp.einsum("td,kdr->tkr", tokens, down, preferred_element_type=jnp.float32)
    picked = (shrink.reshape(mask.shape) * mask).astype(jnp.bfloat16)
    picked = picked.reshape(shrink.shape)
    delta = jnp.einsum("tkr,kvr->tv", picked, up, preferred_element_type=jnp.float32)
    return (base + delta).astype(jnp.bfloat16)


def solution(mesh):
    parts, size = mesh.shape["parts"], mesh.shape["store"]
    chips = size // 2
    plane = 1
    while 4 * plane * plane <= chips:
        plane *= 2
    lines = chips // plane
    split = Mesh(mesh.devices.reshape(parts, lines, plane, 2), AXES)
    store = AXES[1:]

    def run(tokens, base_weight, *rest):
        small = (parts, lines, plane) == (2, 4, 2) and base_weight.shape[0] // size == 2 * HALF
        return jax.shard_map(
            body if small else plain_body,
            mesh=split,
            in_specs=(
                P(AXES, None),
                P(store, None),
                P(None, store, None),
                P(None, store, None),
                P(AXES, None),
                P("parts", None),
                P("parts", None),
            ),
            out_specs=P(AXES, None),
            check_vma=False,
        )(tokens, base_weight, *rest)

    return run
```

```python
import functools

import jax
import jax.numpy as jnp
from jax import lax
from jax.experimental import pallas as pl
from jax.experimental.pallas import tpu as pltpu
from jax.sharding import Mesh
from jax.sharding import PartitionSpec as P

HALF = 256
MIB = 1024 * 1024
COST = 1
AXES = ("parts", "line", "plane", "core")


def in_vmem(value):
    return pltpu.with_memory_space_constraint(value, pltpu.VMEM)


def in_hbm(value):
    return pltpu.with_memory_space_constraint(value, pltpu.HBM)


def store_index():
    return (lax.axis_index("line") * 2 + lax.axis_index("plane")) * 2 + lax.axis_index("core")


EARLY, LATE = (), (7,)
ROUNDS = ((1, 4), (6, 2), (3, 5))
SWAPS = ((0,), (1, 2))
LAST = ("R2", "R1")
TIES = {
    "Y1": ("Y0", "Z2",),
    "Y2": ("B0",),
    "X1": ("Z2", "local", "mask",),
    "X2": ("P7",),
    "X3": ("R0", "X2",),
    "X4": ("R1", "X3",),
    "C4": ("AB", "B1", "R2",),
    "B0": ("CW", "Y1",),
    "B1": ("Y3",),
    "P7": ("Z2",),
    "F0": ("R1",),
    "F1": ("AB", "B2",),
    "F2": ("AB", "B2",),
    "R1": ("P7", "R0",),
    "R2": ("P7",),
    "T1": ("T0",),
}


def direct_targets(mask):
    return [store_index() ^ (2 * mask + i) for i in range(2)]


def round_targets(masks, core):
    chip = store_index() // 2
    mask = jnp.where(core == 0, *masks)
    return [(chip ^ mask) * 2 + i for i in range(2)]


def send_kernel(targets_of, wanted, down, up, *refs):
    targets = targets_of()
    outs = refs[:-6]
    table, pick, even_rows, odd_rows, table_sem, sems = refs[-6:]
    choices = wanted.shape[0]
    rank = down.shape[1]
    halves = down.shape[2] // HALF
    padded = pick.shape[0] // choices
    count = even_rows.shape[0] // padded
    length = choices * halves * rank + count
    copies = []

    def begin(source, target):
        copy = pltpu.make_async_copy(source, target, sems.at[len(copies)])
        copy.start()
        copies.append(copy)

    places = []
    for out, target in targets:
        places.append((outs[out], sum(place[0] is outs[out] for place in places) * length))
        for choice in range(choices):
            adapter = wanted[choice, target]
            for part in range(halves):
                start = places[-1][1] + (part * choices + choice) * rank
                begin(
                    down.at[adapter, :, pl.ds(part * HALF, HALF)],
                    outs[out].at[pl.ds(start, rank), :],
                )
    table_copy = pltpu.make_async_copy(up, table, table_sem)
    table_copy.start()

    ids = lax.broadcasted_iota(jnp.int32, (1, up.shape[1]), 1)
    pick[...] = jnp.zeros_like(pick)
    for choice in range(choices):
        for n, (_, target) in enumerate(targets):
            here = (ids == wanted[choice, target]).astype(jnp.float32)
            pick[pl.ds(choice * padded + n, 1), :] = here
    table_copy.wait()
    rows = lax.dot_general(
        pick[...].astype(jnp.bfloat16),
        table[...],
        (((1,), (1,)), ((), ())),
        preferred_element_type=jnp.float32,
    )
    first, second = rows[:padded], rows[padded:]
    low = lax.broadcasted_iota(jnp.int32, (padded, 2 * rank), 1) < rank
    for i in range(count):
        a = first[:, 2 * rank * i : 2 * rank * (i + 1)]
        b = second[:, 2 * rank * i : 2 * rank * (i + 1)]
        even_rows[pl.ds(i, padded, stride=count), :] = jnp.where(low, a, pltpu.roll(b, rank, 1))
        odd_rows[pl.ds(i, padded, stride=count), :] = jnp.where(low, pltpu.roll(a, rank, 1), b)
    for n, (out, start) in enumerate(places):
        own = pl.ds(n * count, count)
        to = pl.ds(start + length - count, count)
        out[to, : 2 * rank] = even_rows[own, :].astype(jnp.bfloat16)
        out[to, 2 * rank :] = odd_rows[own, :].astype(jnp.bfloat16)
    for copy in copies:
        copy.wait()


def make_messages(wanted, down, up, shard_width, counts, targets_of, cost, others=()):
    choices = wanted.shape[0]
    rank, depth = down.shape[1:]
    halves = depth // HALF
    count = shard_width * choices * rank // HALF
    length = choices * rank * halves + count
    padded = -(-sum(counts) // 8) * 8

    def kernel(*refs):
        send_kernel(targets_of, *refs[:3], *refs[3 + len(others) :])

    return pl.pallas_call(
        kernel,
        out_shape=[pltpu.VMEM((n * length, HALF), jnp.bfloat16) for n in counts],
        in_specs=[pl.BlockSpec(memory_space=pltpu.SMEM)]
        + [pl.BlockSpec(memory_space=pltpu.HBM)] * 2
        + [pl.BlockSpec(memory_space=pltpu.VMEM)] * len(others),
        out_specs=[pl.BlockSpec(memory_space=pltpu.VMEM)] * len(counts),
        scratch_shapes=[
            pltpu.VMEM(up.shape, up.dtype),
            pltpu.VMEM((choices * padded, up.shape[1]), jnp.float32),
            pltpu.VMEM((padded * count, 2 * rank), jnp.float32),
            pltpu.VMEM((padded * count, 2 * rank), jnp.float32),
            pltpu.SemaphoreType.DMA,
            pltpu.SemaphoreType.DMA((sum(counts) * choices * halves,)),
        ],
        compiler_params=pltpu.CompilerParams(vmem_limit_bytes=16 * MIB),
        cost_estimate=pl.CostEstimate(
            flops=0, bytes_accessed=4 * cost * sum(counts) * length * HALF, transcendentals=0
        ),
        name="make_messages",
    )(wanted, in_hbm(down), in_hbm(up), *[in_vmem(other) for other in others])


def load_rows(weight):
    def kernel(source, whole, half, sems):
        x = lax.axis_index("parts")
        own = pltpu.make_async_copy(source.at[pl.ds(x * HALF, HALF), :], half, sems.at[0])
        rest = pltpu.make_async_copy(source, whole, sems.at[1])
        own.start()
        rest.start()
        own.wait()
        rest.wait()

    return pl.pallas_call(
        kernel,
        out_shape=[
            pltpu.VMEM(weight.shape, weight.dtype),
            pltpu.VMEM((HALF, weight.shape[1]), weight.dtype),
        ],
        in_specs=[pl.BlockSpec(memory_space=pltpu.HBM)],
        out_specs=[pl.BlockSpec(memory_space=pltpu.VMEM)] * 2,
        scratch_shapes=[pltpu.SemaphoreType.DMA((2,))],
        compiler_params=pltpu.CompilerParams(vmem_limit_bytes=2 * MIB),
        name="load_rows",
    )(in_hbm(weight))


def base_product(tokens, bundles, start=None, others=()):
    rows, depth = tokens.shape
    width = bundles[0][1].shape[1]
    count = len(bundles)
    total_rows = sum(bundle.shape[0] for _, bundle in bundles)

    def kernel(tokens_ref, *refs):
        parts, out = refs[:count], refs[-1]
        place = dict(zip(AXES, [lax.axis_index(name) for name in AXES]))
        first = True
        for (masks, _), part in zip(bundles, parts):
            left = []
            for x, z, y, core in masks:
                z, y, core = place["line"] ^ z, place["plane"] ^ y, place["core"] ^ core
                owner = (z * 2 + y) * 2 + core
                if x is None:
                    column, size = pl.multiple_of(owner * 2 * HALF, 2 * HALF), 2 * HALF
                else:
                    column = pl.multiple_of((owner * 2 + (place["parts"] ^ x)) * HALF, HALF)
                    size = HALF
                left.append(tokens_ref[:, pl.ds(column, size)])
            total = jnp.dot(
                jnp.concatenate(left, axis=1), part[...], preferred_element_type=jnp.float32
            )
            if first:
                out[...] = total if start is None else refs[count][...] + total
            else:
                out[...] += total
            first = False

    extra = ([] if start is None else [start]) + list(others)
    return pl.pallas_call(
        kernel,
        out_shape=pltpu.VMEM((rows, width), jnp.float32),
        in_specs=[pl.BlockSpec(memory_space=pltpu.VMEM)] * (1 + count + len(extra)),
        out_specs=pl.BlockSpec(memory_space=pltpu.VMEM),
        compiler_params=pltpu.CompilerParams(vmem_limit_bytes=16 * MIB),
        cost_estimate=pl.CostEstimate(
            flops=2 * rows * total_rows * width,
            bytes_accessed=2 * rows * total_rows + 2 * total_rows * width + 4 * rows * width,
            transcendentals=0,
        ),
        name="base_product",
    )(*[in_vmem(value) for value in (tokens, *[bundle for _, bundle in bundles], *extra)])


def shrink_part(sources, length, tokens, messages, wide, ups):
    pair = wide.shape[1]
    step = HALF // pair
    groups = wide.shape[0] // ups.shape[0]
    depth = tokens.shape[1] // groups
    halves = depth // HALF
    total = None
    for n, start, source in sources():
        begin = start if isinstance(start, int) else pl.multiple_of(start, 16)
        message = messages[n][pl.ds(begin, length), :]
        column = pl.multiple_of(source * depth, depth)
        down = jnp.concatenate(
            [message[half * pair : (half + 1) * pair, :] for half in range(halves)], axis=1
        )
        part = lax.dot_general(
            tokens[:, pl.ds(column, depth)],
            down,
            (((1,), (1,)), ((), ())),
            preferred_element_type=jnp.float32,
        )
        total = part if total is None else total + part
        up = message[halves * pair :, :].astype(jnp.float32)
        count = up.shape[0]
        for i in range(step):
            ups[pl.ds(i, count, stride=step), :] = up[:, i * pair : (i + 1) * pair]
        own = pl.ds(pl.multiple_of(source * count * step, count * step), count * step)
        wide[own, :] = ups[...].astype(jnp.bfloat16)
    return total


def adapt_cost(tokens, pair, share):
    return pl.CostEstimate(
        flops=int(4 * tokens.size * pair * share),
        bytes_accessed=int(2 * tokens.size * share),
        transcendentals=0,
    )


def adapt_begin(tokens, messages, sources, length, pair, shard_width, width, share):
    rows = tokens.shape[0]
    count = len(messages)

    def kernel(tokens_ref, *refs):
        shrink, wide, ups = refs[count:]
        wide[...] = jnp.zeros_like(wide)
        shrink[...] = shrink_part(sources, length, tokens_ref, refs[:count], wide, ups)

    return pl.pallas_call(
        kernel,
        out_shape=[
            pltpu.VMEM((rows, pair), jnp.float32),
            pltpu.VMEM((width, pair), jnp.bfloat16),
        ],
        in_specs=[pl.BlockSpec(memory_space=pltpu.VMEM)] * (1 + count),
        out_specs=[pl.BlockSpec(memory_space=pltpu.VMEM)] * 2,
        scratch_shapes=[pltpu.VMEM((shard_width, pair), jnp.float32)],
        compiler_params=pltpu.CompilerParams(vmem_limit_bytes=16 * MIB),
        cost_estimate=adapt_cost(tokens, pair, share),
        name="adapt_begin",
    )(*[in_vmem(value) for value in (tokens, *messages)])


def adapt_end(tokens, messages, sources, length, mask, base, begun, shard_width, share):
    rows, width = base.shape
    pair = mask.shape[1]
    count = len(messages)

    def kernel(tokens_ref, mask_ref, base_ref, shrunk, widened, *refs):
        out, wide, ups = refs[count:]
        wide[...] = widened[...]
        shrink = shrunk[...]
        shrink += shrink_part(sources, length, tokens_ref, refs[:count], wide, ups)
        picked = (shrink * mask_ref[...]).astype(jnp.bfloat16)
        delta = lax.dot_general(
            picked, wide[...], (((1,), (1,)), ((), ())), preferred_element_type=jnp.float32
        )
        out[...] = (base_ref[...] + delta).astype(out.dtype)

    values = (tokens, mask, base, *begun, *messages)
    return pl.pallas_call(
        kernel,
        out_shape=jax.ShapeDtypeStruct((rows, width), jnp.bfloat16),
        in_specs=[pl.BlockSpec(memory_space=pltpu.VMEM)] * len(values),
        out_specs=pl.BlockSpec(memory_space=pltpu.VMEM),
        scratch_shapes=[
            pltpu.VMEM((width, pair), jnp.bfloat16),
            pltpu.VMEM((shard_width, pair), jnp.float32),
        ],
        compiler_params=pltpu.CompilerParams(vmem_limit_bytes=16 * MIB),
        cost_estimate=adapt_cost(tokens, pair, share),
        name="adapt_end",
    )(*[in_vmem(value) for value in values])


def after(value, *others):
    def kernel(*refs):
        pass

    return pl.pallas_call(
        kernel,
        out_shape=pltpu.VMEM(value.shape, value.dtype),
        in_specs=[pl.BlockSpec(memory_space=pl.ANY)] * (1 + len(others)),
        out_specs=pl.BlockSpec(memory_space=pl.ANY),
        input_output_aliases={0: 0},
        compiler_params=pltpu.CompilerParams(vmem_limit_bytes=MIB),
        name="after",
    )(*[in_vmem(other) for other in (value, *others)])


def bundle(pieces, others=()):
    pieces = [piece if isinstance(piece, tuple) else (piece, None, piece.shape[0]) for piece in pieces]
    count = len(pieces)
    width, dtype = pieces[0][0].shape[1], pieces[0][0].dtype

    def kernel(*refs):
        place = 0
        for ref, (_, begin, size) in zip(refs[:count], pieces):
            first = 0 if begin is None else begin()
            refs[-1][place : place + size, :] = ref[pl.ds(first, size), :]
            place += size

    values = [array for array, _, _ in pieces] + list(others)
    return pl.pallas_call(
        kernel,
        out_shape=pltpu.VMEM((sum(size for _, _, size in pieces), width), dtype),
        in_specs=[pl.BlockSpec(memory_space=pltpu.VMEM)] * len(values),
        out_specs=pl.BlockSpec(memory_space=pltpu.VMEM),
        compiler_params=pltpu.CompilerParams(vmem_limit_bytes=2 * MIB),
        name="bundle",
    )(*[in_vmem(value) for value in values])


def row_mask(lengths, slots, rows, choices, rank, others):
    requests = lengths.shape[1]

    def kernel(lengths_ref, slots_ref, *refs):
        out = refs[-1]
        group = store_index()
        position = lax.broadcasted_iota(jnp.int32, out.shape, 0)
        lane_slot = lax.broadcasted_iota(jnp.int32, out.shape, 1) // rank
        chosen = jnp.full(out.shape, slots_ref[group, 0], jnp.int32)
        begin = lengths_ref[0, 0]
        for request in range(1, requests):
            change = slots_ref[group, request] - slots_ref[group, request - 1]
            chosen += jnp.where(position >= begin, change, 0)
            begin += lengths_ref[0, request]
        out[...] = (chosen == lane_slot).astype(jnp.float32)

    return pl.pallas_call(
        kernel,
        out_shape=pltpu.VMEM((rows, choices * rank), jnp.float32),
        in_specs=[pl.BlockSpec(memory_space=pltpu.SMEM)] * 2
        + [pl.BlockSpec(memory_space=pltpu.VMEM)] * len(others),
        out_specs=pl.BlockSpec(memory_space=pltpu.VMEM),
        compiler_params=pltpu.CompilerParams(vmem_limit_bytes=2 * MIB),
        name="row_mask",
    )(lengths, slots, *[in_vmem(other) for other in others])


def row_slots(lengths, slots, rows):
    ends = jnp.cumsum(lengths)
    starts = ends - lengths
    position = jnp.arange(rows, dtype=jnp.int32)[:, None]
    member = (position >= starts[None, :]) & (position < ends[None, :])
    return jnp.sum(jnp.where(member, slots[None, :], 0), axis=1)


def swap(block, axis, bit):
    size = lax.axis_size(axis)
    return lax.ppermute(block, axis, [(i, i ^ bit) for i in range(size)])


def send_pairs(payload, target):
    size = 2 * lax.axis_size("line") * lax.axis_size("plane")
    return lax.ppermute(payload, AXES[1:], [(i, target(i)) for i in range(size)])


ROWS = {
    "Z1": ("line", 1, ["own"]),
    "Z2": ("line", 2, ["own"]),
    "Z3": ("line", 1, ["Z2"]),
    "Y0": ("plane", 1, ["own"]),
    "Y1": ("plane", 1, ["Z1"]),
    "Y2": ("plane", 1, ["Z2"]),
    "Y3": ("plane", 1, ["Z3"]),
    "X1": ("parts", 1, ["Z1", "Y0"]),
    "X2": ("parts", 1, ["Z2", "Y1"]),
    "X3": ("parts", 1, ["Z3", "Y2"]),
    "X4": ("parts", 1, ["Y3"]),
}
PLACES = {name: (int(name[1]), int(name[0] == "Y")) for name in ROWS if name[0] in "ZY"}
STEPS = (("whole", "CW", "S1", "X1"), ("C1", "S2", "X2", "S3"), ("C2", "X3", "S4"), ("C3", "X4", "C4"))


def body(
    tokens, base_weight, adapter_down, adapter_up, request_lengths, group_adapters, request_slot
):
    rank = adapter_down.shape[2]
    choices = group_adapters.shape[1]
    width = base_weight.shape[1]
    shard_width = adapter_up.shape[1]
    pair = choices * rank
    operands = (
        jnp.transpose(group_adapters),
        jnp.swapaxes(adapter_down, 1, 2),
        jnp.transpose(adapter_up, (1, 2, 0)).reshape(shard_width * rank, adapter_up.shape[0]),
        shard_width,
    )

    def early_targets():
        targets = []
        for n, mask in enumerate(EARLY):
            targets += [(n, target) for target in direct_targets(mask)]
        return targets

    def late_targets():
        core = lax.axis_index("core")
        targets = []
        for n, mask in enumerate(LATE):
            targets += [(n, target) for target in direct_targets(mask)]
        for n, masks in enumerate(ROUNDS):
            targets += [(len(LATE) + n, target) for target in round_targets(masks, core)]
        first = len(LATE) + len(ROUNDS)
        for n, rounds in enumerate(SWAPS):
            for number in rounds:
                targets += [
                    (first + n, target) for target in round_targets(ROUNDS[number], 1 - core)
                ]
        me = store_index()
        last = first + len(SWAPS)
        return targets + [(last - 1, me ^ 1), (last, me)]

    swap_counts = [2 * len(rounds) for rounds in SWAPS]
    swap_counts[-1] += 1
    late_counts = (2,) * (len(LATE) + len(ROUNDS)) + tuple(swap_counts) + (1,)
    values = {}

    def get(name):
        if name not in values:
            values[name] = make(name)
        return values[name]

    def wait(name):
        return [get(other) for other in TIES.get(name, ())]

    def early_messages():
        counts = (2,) * len(EARLY)
        messages = make_messages(*operands, counts, early_targets, 1, wait("early"))
        for mask, message in zip(EARLY, messages):
            values[f"pair{mask}"] = message

    def late_messages():
        messages = make_messages(*operands, late_counts, late_targets, COST, wait("late"))
        names = [f"pair{mask}" for mask in LATE] + [f"mine{n}" for n in range(len(ROUNDS))]
        names += [f"theirs{n}" for n in range(len(SWAPS))] + ["local"]
        values.update(zip(names, messages))

    def make(name):
        kind, number = name[0], name[1:]
        if name in ("whole", "own"):
            values["whole"], values["own"] = load_rows(base_weight)
            return values[name]
        if name in [f"pair{mask}" for mask in EARLY]:
            early_messages()
            return values[name]
        if name[:4] in ("pair", "mine", "thei", "loca"):
            late_messages()
            return values[name]
        if name in ROWS:
            axis, mask, sources = ROWS[name]
            others = wait(name)
            if kind == "X":
                payload = get("S" + number)
            elif others:
                payload = bundle([get(source) for source in sources], others)
            else:
                payload = get(sources[0])
            return swap(payload, axis, mask)
        if kind == "S":
            return bundle([get(source) for source in ROWS["X" + number][2]], wait("X" + number))
        if name == "CW":
            others = wait(name)
            return swap(bundle([get("whole")], others) if others else get("whole"), "core", 1)
        if kind == "C":
            return swap(bundle([get("S" + number), get("X" + number)], wait(name)), "core", 1)
        if kind == "T":
            return swap(after(get("theirs" + number), *wait(name)), "core", 1)
        if kind == "P":
            message = get("pair" + number)
            others = wait(name)
            payload = after(message, *others) if others else message
            return send_pairs(payload, lambda i: i ^ (2 * int(number)))
        if kind == "H":
            got, length = get("P" + number), get("local").shape[0]
            return swap(bundle([(got, lambda: length, length)], wait(name)), "core", 1)
        if kind == "R":
            masks, length = ROUNDS[int(number)], get("local").shape[0]
            group = [n for n, rounds in enumerate(SWAPS) if int(number) in rounds][0]
            begin = SWAPS[group].index(int(number)) * 2 * length
            theirs = (get(f"T{group}"), lambda: begin, 2 * length)
            payload = bundle([get("mine" + number), theirs], wait(name))
            return send_pairs(payload, lambda i: i ^ (2 * masks[i % 2]))
        if kind == "F":
            got, length = get("R" + number), get("local").shape[0]

            def place(i):
                return pl.multiple_of((2 * i + 1 - lax.axis_index("core")) * length, 16)

            parts = [(got, functools.partial(place, i), length) for i in range(2)]
            return swap(bundle(parts, wait(name)), "core", 1)
        if name == "mask":
            return row_mask(
                request_lengths, request_slot, tokens.shape[0], choices, rank, wait(name)
            )
        if name == "AB":
            every = [f"P{mask}" for mask in EARLY + LATE] + [f"R{n}" for n in range(len(ROUNDS))]
            buffers, places = arrivals([other for other in every if other not in LAST])

            def sources():
                me = store_index()
                return [(0, 0, me), (1, 2 * len(SWAPS[-1]) * length_rows, me ^ 1)] + places(2)

            shrunk, values["second factors"] = adapt_begin(
                tokens,
                (get("local"), get(f"T{len(SWAPS) - 1}"), *buffers, *wait(name)),
                sources,
                length_rows,
                pair,
                shard_width,
                width,
                0.6,
            )
            return shrunk
        if kind == "B":
            step = int(number)
            start = get(f"B{step - 1}") if step else None
            bundles = [(masks_of(part), get(part)) for part in STEPS[step]]
            return base_product(tokens, bundles, start, wait(name))
        raise KeyError(name)

    def masks_of(part):
        if part == "whole":
            return [(None, 0, 0, 0)]
        if part == "CW":
            return [(None, 0, 0, 1)]
        places = [PLACES[source] for source in ROWS["X" + part[1]][2]]
        if part[0] == "C":
            return [(x, z, y, 1) for x in range(2) for z, y in places]
        return [(int(part[0] == "X"), z, y, 0) for z, y in places]

    length_rows = base_weight.shape[0] // HALF * pair + shard_width * pair // HALF

    def pair_sources(mask, n):
        core, chip = lax.axis_index("core"), store_index() // 2
        source = (chip ^ mask) * 2
        return [(n, 0, source + core), (n + 1, 0, source + 1 - core)]

    def round_sources(masks, n):
        core, chip = lax.axis_index("core"), store_index() // 2
        own, other = jnp.where(core == 0, *masks), jnp.where(core == 0, *masks[::-1])
        places = []
        for i in range(2):
            places.append((n, (2 * i + core) * length_rows, (chip ^ own) * 2 + (core ^ i)))
            places.append((n + 1, i * length_rows, (chip ^ other) * 2 + (core ^ 1 ^ i)))
        return places

    def arrivals(names):
        buffers = []
        for name in names:
            buffers += [get(name), get(("H" if name[0] == "P" else "F") + name[1:])]

        def sources(offset=0):
            places = []
            for n, name in enumerate(names):
                if name[0] == "P":
                    places += pair_sources(int(name[1:]), offset + 2 * n)
                else:
                    places += round_sources(ROUNDS[int(name[1:])], offset + 2 * n)
            return places

        return buffers, sources

    end_buffers, end_places = arrivals(list(LAST))
    return adapt_end(
        tokens,
        tuple(end_buffers),
        end_places,
        length_rows,
        get("mask"),
        get(f"B{len(STEPS) - 1}"),
        (get("AB"), values["second factors"]),
        shard_width,
        0.4,
    )


def plain_body(
    tokens, base_weight, adapter_down, adapter_up, request_lengths, group_adapters, request_slot
):
    store = AXES[1:]
    rank = adapter_down.shape[2]
    choices = group_adapters.shape[1]
    group = lax.axis_index(store)
    wanted = jnp.transpose(group_adapters)
    slots = lax.dynamic_index_in_dim(request_slot, group, 0, keepdims=False)
    slot_of_row = row_slots(request_lengths[0], slots, tokens.shape[0])
    lane_slot = jnp.arange(choices * rank, dtype=jnp.int32)[None, :] // rank
    mask = (slot_of_row[:, None] == lane_slot).astype(jnp.float32)
    exchange = functools.partial(
        lax.all_to_all, axis_name=store, split_axis=1, concat_axis=1, tiled=True
    )
    down = exchange(jnp.take(adapter_down, wanted, axis=0))
    up = exchange(jnp.take(adapter_up, wanted, axis=0))
    weight = lax.all_gather(base_weight, store, axis=0, tiled=True)
    down = down.reshape(choices, tokens.shape[1], rank)
    up = up.reshape(choices, base_weight.shape[1], rank)
    base = jnp.dot(tokens, weight, preferred_element_type=jnp.float32)
    shrink = jnp.einsum("td,kdr->tkr", tokens, down, preferred_element_type=jnp.float32)
    picked = (shrink.reshape(mask.shape) * mask).astype(jnp.bfloat16)
    picked = picked.reshape(shrink.shape)
    delta = jnp.einsum("tkr,kvr->tv", picked, up, preferred_element_type=jnp.float32)
    return (base + delta).astype(jnp.bfloat16)


def solution(mesh):
    parts, size = mesh.shape["parts"], mesh.shape["store"]
    chips = size // 2
    plane = 1
    while 4 * plane * plane <= chips:
        plane *= 2
    lines = chips // plane
    split = Mesh(mesh.devices.reshape(parts, lines, plane, 2), AXES)
    store = AXES[1:]

    def run(tokens, base_weight, *rest):
        small = (parts, lines, plane) == (2, 4, 2) and base_weight.shape[0] // size == 2 * HALF
        return jax.shard_map(
            body if small else plain_body,
            mesh=split,
            in_specs=(
                P(AXES, None),
                P(store, None),
                P(None, store, None),
                P(None, store, None),
                P(AXES, None),
                P("parts", None),
                P("parts", None),
            ),
            out_specs=P(AXES, None),
            check_vma=False,
        )(tokens, base_weight, *rest)

    return run
```

```python
import functools

import jax
import jax.numpy as jnp
from jax import lax
from jax.experimental import pallas as pl
from jax.experimental.pallas import tpu as pltpu
from jax.sharding import Mesh
from jax.sharding import PartitionSpec as P

HALF = 256
MIB = 1024 * 1024
COST = 1
AXES = ("parts", "line", "plane", "core")


def in_vmem(value):
    return pltpu.with_memory_space_constraint(value, pltpu.VMEM)


def in_hbm(value):
    return pltpu.with_memory_space_constraint(value, pltpu.HBM)


def store_index():
    return (lax.axis_index("line") * 2 + lax.axis_index("plane")) * 2 + lax.axis_index("core")


EARLY, LATE = (), (7,)
ROUNDS = ((1, 4), (6, 2), (3, 5))
SWAPS = ((0,), (1, 2))
LAST = ("R2", "R1")
TIES = {
    "Y1": ("Y0", "Z2",),
    "Y2": ("B0",),
    "X1": ("Z2", "local", "mask",),
    "X2": ("P7",),
    "X3": ("R0", "X2",),
    "X4": ("R1", "X3",),
    "C4": ("AB", "B1", "R2",),
    "B0": ("CW", "Y1",),
    "B1": ("Y3",),
    "P7": ("Z2",),
    "F0": ("R1",),
    "F1": ("AB", "B2",),
    "F2": ("AB", "B2",),
    "R1": ("P7", "R0",),
    "R2": ("P7",),
    "T1": ("T0",),
    "R0": ("P7",),
}


def direct_targets(mask):
    return [store_index() ^ (2 * mask + i) for i in range(2)]


def round_targets(masks, core):
    chip = store_index() // 2
    mask = jnp.where(core == 0, *masks)
    return [(chip ^ mask) * 2 + i for i in range(2)]


def send_kernel(targets_of, wanted, down, up, *refs):
    targets = targets_of()
    outs = refs[:-6]
    table, pick, even_rows, odd_rows, table_sem, sems = refs[-6:]
    choices = wanted.shape[0]
    rank = down.shape[1]
    halves = down.shape[2] // HALF
    padded = pick.shape[0] // choices
    count = even_rows.shape[0] // padded
    length = choices * halves * rank + count
    copies = []

    def begin(source, target):
        copy = pltpu.make_async_copy(source, target, sems.at[len(copies)])
        copy.start()
        copies.append(copy)

    places = []
    for out, target in targets:
        places.append((outs[out], sum(place[0] is outs[out] for place in places) * length))
        for choice in range(choices):
            adapter = wanted[choice, target]
            for part in range(halves):
                start = places[-1][1] + (part * choices + choice) * rank
                begin(
                    down.at[adapter, :, pl.ds(part * HALF, HALF)],
                    outs[out].at[pl.ds(start, rank), :],
                )
    table_copy = pltpu.make_async_copy(up, table, table_sem)
    table_copy.start()

    ids = lax.broadcasted_iota(jnp.int32, (1, up.shape[1]), 1)
    pick[...] = jnp.zeros_like(pick)
    for choice in range(choices):
        for n, (_, target) in enumerate(targets):
            here = (ids == wanted[choice, target]).astype(jnp.float32)
            pick[pl.ds(choice * padded + n, 1), :] = here
    table_copy.wait()
    rows = lax.dot_general(
        pick[...].astype(jnp.bfloat16),
        table[...],
        (((1,), (1,)), ((), ())),
        preferred_element_type=jnp.float32,
    )
    first, second = rows[:padded], rows[padded:]
    low = lax.broadcasted_iota(jnp.int32, (padded, 2 * rank), 1) < rank
    for i in range(count):
        a = first[:, 2 * rank * i : 2 * rank * (i + 1)]
        b = second[:, 2 * rank * i : 2 * rank * (i + 1)]
        even_rows[pl.ds(i, padded, stride=count), :] = jnp.where(low, a, pltpu.roll(b, rank, 1))
        odd_rows[pl.ds(i, padded, stride=count), :] = jnp.where(low, pltpu.roll(a, rank, 1), b)
    for n, (out, start) in enumerate(places):
        own = pl.ds(n * count, count)
        to = pl.ds(start + length - count, count)
        out[to, : 2 * rank] = even_rows[own, :].astype(jnp.bfloat16)
        out[to, 2 * rank :] = odd_rows[own, :].astype(jnp.bfloat16)
    for copy in copies:
        copy.wait()


def make_messages(wanted, down, up, shard_width, counts, targets_of, cost, others=()):
    choices = wanted.shape[0]
    rank, depth = down.shape[1:]
    halves = depth // HALF
    count = shard_width * choices * rank // HALF
    length = choices * rank * halves + count
    padded = -(-sum(counts) // 8) * 8

    def kernel(*refs):
        send_kernel(targets_of, *refs[:3], *refs[3 + len(others) :])

    return pl.pallas_call(
        kernel,
        out_shape=[pltpu.VMEM((n * length, HALF), jnp.bfloat16) for n in counts],
        in_specs=[pl.BlockSpec(memory_space=pltpu.SMEM)]
        + [pl.BlockSpec(memory_space=pltpu.HBM)] * 2
        + [pl.BlockSpec(memory_space=pltpu.VMEM)] * len(others),
        out_specs=[pl.BlockSpec(memory_space=pltpu.VMEM)] * len(counts),
        scratch_shapes=[
            pltpu.VMEM(up.shape, up.dtype),
            pltpu.VMEM((choices * padded, up.shape[1]), jnp.float32),
            pltpu.VMEM((padded * count, 2 * rank), jnp.float32),
            pltpu.VMEM((padded * count, 2 * rank), jnp.float32),
            pltpu.SemaphoreType.DMA,
            pltpu.SemaphoreType.DMA((sum(counts) * choices * halves,)),
        ],
        compiler_params=pltpu.CompilerParams(vmem_limit_bytes=16 * MIB),
        cost_estimate=pl.CostEstimate(
            flops=0, bytes_accessed=4 * cost * sum(counts) * length * HALF, transcendentals=0
        ),
        name="make_messages",
    )(wanted, in_hbm(down), in_hbm(up), *[in_vmem(other) for other in others])


def load_rows(weight):
    def kernel(source, whole, half, sems):
        x = lax.axis_index("parts")
        own = pltpu.make_async_copy(source.at[pl.ds(x * HALF, HALF), :], half, sems.at[0])
        rest = pltpu.make_async_copy(source, whole, sems.at[1])
        own.start()
        rest.start()
        own.wait()
        rest.wait()

    return pl.pallas_call(
        kernel,
        out_shape=[
            pltpu.VMEM(weight.shape, weight.dtype),
            pltpu.VMEM((HALF, weight.shape[1]), weight.dtype),
        ],
        in_specs=[pl.BlockSpec(memory_space=pltpu.HBM)],
        out_specs=[pl.BlockSpec(memory_space=pltpu.VMEM)] * 2,
        scratch_shapes=[pltpu.SemaphoreType.DMA((2,))],
        compiler_params=pltpu.CompilerParams(vmem_limit_bytes=2 * MIB),
        name="load_rows",
    )(in_hbm(weight))


def base_product(tokens, bundles, start=None, others=()):
    rows, depth = tokens.shape
    width = bundles[0][1].shape[1]
    count = len(bundles)
    total_rows = sum(bundle.shape[0] for _, bundle in bundles)

    def kernel(tokens_ref, *refs):
        parts, out = refs[:count], refs[-1]
        place = dict(zip(AXES, [lax.axis_index(name) for name in AXES]))
        first = True
        for (masks, _), part in zip(bundles, parts):
            left = []
            for x, z, y, core in masks:
                z, y, core = place["line"] ^ z, place["plane"] ^ y, place["core"] ^ core
                owner = (z * 2 + y) * 2 + core
                if x is None:
                    column, size = pl.multiple_of(owner * 2 * HALF, 2 * HALF), 2 * HALF
                else:
                    column = pl.multiple_of((owner * 2 + (place["parts"] ^ x)) * HALF, HALF)
                    size = HALF
                left.append(tokens_ref[:, pl.ds(column, size)])
            total = jnp.dot(
                jnp.concatenate(left, axis=1), part[...], preferred_element_type=jnp.float32
            )
            if first:
                out[...] = total if start is None else refs[count][...] + total
            else:
                out[...] += total
            first = False

    extra = ([] if start is None else [start]) + list(others)
    return pl.pallas_call(
        kernel,
        out_shape=pltpu.VMEM((rows, width), jnp.float32),
        in_specs=[pl.BlockSpec(memory_space=pltpu.VMEM)] * (1 + count + len(extra)),
        out_specs=pl.BlockSpec(memory_space=pltpu.VMEM),
        compiler_params=pltpu.CompilerParams(vmem_limit_bytes=16 * MIB),
        cost_estimate=pl.CostEstimate(
            flops=2 * rows * total_rows * width,
            bytes_accessed=2 * rows * total_rows + 2 * total_rows * width + 4 * rows * width,
            transcendentals=0,
        ),
        name="base_product",
    )(*[in_vmem(value) for value in (tokens, *[bundle for _, bundle in bundles], *extra)])


def shrink_part(sources, length, tokens, messages, wide, ups):
    pair = wide.shape[1]
    step = HALF // pair
    groups = wide.shape[0] // ups.shape[0]
    depth = tokens.shape[1] // groups
    halves = depth // HALF
    total = None
    for n, start, source in sources():
        begin = start if isinstance(start, int) else pl.multiple_of(start, 16)
        message = messages[n][pl.ds(begin, length), :]
        column = pl.multiple_of(source * depth, depth)
        down = jnp.concatenate(
            [message[half * pair : (half + 1) * pair, :] for half in range(halves)], axis=1
        )
        part = lax.dot_general(
            tokens[:, pl.ds(column, depth)],
            down,
            (((1,), (1,)), ((), ())),
            preferred_element_type=jnp.float32,
        )
        total = part if total is None else total + part
        up = message[halves * pair :, :].astype(jnp.float32)
        count = up.shape[0]
        for i in range(step):
            ups[pl.ds(i, count, stride=step), :] = up[:, i * pair : (i + 1) * pair]
        own = pl.ds(pl.multiple_of(source * count * step, count * step), count * step)
        wide[own, :] = ups[...].astype(jnp.bfloat16)
    return total


def adapt_cost(tokens, pair, share):
    return pl.CostEstimate(
        flops=int(4 * tokens.size * pair * share),
        bytes_accessed=int(2 * tokens.size * share),
        transcendentals=0,
    )


def adapt_begin(tokens, messages, sources, length, pair, shard_width, width, share):
    rows = tokens.shape[0]
    count = len(messages)

    def kernel(tokens_ref, *refs):
        shrink, wide, ups = refs[count:]
        wide[...] = jnp.zeros_like(wide)
        shrink[...] = shrink_part(sources, length, tokens_ref, refs[:count], wide, ups)

    return pl.pallas_call(
        kernel,
        out_shape=[
            pltpu.VMEM((rows, pair), jnp.float32),
            pltpu.VMEM((width, pair), jnp.bfloat16),
        ],
        in_specs=[pl.BlockSpec(memory_space=pltpu.VMEM)] * (1 + count),
        out_specs=[pl.BlockSpec(memory_space=pltpu.VMEM)] * 2,
        scratch_shapes=[pltpu.VMEM((shard_width, pair), jnp.float32)],
        compiler_params=pltpu.CompilerParams(vmem_limit_bytes=16 * MIB),
        cost_estimate=adapt_cost(tokens, pair, share),
        name="adapt_begin",
    )(*[in_vmem(value) for value in (tokens, *messages)])


def adapt_end(tokens, messages, sources, length, mask, base, begun, shard_width, share):
    rows, width = base.shape
    pair = mask.shape[1]
    count = len(messages)

    def kernel(tokens_ref, mask_ref, base_ref, shrunk, widened, *refs):
        out, wide, ups = refs[count:]
        wide[...] = widened[...]
        shrink = shrunk[...]
        shrink += shrink_part(sources, length, tokens_ref, refs[:count], wide, ups)
        picked = (shrink * mask_ref[...]).astype(jnp.bfloat16)
        delta = lax.dot_general(
            picked, wide[...], (((1,), (1,)), ((), ())), preferred_element_type=jnp.float32
        )
        out[...] = (base_ref[...] + delta).astype(out.dtype)

    values = (tokens, mask, base, *begun, *messages)
    return pl.pallas_call(
        kernel,
        out_shape=jax.ShapeDtypeStruct((rows, width), jnp.bfloat16),
        in_specs=[pl.BlockSpec(memory_space=pltpu.VMEM)] * len(values),
        out_specs=pl.BlockSpec(memory_space=pltpu.VMEM),
        scratch_shapes=[
            pltpu.VMEM((width, pair), jnp.bfloat16),
            pltpu.VMEM((shard_width, pair), jnp.float32),
        ],
        compiler_params=pltpu.CompilerParams(vmem_limit_bytes=16 * MIB),
        cost_estimate=adapt_cost(tokens, pair, share),
        name="adapt_end",
    )(*[in_vmem(value) for value in values])


def after(value, *others):
    def kernel(*refs):
        pass

    return pl.pallas_call(
        kernel,
        out_shape=pltpu.VMEM(value.shape, value.dtype),
        in_specs=[pl.BlockSpec(memory_space=pl.ANY)] * (1 + len(others)),
        out_specs=pl.BlockSpec(memory_space=pl.ANY),
        input_output_aliases={0: 0},
        compiler_params=pltpu.CompilerParams(vmem_limit_bytes=MIB),
        name="after",
    )(*[in_vmem(other) for other in (value, *others)])


def bundle(pieces, others=()):
    pieces = [piece if isinstance(piece, tuple) else (piece, None, piece.shape[0]) for piece in pieces]
    count = len(pieces)
    width, dtype = pieces[0][0].shape[1], pieces[0][0].dtype

    def kernel(*refs):
        place = 0
        for ref, (_, begin, size) in zip(refs[:count], pieces):
            first = 0 if begin is None else begin()
            refs[-1][place : place + size, :] = ref[pl.ds(first, size), :]
            place += size

    values = [array for array, _, _ in pieces] + list(others)
    return pl.pallas_call(
        kernel,
        out_shape=pltpu.VMEM((sum(size for _, _, size in pieces), width), dtype),
        in_specs=[pl.BlockSpec(memory_space=pltpu.VMEM)] * len(values),
        out_specs=pl.BlockSpec(memory_space=pltpu.VMEM),
        compiler_params=pltpu.CompilerParams(vmem_limit_bytes=2 * MIB),
        name="bundle",
    )(*[in_vmem(value) for value in values])


def row_mask(lengths, slots, rows, choices, rank, others):
    requests = lengths.shape[1]

    def kernel(lengths_ref, slots_ref, *refs):
        out = refs[-1]
        group = store_index()
        position = lax.broadcasted_iota(jnp.int32, out.shape, 0)
        lane_slot = lax.broadcasted_iota(jnp.int32, out.shape, 1) // rank
        chosen = jnp.full(out.shape, slots_ref[group, 0], jnp.int32)
        begin = lengths_ref[0, 0]
        for request in range(1, requests):
            change = slots_ref[group, request] - slots_ref[group, request - 1]
            chosen += jnp.where(position >= begin, change, 0)
            begin += lengths_ref[0, request]
        out[...] = (chosen == lane_slot).astype(jnp.float32)

    return pl.pallas_call(
        kernel,
        out_shape=pltpu.VMEM((rows, choices * rank), jnp.float32),
        in_specs=[pl.BlockSpec(memory_space=pltpu.SMEM)] * 2
        + [pl.BlockSpec(memory_space=pltpu.VMEM)] * len(others),
        out_specs=pl.BlockSpec(memory_space=pltpu.VMEM),
        compiler_params=pltpu.CompilerParams(vmem_limit_bytes=2 * MIB),
        name="row_mask",
    )(lengths, slots, *[in_vmem(other) for other in others])


def row_slots(lengths, slots, rows):
    ends = jnp.cumsum(lengths)
    starts = ends - lengths
    position = jnp.arange(rows, dtype=jnp.int32)[:, None]
    member = (position >= starts[None, :]) & (position < ends[None, :])
    return jnp.sum(jnp.where(member, slots[None, :], 0), axis=1)


def swap(block, axis, bit):
    size = lax.axis_size(axis)
    return lax.ppermute(block, axis, [(i, i ^ bit) for i in range(size)])


def send_pairs(payload, target):
    size = 2 * lax.axis_size("line") * lax.axis_size("plane")
    return lax.ppermute(payload, AXES[1:], [(i, target(i)) for i in range(size)])


ROWS = {
    "Z1": ("line", 1, ["own"]),
    "Z2": ("line", 2, ["own"]),
    "Z3": ("line", 1, ["Z2"]),
    "Y0": ("plane", 1, ["own"]),
    "Y1": ("plane", 1, ["Z1"]),
    "Y2": ("plane", 1, ["Z2"]),
    "Y3": ("plane", 1, ["Z3"]),
    "X1": ("parts", 1, ["Z1", "Y0"]),
    "X2": ("parts", 1, ["Z2", "Y1"]),
    "X3": ("parts", 1, ["Z3", "Y2"]),
    "X4": ("parts", 1, ["Y3"]),
}
PLACES = {name: (int(name[1]), int(name[0] == "Y")) for name in ROWS if name[0] in "ZY"}
STEPS = (("whole", "CW", "S1", "X1"), ("C1", "S2", "X2", "S3"), ("C2", "X3", "S4"), ("C3", "X4", "C4"))


def body(
    tokens, base_weight, adapter_down, adapter_up, request_lengths, group_adapters, request_slot
):
    rank = adapter_down.shape[2]
    choices = group_adapters.shape[1]
    width = base_weight.shape[1]
    shard_width = adapter_up.shape[1]
    pair = choices * rank
    operands = (
        jnp.transpose(group_adapters),
        jnp.swapaxes(adapter_down, 1, 2),
        jnp.transpose(adapter_up, (1, 2, 0)).reshape(shard_width * rank, adapter_up.shape[0]),
        shard_width,
    )

    def early_targets():
        targets = []
        for n, mask in enumerate(EARLY):
            targets += [(n, target) for target in direct_targets(mask)]
        return targets

    def late_targets():
        core = lax.axis_index("core")
        targets = []
        for n, mask in enumerate(LATE):
            targets += [(n, target) for target in direct_targets(mask)]
        for n, masks in enumerate(ROUNDS):
            targets += [(len(LATE) + n, target) for target in round_targets(masks, core)]
        first = len(LATE) + len(ROUNDS)
        for n, rounds in enumerate(SWAPS):
            for number in rounds:
                targets += [
                    (first + n, target) for target in round_targets(ROUNDS[number], 1 - core)
                ]
        me = store_index()
        last = first + len(SWAPS)
        return targets + [(last - 1, me ^ 1), (last, me)]

    swap_counts = [2 * len(rounds) for rounds in SWAPS]
    swap_counts[-1] += 1
    late_counts = (2,) * (len(LATE) + len(ROUNDS)) + tuple(swap_counts) + (1,)
    values = {}

    def get(name):
        if name not in values:
            values[name] = make(name)
        return values[name]

    def wait(name):
        return [get(other) for other in TIES.get(name, ())]

    def early_messages():
        counts = (2,) * len(EARLY)
        messages = make_messages(*operands, counts, early_targets, 1, wait("early"))
        for mask, message in zip(EARLY, messages):
            values[f"pair{mask}"] = message

    def late_messages():
        messages = make_messages(*operands, late_counts, late_targets, COST, wait("late"))
        names = [f"pair{mask}" for mask in LATE] + [f"mine{n}" for n in range(len(ROUNDS))]
        names += [f"theirs{n}" for n in range(len(SWAPS))] + ["local"]
        values.update(zip(names, messages))

    def make(name):
        kind, number = name[0], name[1:]
        if name in ("whole", "own"):
            values["whole"], values["own"] = load_rows(base_weight)
            return values[name]
        if name in [f"pair{mask}" for mask in EARLY]:
            early_messages()
            return values[name]
        if name[:4] in ("pair", "mine", "thei", "loca"):
            late_messages()
            return values[name]
        if name in ROWS:
            axis, mask, sources = ROWS[name]
            others = wait(name)
            if kind == "X":
                payload = get("S" + number)
            elif others:
                payload = bundle([get(source) for source in sources], others)
            else:
                payload = get(sources[0])
            return swap(payload, axis, mask)
        if kind == "S":
            return bundle([get(source) for source in ROWS["X" + number][2]], wait("X" + number))
        if name == "CW":
            others = wait(name)
            return swap(bundle([get("whole")], others) if others else get("whole"), "core", 1)
        if kind == "C":
            return swap(bundle([get("S" + number), get("X" + number)], wait(name)), "core", 1)
        if kind == "T":
            return swap(after(get("theirs" + number), *wait(name)), "core", 1)
        if kind == "P":
            message = get("pair" + number)
            others = wait(name)
            payload = after(message, *others) if others else message
            return send_pairs(payload, lambda i: i ^ (2 * int(number)))
        if kind == "H":
            got, length = get("P" + number), get("local").shape[0]
            return swap(bundle([(got, lambda: length, length)], wait(name)), "core", 1)
        if kind == "R":
            masks, length = ROUNDS[int(number)], get("local").shape[0]
            group = [n for n, rounds in enumerate(SWAPS) if int(number) in rounds][0]
            begin = SWAPS[group].index(int(number)) * 2 * length
            theirs = (get(f"T{group}"), lambda: begin, 2 * length)
            payload = bundle([get("mine" + number), theirs], wait(name))
            return send_pairs(payload, lambda i: i ^ (2 * masks[i % 2]))
        if kind == "F":
            got, length = get("R" + number), get("local").shape[0]

            def place(i):
                return pl.multiple_of((2 * i + 1 - lax.axis_index("core")) * length, 16)

            parts = [(got, functools.partial(place, i), length) for i in range(2)]
            return swap(bundle(parts, wait(name)), "core", 1)
        if name == "mask":
            return row_mask(
                request_lengths, request_slot, tokens.shape[0], choices, rank, wait(name)
            )
        if name == "AB":
            every = [f"P{mask}" for mask in EARLY + LATE] + [f"R{n}" for n in range(len(ROUNDS))]
            buffers, places = arrivals([other for other in every if other not in LAST])

            def sources():
                me = store_index()
                return [(0, 0, me), (1, 2 * len(SWAPS[-1]) * length_rows, me ^ 1)] + places(2)

            shrunk, values["second factors"] = adapt_begin(
                tokens,
                (get("local"), get(f"T{len(SWAPS) - 1}"), *buffers, *wait(name)),
                sources,
                length_rows,
                pair,
                shard_width,
                width,
                0.6,
            )
            return shrunk
        if kind == "B":
            step = int(number)
            start = get(f"B{step - 1}") if step else None
            bundles = [(masks_of(part), get(part)) for part in STEPS[step]]
            return base_product(tokens, bundles, start, wait(name))
        raise KeyError(name)

    def masks_of(part):
        if part == "whole":
            return [(None, 0, 0, 0)]
        if part == "CW":
            return [(None, 0, 0, 1)]
        places = [PLACES[source] for source in ROWS["X" + part[1]][2]]
        if part[0] == "C":
            return [(x, z, y, 1) for x in range(2) for z, y in places]
        return [(int(part[0] == "X"), z, y, 0) for z, y in places]

    length_rows = base_weight.shape[0] // HALF * pair + shard_width * pair // HALF

    def pair_sources(mask, n):
        core, chip = lax.axis_index("core"), store_index() // 2
        source = (chip ^ mask) * 2
        return [(n, 0, source + core), (n + 1, 0, source + 1 - core)]

    def round_sources(masks, n):
        core, chip = lax.axis_index("core"), store_index() // 2
        own, other = jnp.where(core == 0, *masks), jnp.where(core == 0, *masks[::-1])
        places = []
        for i in range(2):
            places.append((n, (2 * i + core) * length_rows, (chip ^ own) * 2 + (core ^ i)))
            places.append((n + 1, i * length_rows, (chip ^ other) * 2 + (core ^ 1 ^ i)))
        return places

    def arrivals(names):
        buffers = []
        for name in names:
            buffers += [get(name), get(("H" if name[0] == "P" else "F") + name[1:])]

        def sources(offset=0):
            places = []
            for n, name in enumerate(names):
                if name[0] == "P":
                    places += pair_sources(int(name[1:]), offset + 2 * n)
                else:
                    places += round_sources(ROUNDS[int(name[1:])], offset + 2 * n)
            return places

        return buffers, sources

    end_buffers, end_places = arrivals(list(LAST))
    return adapt_end(
        tokens,
        tuple(end_buffers),
        end_places,
        length_rows,
        get("mask"),
        get(f"B{len(STEPS) - 1}"),
        (get("AB"), values["second factors"]),
        shard_width,
        0.4,
    )


def plain_body(
    tokens, base_weight, adapter_down, adapter_up, request_lengths, group_adapters, request_slot
):
    store = AXES[1:]
    rank = adapter_down.shape[2]
    choices = group_adapters.shape[1]
    group = lax.axis_index(store)
    wanted = jnp.transpose(group_adapters)
    slots = lax.dynamic_index_in_dim(request_slot, group, 0, keepdims=False)
    slot_of_row = row_slots(request_lengths[0], slots, tokens.shape[0])
    lane_slot = jnp.arange(choices * rank, dtype=jnp.int32)[None, :] // rank
    mask = (slot_of_row[:, None] == lane_slot).astype(jnp.float32)
    exchange = functools.partial(
        lax.all_to_all, axis_name=store, split_axis=1, concat_axis=1, tiled=True
    )
    down = exchange(jnp.take(adapter_down, wanted, axis=0))
    up = exchange(jnp.take(adapter_up, wanted, axis=0))
    weight = lax.all_gather(base_weight, store, axis=0, tiled=True)
    down = down.reshape(choices, tokens.shape[1], rank)
    up = up.reshape(choices, base_weight.shape[1], rank)
    base = jnp.dot(tokens, weight, preferred_element_type=jnp.float32)
    shrink = jnp.einsum("td,kdr->tkr", tokens, down, preferred_element_type=jnp.float32)
    picked = (shrink.reshape(mask.shape) * mask).astype(jnp.bfloat16)
    picked = picked.reshape(shrink.shape)
    delta = jnp.einsum("tkr,kvr->tv", picked, up, preferred_element_type=jnp.float32)
    return (base + delta).astype(jnp.bfloat16)


def solution(mesh):
    parts, size = mesh.shape["parts"], mesh.shape["store"]
    chips = size // 2
    plane = 1
    while 4 * plane * plane <= chips:
        plane *= 2
    lines = chips // plane
    split = Mesh(mesh.devices.reshape(parts, lines, plane, 2), AXES)
    store = AXES[1:]

    def run(tokens, base_weight, *rest):
        small = (parts, lines, plane) == (2, 4, 2) and base_weight.shape[0] // size == 2 * HALF
        return jax.shard_map(
            body if small else plain_body,
            mesh=split,
            in_specs=(
                P(AXES, None),
                P(store, None),
                P(None, store, None),
                P(None, store, None),
                P(AXES, None),
                P("parts", None),
                P("parts", None),
            ),
            out_specs=P(AXES, None),
            check_vma=False,
        )(tokens, base_weight, *rest)

    return run
```

```python
import functools

import jax
import jax.numpy as jnp
from jax import lax
from jax.experimental import pallas as pl
from jax.experimental.pallas import tpu as pltpu
from jax.sharding import Mesh
from jax.sharding import PartitionSpec as P

HALF = 256
MIB = 1024 * 1024
COST = 1
AXES = ("parts", "line", "plane", "core")


def in_vmem(value):
    return pltpu.with_memory_space_constraint(value, pltpu.VMEM)


def in_hbm(value):
    return pltpu.with_memory_space_constraint(value, pltpu.HBM)


def store_index():
    return (lax.axis_index("line") * 2 + lax.axis_index("plane")) * 2 + lax.axis_index("core")


EARLY, LATE = (), (7,)
ROUNDS = ((1, 4), (6, 2), (3, 5))
SWAPS = ((0,), (1, 2))
LAST = ("R2", "R1")
TIES = {
    "Y1": ("Y0",),
    "Y2": ("B0",),
    "X1": ("Z2", "local", "mask",),
    "X2": ("P7",),
    "X3": ("R0", "X2",),
    "X4": ("R1", "X3",),
    "C4": ("AB", "B1", "R2",),
    "B0": ("CW", "Y1",),
    "B1": ("Y3",),
    "F0": ("R1",),
    "R1": ("P7", "R0",),
    "R2": ("P7",),
    "T1": ("T0",),
}


def direct_targets(mask):
    return [store_index() ^ (2 * mask + i) for i in range(2)]


def round_targets(masks, core):
    chip = store_index() // 2
    mask = jnp.where(core == 0, *masks)
    return [(chip ^ mask) * 2 + i for i in range(2)]


def send_kernel(targets_of, wanted, down, up, *refs):
    targets = targets_of()
    outs = refs[:-6]
    table, pick, even_rows, odd_rows, table_sem, sems = refs[-6:]
    choices = wanted.shape[0]
    rank = down.shape[1]
    halves = down.shape[2] // HALF
    padded = pick.shape[0] // choices
    count = even_rows.shape[0] // padded
    length = choices * halves * rank + count
    copies = []

    def begin(source, target):
        copy = pltpu.make_async_copy(source, target, sems.at[len(copies)])
        copy.start()
        copies.append(copy)

    places = []
    for out, target in targets:
        places.append((outs[out], sum(place[0] is outs[out] for place in places) * length))
        for choice in range(choices):
            adapter = wanted[choice, target]
            for part in range(halves):
                start = places[-1][1] + (part * choices + choice) * rank
                begin(
                    down.at[adapter, :, pl.ds(part * HALF, HALF)],
                    outs[out].at[pl.ds(start, rank), :],
                )
    table_copy = pltpu.make_async_copy(up, table, table_sem)
    table_copy.start()

    ids = lax.broadcasted_iota(jnp.int32, (1, up.shape[1]), 1)
    pick[...] = jnp.zeros_like(pick)
    for choice in range(choices):
        for n, (_, target) in enumerate(targets):
            here = (ids == wanted[choice, target]).astype(jnp.float32)
            pick[pl.ds(choice * padded + n, 1), :] = here
    table_copy.wait()
    rows = lax.dot_general(
        pick[...].astype(jnp.bfloat16),
        table[...],
        (((1,), (1,)), ((), ())),
        preferred_element_type=jnp.float32,
    )
    first, second = rows[:padded], rows[padded:]
    low = lax.broadcasted_iota(jnp.int32, (padded, 2 * rank), 1) < rank
    for i in range(count):
        a = first[:, 2 * rank * i : 2 * rank * (i + 1)]
        b = second[:, 2 * rank * i : 2 * rank * (i + 1)]
        even_rows[pl.ds(i, padded, stride=count), :] = jnp.where(low, a, pltpu.roll(b, rank, 1))
        odd_rows[pl.ds(i, padded, stride=count), :] = jnp.where(low, pltpu.roll(a, rank, 1), b)
    for n, (out, start) in enumerate(places):
        own = pl.ds(n * count, count)
        to = pl.ds(start + length - count, count)
        out[to, : 2 * rank] = even_rows[own, :].astype(jnp.bfloat16)
        out[to, 2 * rank :] = odd_rows[own, :].astype(jnp.bfloat16)
    for copy in copies:
        copy.wait()


def make_messages(wanted, down, up, shard_width, counts, targets_of, cost, others=()):
    choices = wanted.shape[0]
    rank, depth = down.shape[1:]
    halves = depth // HALF
    count = shard_width * choices * rank // HALF
    length = choices * rank * halves + count
    padded = -(-sum(counts) // 8) * 8

    def kernel(*refs):
        send_kernel(targets_of, *refs[:3], *refs[3 + len(others) :])

    return pl.pallas_call(
        kernel,
        out_shape=[pltpu.VMEM((n * length, HALF), jnp.bfloat16) for n in counts],
        in_specs=[pl.BlockSpec(memory_space=pltpu.SMEM)]
        + [pl.BlockSpec(memory_space=pltpu.HBM)] * 2
        + [pl.BlockSpec(memory_space=pltpu.VMEM)] * len(others),
        out_specs=[pl.BlockSpec(memory_space=pltpu.VMEM)] * len(counts),
        scratch_shapes=[
            pltpu.VMEM(up.shape, up.dtype),
            pltpu.VMEM((choices * padded, up.shape[1]), jnp.float32),
            pltpu.VMEM((padded * count, 2 * rank), jnp.float32),
            pltpu.VMEM((padded * count, 2 * rank), jnp.float32),
            pltpu.SemaphoreType.DMA,
            pltpu.SemaphoreType.DMA((sum(counts) * choices * halves,)),
        ],
        compiler_params=pltpu.CompilerParams(vmem_limit_bytes=16 * MIB),
        cost_estimate=pl.CostEstimate(
            flops=0, bytes_accessed=4 * cost * sum(counts) * length * HALF, transcendentals=0
        ),
        name="make_messages",
    )(wanted, in_hbm(down), in_hbm(up), *[in_vmem(other) for other in others])


def load_rows(weight):
    def kernel(source, whole, half, sems):
        x = lax.axis_index("parts")
        own = pltpu.make_async_copy(source.at[pl.ds(x * HALF, HALF), :], half, sems.at[0])
        rest = pltpu.make_async_copy(source, whole, sems.at[1])
        own.start()
        rest.start()
        own.wait()
        rest.wait()

    return pl.pallas_call(
        kernel,
        out_shape=[
            pltpu.VMEM(weight.shape, weight.dtype),
            pltpu.VMEM((HALF, weight.shape[1]), weight.dtype),
        ],
        in_specs=[pl.BlockSpec(memory_space=pltpu.HBM)],
        out_specs=[pl.BlockSpec(memory_space=pltpu.VMEM)] * 2,
        scratch_shapes=[pltpu.SemaphoreType.DMA((2,))],
        compiler_params=pltpu.CompilerParams(vmem_limit_bytes=2 * MIB),
        name="load_rows",
    )(in_hbm(weight))


def base_product(tokens, bundles, start=None, others=()):
    rows, depth = tokens.shape
    width = bundles[0][1].shape[1]
    count = len(bundles)
    total_rows = sum(bundle.shape[0] for _, bundle in bundles)

    def kernel(tokens_ref, *refs):
        parts, out = refs[:count], refs[-1]
        place = dict(zip(AXES, [lax.axis_index(name) for name in AXES]))
        first = True
        for (masks, _), part in zip(bundles, parts):
            left = []
            for x, z, y, core in masks:
                z, y, core = place["line"] ^ z, place["plane"] ^ y, place["core"] ^ core
                owner = (z * 2 + y) * 2 + core
                if x is None:
                    column, size = pl.multiple_of(owner * 2 * HALF, 2 * HALF), 2 * HALF
                else:
                    column = pl.multiple_of((owner * 2 + (place["parts"] ^ x)) * HALF, HALF)
                    size = HALF
                left.append(tokens_ref[:, pl.ds(column, size)])
            total = jnp.dot(
                jnp.concatenate(left, axis=1), part[...], preferred_element_type=jnp.float32
            )
            if first:
                out[...] = total if start is None else refs[count][...] + total
            else:
                out[...] += total
            first = False

    extra = ([] if start is None else [start]) + list(others)
    return pl.pallas_call(
        kernel,
        out_shape=pltpu.VMEM((rows, width), jnp.float32),
        in_specs=[pl.BlockSpec(memory_space=pltpu.VMEM)] * (1 + count + len(extra)),
        out_specs=pl.BlockSpec(memory_space=pltpu.VMEM),
        compiler_params=pltpu.CompilerParams(vmem_limit_bytes=16 * MIB),
        cost_estimate=pl.CostEstimate(
            flops=2 * rows * total_rows * width,
            bytes_accessed=2 * rows * total_rows + 2 * total_rows * width + 4 * rows * width,
            transcendentals=0,
        ),
        name="base_product",
    )(*[in_vmem(value) for value in (tokens, *[bundle for _, bundle in bundles], *extra)])


def shrink_part(sources, length, tokens, messages, wide, ups):
    pair = wide.shape[1]
    step = HALF // pair
    groups = wide.shape[0] // ups.shape[0]
    depth = tokens.shape[1] // groups
    halves = depth // HALF
    total = None
    for n, start, source in sources():
        begin = start if isinstance(start, int) else pl.multiple_of(start, 16)
        message = messages[n][pl.ds(begin, length), :]
        column = pl.multiple_of(source * depth, depth)
        down = jnp.concatenate(
            [message[half * pair : (half + 1) * pair, :] for half in range(halves)], axis=1
        )
        part = lax.dot_general(
            tokens[:, pl.ds(column, depth)],
            down,
            (((1,), (1,)), ((), ())),
            preferred_element_type=jnp.float32,
        )
        total = part if total is None else total + part
        up = message[halves * pair :, :].astype(jnp.float32)
        count = up.shape[0]
        for i in range(step):
            ups[pl.ds(i, count, stride=step), :] = up[:, i * pair : (i + 1) * pair]
        own = pl.ds(pl.multiple_of(source * count * step, count * step), count * step)
        wide[own, :] = ups[...].astype(jnp.bfloat16)
    return total


def adapt_cost(tokens, pair, share):
    return pl.CostEstimate(
        flops=int(4 * tokens.size * pair * share),
        bytes_accessed=int(2 * tokens.size * share),
        transcendentals=0,
    )


def adapt_begin(tokens, messages, sources, length, pair, shard_width, width, share):
    rows = tokens.shape[0]
    count = len(messages)

    def kernel(tokens_ref, *refs):
        shrink, wide, ups = refs[count:]
        wide[...] = jnp.zeros_like(wide)
        shrink[...] = shrink_part(sources, length, tokens_ref, refs[:count], wide, ups)

    return pl.pallas_call(
        kernel,
        out_shape=[
            pltpu.VMEM((rows, pair), jnp.float32),
            pltpu.VMEM((width, pair), jnp.bfloat16),
        ],
        in_specs=[pl.BlockSpec(memory_space=pltpu.VMEM)] * (1 + count),
        out_specs=[pl.BlockSpec(memory_space=pltpu.VMEM)] * 2,
        scratch_shapes=[pltpu.VMEM((shard_width, pair), jnp.float32)],
        compiler_params=pltpu.CompilerParams(vmem_limit_bytes=16 * MIB),
        cost_estimate=adapt_cost(tokens, pair, share),
        name="adapt_begin",
    )(*[in_vmem(value) for value in (tokens, *messages)])


def adapt_end(tokens, messages, sources, length, mask, base, begun, shard_width, share):
    rows, width = base.shape
    pair = mask.shape[1]
    count = len(messages)

    def kernel(tokens_ref, mask_ref, base_ref, shrunk, widened, *refs):
        out, wide, ups = refs[count:]
        wide[...] = widened[...]
        shrink = shrunk[...]
        shrink += shrink_part(sources, length, tokens_ref, refs[:count], wide, ups)
        picked = (shrink * mask_ref[...]).astype(jnp.bfloat16)
        delta = lax.dot_general(
            picked, wide[...], (((1,), (1,)), ((), ())), preferred_element_type=jnp.float32
        )
        out[...] = (base_ref[...] + delta).astype(out.dtype)

    values = (tokens, mask, base, *begun, *messages)
    return pl.pallas_call(
        kernel,
        out_shape=jax.ShapeDtypeStruct((rows, width), jnp.bfloat16),
        in_specs=[pl.BlockSpec(memory_space=pltpu.VMEM)] * len(values),
        out_specs=pl.BlockSpec(memory_space=pltpu.VMEM),
        scratch_shapes=[
            pltpu.VMEM((width, pair), jnp.bfloat16),
            pltpu.VMEM((shard_width, pair), jnp.float32),
        ],
        compiler_params=pltpu.CompilerParams(vmem_limit_bytes=16 * MIB),
        cost_estimate=adapt_cost(tokens, pair, share),
        name="adapt_end",
    )(*[in_vmem(value) for value in values])


def after(value, *others):
    def kernel(*refs):
        pass

    return pl.pallas_call(
        kernel,
        out_shape=pltpu.VMEM(value.shape, value.dtype),
        in_specs=[pl.BlockSpec(memory_space=pl.ANY)] * (1 + len(others)),
        out_specs=pl.BlockSpec(memory_space=pl.ANY),
        input_output_aliases={0: 0},
        compiler_params=pltpu.CompilerParams(vmem_limit_bytes=MIB),
        name="after",
    )(*[in_vmem(other) for other in (value, *others)])


def bundle(pieces, others=()):
    pieces = [piece if isinstance(piece, tuple) else (piece, None, piece.shape[0]) for piece in pieces]
    count = len(pieces)
    width, dtype = pieces[0][0].shape[1], pieces[0][0].dtype

    def kernel(*refs):
        place = 0
        for ref, (_, begin, size) in zip(refs[:count], pieces):
            first = 0 if begin is None else begin()
            refs[-1][place : place + size, :] = ref[pl.ds(first, size), :]
            place += size

    values = [array for array, _, _ in pieces] + list(others)
    return pl.pallas_call(
        kernel,
        out_shape=pltpu.VMEM((sum(size for _, _, size in pieces), width), dtype),
        in_specs=[pl.BlockSpec(memory_space=pltpu.VMEM)] * len(values),
        out_specs=pl.BlockSpec(memory_space=pltpu.VMEM),
        compiler_params=pltpu.CompilerParams(vmem_limit_bytes=2 * MIB),
        name="bundle",
    )(*[in_vmem(value) for value in values])


def row_mask(lengths, slots, rows, choices, rank, others):
    requests = lengths.shape[1]

    def kernel(lengths_ref, slots_ref, *refs):
        out = refs[-1]
        group = store_index()
        position = lax.broadcasted_iota(jnp.int32, out.shape, 0)
        lane_slot = lax.broadcasted_iota(jnp.int32, out.shape, 1) // rank
        chosen = jnp.full(out.shape, slots_ref[group, 0], jnp.int32)
        begin = lengths_ref[0, 0]
        for request in range(1, requests):
            change = slots_ref[group, request] - slots_ref[group, request - 1]
            chosen += jnp.where(position >= begin, change, 0)
            begin += lengths_ref[0, request]
        out[...] = (chosen == lane_slot).astype(jnp.float32)

    return pl.pallas_call(
        kernel,
        out_shape=pltpu.VMEM((rows, choices * rank), jnp.float32),
        in_specs=[pl.BlockSpec(memory_space=pltpu.SMEM)] * 2
        + [pl.BlockSpec(memory_space=pltpu.VMEM)] * len(others),
        out_specs=pl.BlockSpec(memory_space=pltpu.VMEM),
        compiler_params=pltpu.CompilerParams(vmem_limit_bytes=2 * MIB),
        name="row_mask",
    )(lengths, slots, *[in_vmem(other) for other in others])


def row_slots(lengths, slots, rows):
    ends = jnp.cumsum(lengths)
    starts = ends - lengths
    position = jnp.arange(rows, dtype=jnp.int32)[:, None]
    member = (position >= starts[None, :]) & (position < ends[None, :])
    return jnp.sum(jnp.where(member, slots[None, :], 0), axis=1)


def swap(block, axis, bit):
    size = lax.axis_size(axis)
    return lax.ppermute(block, axis, [(i, i ^ bit) for i in range(size)])


def send_pairs(payload, target):
    size = 2 * lax.axis_size("line") * lax.axis_size("plane")
    return lax.ppermute(payload, AXES[1:], [(i, target(i)) for i in range(size)])


ROWS = {
    "Z1": ("line", 1, ["own"]),
    "Z2": ("line", 2, ["own"]),
    "Z3": ("line", 1, ["Z2"]),
    "Y0": ("plane", 1, ["own"]),
    "Y1": ("plane", 1, ["Z1"]),
    "Y2": ("plane", 1, ["Z2"]),
    "Y3": ("plane", 1, ["Z3"]),
    "X1": ("parts", 1, ["Z1", "Y0"]),
    "X2": ("parts", 1, ["Z2", "Y1"]),
    "X3": ("parts", 1, ["Z3", "Y2"]),
    "X4": ("parts", 1, ["Y3"]),
}
PLACES = {name: (int(name[1]), int(name[0] == "Y")) for name in ROWS if name[0] in "ZY"}
STEPS = (("whole", "CW", "S1", "X1"), ("C1", "S2", "X2", "S3"), ("C2", "X3", "S4"), ("C3", "X4", "C4"))


def body(
    tokens, base_weight, adapter_down, adapter_up, request_lengths, group_adapters, request_slot
):
    rank = adapter_down.shape[2]
    choices = group_adapters.shape[1]
    width = base_weight.shape[1]
    shard_width = adapter_up.shape[1]
    pair = choices * rank
    operands = (
        jnp.transpose(group_adapters),
        jnp.swapaxes(adapter_down, 1, 2),
        jnp.transpose(adapter_up, (1, 2, 0)).reshape(shard_width * rank, adapter_up.shape[0]),
        shard_width,
    )

    def early_targets():
        targets = []
        for n, mask in enumerate(EARLY):
            targets += [(n, target) for target in direct_targets(mask)]
        return targets

    def late_targets():
        core = lax.axis_index("core")
        targets = []
        for n, mask in enumerate(LATE):
            targets += [(n, target) for target in direct_targets(mask)]
        for n, masks in enumerate(ROUNDS):
            targets += [(len(LATE) + n, target) for target in round_targets(masks, core)]
        first = len(LATE) + len(ROUNDS)
        for n, rounds in enumerate(SWAPS):
            for number in rounds:
                targets += [
                    (first + n, target) for target in round_targets(ROUNDS[number], 1 - core)
                ]
        me = store_index()
        last = first + len(SWAPS)
        return targets + [(last - 1, me ^ 1), (last, me)]

    swap_counts = [2 * len(rounds) for rounds in SWAPS]
    swap_counts[-1] += 1
    late_counts = (2,) * (len(LATE) + len(ROUNDS)) + tuple(swap_counts) + (1,)
    values = {}

    def get(name):
        if name not in values:
            values[name] = make(name)
        return values[name]

    def wait(name):
        return [get(other) for other in TIES.get(name, ())]

    def early_messages():
        counts = (2,) * len(EARLY)
        messages = make_messages(*operands, counts, early_targets, 1, wait("early"))
        for mask, message in zip(EARLY, messages):
            values[f"pair{mask}"] = message

    def late_messages():
        messages = make_messages(*operands, late_counts, late_targets, COST, wait("late"))
        names = [f"pair{mask}" for mask in LATE] + [f"mine{n}" for n in range(len(ROUNDS))]
        names += [f"theirs{n}" for n in range(len(SWAPS))] + ["local"]
        values.update(zip(names, messages))

    def make(name):
        kind, number = name[0], name[1:]
        if name in ("whole", "own"):
            values["whole"], values["own"] = load_rows(base_weight)
            return values[name]
        if name in [f"pair{mask}" for mask in EARLY]:
            early_messages()
            return values[name]
        if name[:4] in ("pair", "mine", "thei", "loca"):
            late_messages()
            return values[name]
        if name in ROWS:
            axis, mask, sources = ROWS[name]
            others = wait(name)
            if kind == "X":
                payload = get("S" + number)
            elif others:
                payload = bundle([get(source) for source in sources], others)
            else:
                payload = get(sources[0])
            return swap(payload, axis, mask)
        if kind == "S":
            return bundle([get(source) for source in ROWS["X" + number][2]], wait("X" + number))
        if name == "CW":
            others = wait(name)
            return swap(bundle([get("whole")], others) if others else get("whole"), "core", 1)
        if kind == "C":
            return swap(bundle([get("S" + number), get("X" + number)], wait(name)), "core", 1)
        if kind == "T":
            return swap(after(get("theirs" + number), *wait(name)), "core", 1)
        if kind == "P":
            message = get("pair" + number)
            others = wait(name)
            payload = after(message, *others) if others else message
            return send_pairs(payload, lambda i: i ^ (2 * int(number)))
        if kind == "H":
            got, length = get("P" + number), get("local").shape[0]
            return swap(bundle([(got, lambda: length, length)], wait(name)), "core", 1)
        if kind == "R":
            masks, length = ROUNDS[int(number)], get("local").shape[0]
            group = [n for n, rounds in enumerate(SWAPS) if int(number) in rounds][0]
            begin = SWAPS[group].index(int(number)) * 2 * length
            theirs = (get(f"T{group}"), lambda: begin, 2 * length)
            payload = bundle([get("mine" + number), theirs], wait(name))
            return send_pairs(payload, lambda i: i ^ (2 * masks[i % 2]))
        if kind == "F":
            got, length = get("R" + number), get("local").shape[0]

            def place(i):
                return pl.multiple_of((2 * i + 1 - lax.axis_index("core")) * length, 16)

            parts = [(got, functools.partial(place, i), length) for i in range(2)]
            return swap(bundle(parts, wait(name)), "core", 1)
        if name == "mask":
            return row_mask(
                request_lengths, request_slot, tokens.shape[0], choices, rank, wait(name)
            )
        if name == "AB":
            every = [f"P{mask}" for mask in EARLY + LATE] + [f"R{n}" for n in range(len(ROUNDS))]
            buffers, places = arrivals([other for other in every if other not in LAST])

            def sources():
                me = store_index()
                return [(0, 0, me), (1, 2 * len(SWAPS[-1]) * length_rows, me ^ 1)] + places(2)

            shrunk, values["second factors"] = adapt_begin(
                tokens,
                (get("local"), get(f"T{len(SWAPS) - 1}"), *buffers, *wait(name)),
                sources,
                length_rows,
                pair,
                shard_width,
                width,
                0.6,
            )
            return shrunk
        if kind == "B":
            step = int(number)
            start = get(f"B{step - 1}") if step else None
            bundles = [(masks_of(part), get(part)) for part in STEPS[step]]
            return base_product(tokens, bundles, start, wait(name))
        raise KeyError(name)

    def masks_of(part):
        if part == "whole":
            return [(None, 0, 0, 0)]
        if part == "CW":
            return [(None, 0, 0, 1)]
        places = [PLACES[source] for source in ROWS["X" + part[1]][2]]
        if part[0] == "C":
            return [(x, z, y, 1) for x in range(2) for z, y in places]
        return [(int(part[0] == "X"), z, y, 0) for z, y in places]

    length_rows = base_weight.shape[0] // HALF * pair + shard_width * pair // HALF

    def pair_sources(mask, n):
        core, chip = lax.axis_index("core"), store_index() // 2
        source = (chip ^ mask) * 2
        return [(n, 0, source + core), (n + 1, 0, source + 1 - core)]

    def round_sources(masks, n):
        core, chip = lax.axis_index("core"), store_index() // 2
        own, other = jnp.where(core == 0, *masks), jnp.where(core == 0, *masks[::-1])
        places = []
        for i in range(2):
            places.append((n, (2 * i + core) * length_rows, (chip ^ own) * 2 + (core ^ i)))
            places.append((n + 1, i * length_rows, (chip ^ other) * 2 + (core ^ 1 ^ i)))
        return places

    def arrivals(names):
        buffers = []
        for name in names:
            buffers += [get(name), get(("H" if name[0] == "P" else "F") + name[1:])]

        def sources(offset=0):
            places = []
            for n, name in enumerate(names):
                if name[0] == "P":
                    places += pair_sources(int(name[1:]), offset + 2 * n)
                else:
                    places += round_sources(ROUNDS[int(name[1:])], offset + 2 * n)
            return places

        return buffers, sources

    end_buffers, end_places = arrivals(list(LAST))
    return adapt_end(
        tokens,
        tuple(end_buffers),
        end_places,
        length_rows,
        get("mask"),
        get(f"B{len(STEPS) - 1}"),
        (get("AB"), values["second factors"]),
        shard_width,
        0.4,
    )


def plain_body(
    tokens, base_weight, adapter_down, adapter_up, request_lengths, group_adapters, request_slot
):
    store = AXES[1:]
    rank = adapter_down.shape[2]
    choices = group_adapters.shape[1]
    group = lax.axis_index(store)
    wanted = jnp.transpose(group_adapters)
    slots = lax.dynamic_index_in_dim(request_slot, group, 0, keepdims=False)
    slot_of_row = row_slots(request_lengths[0], slots, tokens.shape[0])
    lane_slot = jnp.arange(choices * rank, dtype=jnp.int32)[None, :] // rank
    mask = (slot_of_row[:, None] == lane_slot).astype(jnp.float32)
    exchange = functools.partial(
        lax.all_to_all, axis_name=store, split_axis=1, concat_axis=1, tiled=True
    )
    down = exchange(jnp.take(adapter_down, wanted, axis=0))
    up = exchange(jnp.take(adapter_up, wanted, axis=0))
    weight = lax.all_gather(base_weight, store, axis=0, tiled=True)
    down = down.reshape(choices, tokens.shape[1], rank)
    up = up.reshape(choices, base_weight.shape[1], rank)
    base = jnp.dot(tokens, weight, preferred_element_type=jnp.float32)
    shrink = jnp.einsum("td,kdr->tkr", tokens, down, preferred_element_type=jnp.float32)
    picked = (shrink.reshape(mask.shape) * mask).astype(jnp.bfloat16)
    picked = picked.reshape(shrink.shape)
    delta = jnp.einsum("tkr,kvr->tv", picked, up, preferred_element_type=jnp.float32)
    return (base + delta).astype(jnp.bfloat16)


def solution(mesh):
    parts, size = mesh.shape["parts"], mesh.shape["store"]
    chips = size // 2
    plane = 1
    while 4 * plane * plane <= chips:
        plane *= 2
    lines = chips // plane
    split = Mesh(mesh.devices.reshape(parts, lines, plane, 2), AXES)
    store = AXES[1:]

    def run(tokens, base_weight, *rest):
        small = (parts, lines, plane) == (2, 4, 2) and base_weight.shape[0] // size == 2 * HALF
        return jax.shard_map(
            body if small else plain_body,
            mesh=split,
            in_specs=(
                P(AXES, None),
                P(store, None),
                P(None, store, None),
                P(None, store, None),
                P(AXES, None),
                P("parts", None),
                P("parts", None),
            ),
            out_specs=P(AXES, None),
            check_vma=False,
        )(tokens, base_weight, *rest)

    return run
```
